32 devices in a mesh: seq: 8 (over z, y), chan: 4 (over x, core).
Axes of the slice: x: 2, y: 2, z: 4, core: 2. Of those that a mesh axis runs over, the one named last changes fastest.
Arguments:
- inputs: bfloat16 [2, 1024, 1024], P(None, 'seq', 'chan'), may hold values from -6 to 6
- lengths: int32 [2], replicated, may hold values from 256 to 1024, as said below
- out_grad: bfloat16 [2, 1024, 1024], P(None, 'seq', 'chan'), may hold values from -6 to 6
- norm_gain: bfloat16 [1024], P('chan'), may hold values from 0.5 to 1.5
- input_projection_weight: bfloat16 [2, 1024, 2048], P(None, None, 'chan'), may hold values from -0.1875 to 0.1875
- conv_weight: float32 [4, 2048], P(None, 'chan'), may hold values from -3 to 3
- conv_bias: float32 [2048], P('chan'), may hold values from -1 to 1
- x_weight: bfloat16 [96, 2048], P(None, 'chan'), may hold values from -0.125 to 0.125
- dt_weight: bfloat16 [64, 2048], P(None, 'chan'), may hold values from -0.75 to 0.75
- dt_bias: float32 [2048], P('chan'), may hold values from -7 to -2
- log_decay: float32 [16, 2048], P(None, 'chan'), may hold values from -5 to 1
- skip_gain: float32 [2048], P('chan'), may hold values from 0.5 to 1.5
- output_projection_weight: bfloat16 [2048, 1024], P('chan'), may hold values from -0.5 to 0.5
Outputs:
- mixed_out: bfloat16 [2, 1024, 1024], P(None, 'seq', 'chan')
- grad_inputs: bfloat16 [2, 1024, 1024], P(None, 'seq', 'chan')
- grad_norm_gain: float32 [1024], P('chan')
- grad_in_weight: float32 [2, 1024, 2048], P(None, None, 'chan')
- grad_conv_weight: float32 [4, 2048], P(None, 'chan')
- grad_conv_bias: float32 [2048], P('chan')
- grad_x_weight: float32 [96, 2048], P(None, 'chan')
- grad_dt_weight: float32 [64, 2048], P(None, 'chan')
- grad_dt_bias: float32 [2048], P('chan')
- grad_log_decay: float32 [16, 2048], P(None, 'chan')
- grad_skip_gain: float32 [2048], P('chan')
- grad_out_weight: float32 [2048, 1024], P('chan')
The draws below stay inside these ranges and needn't reach their ends.
Inputs may be any that keep to these rules, and one draw needn't show every extreme that they name: `lengths`: each sequence's valid tokens come first and padding fills the rest; one sequence fills all 1024 positions.
All inputs are finite; a program needn't handle non-finite values.
Results may differ from the reference program's by a relative error of at most 0.0086.
Values may be sent and summed in bfloat16 or wider, within the bound.
A program may use at most 128 MiB of HBM per device.

```python
import math
from functools import partial
import jax
import jax.numpy as jnp
from jax import lax

D = 1024
E = 2048
D_STATE = 16
CONV = 4
DT_RANK = 64
SEQS = 2
L = 1024
PROJ = 96


def draw_lengths(key, part):
    key = jax.random.fold_in(key, 7)
    first_key, second_key = jax.random.split(key)
    drawn = jax.random.randint(first_key, (SEQS,), L // 4, L + 1, dtype=jnp.int32)
    chosen = jax.random.randint(second_key, (), 0, SEQS, dtype=jnp.int32)
    return jnp.where(jnp.arange(SEQS, dtype=jnp.int32) == chosen, jnp.int32(L), drawn).astype(jnp.int32)


def block_levels(stream_key, dims, cuts, least, top_value):
    def one(dim, blocks):
        steps = jax.random.uniform(jax.random.fold_in(jax.random.fold_in(stream_key, 6), dim), (blocks,), jnp.float32, least / len(cuts), top_value / len(cuts))
        return jnp.repeat(jnp.exp(steps), dims[dim] // blocks).reshape((-1,) + (1,) * (len(dims) - dim - 1))

    factor_of = one(*cuts[0])
    for cut in cuts[1:]:
        factor_of = factor_of * one(*cut)
    return factor_of


def scatter_about(own_key, extent, width, limit, cuts=(), kind=jnp.bfloat16):
    array = jax.random.normal(own_key, extent, jnp.float32) * width
    if len(cuts) > 0:
        array = block_levels(own_key, extent, cuts, -0.22, 0.18) * array
    return jnp.clip(array, min=-limit, max=limit).astype(kind)


def setup_inputs(seed: int = 0) -> dict:
    seeds = jax.random.split(jax.random.key(seed), 14)
    inputs = scatter_about(seeds[0], (SEQS, L, D), 1.0, 6.0, ((1, 8), (2, 4)))
    lengths = draw_lengths(jax.random.fold_in(seeds[13], 71), 0)
    out_grad = scatter_about(seeds[2], (SEQS, L, D), 1.0, 6.0, ((1, 8), (2, 4)))
    norm_gain = jnp.clip(1.0 + 0.1 * jax.random.normal(seeds[3], (D,), jnp.float32), 0.5, 1.5).astype(jnp.bfloat16)
    input_projection_weight = scatter_about(seeds[4], (2, D, E), D ** -0.5, 0.1875, ((2, 4),))
    conv_weight = scatter_about(seeds[5], (CONV, E), CONV ** -0.5, 3.0, ((1, 4),), jnp.float32)
    conv_bias = jnp.clip(jax.random.uniform(seeds[6], (E,), jnp.float32, -1.0, 1.0) * block_levels(seeds[6], (E,), ((0, 4),), -0.4, 0.0), -1.0, 1.0)
    x_weight = scatter_about(seeds[7], (PROJ, E), E ** -0.5, 0.125, ((1, 4),))
    dt_weight = scatter_about(seeds[8], (DT_RANK, E), DT_RANK ** -0.5, 0.75, ((1, 4),))
    dt_bias = jnp.clip(-7.0 + 5.0 * jax.random.uniform(seeds[9], (E,), jnp.float32) ** block_levels(seeds[9], (E,), ((0, 4),), -0.2, 0.2), -7.0, -2.0)
    log_decay = jnp.clip(-5.0 + 6.0 * jax.random.uniform(seeds[10], (D_STATE, E), jnp.float32) ** block_levels(seeds[10], (D_STATE, E), ((1, 4),), -0.2, 0.2), -5.0, 1.0)
    skip_gain = jnp.clip(0.5 + 1.0 * jax.random.uniform(seeds[11], (E,), jnp.float32) ** block_levels(seeds[11], (E,), ((0, 4),), -0.2, 0.2), 0.5, 1.5)
    output_projection_weight = scatter_about(seeds[12], (E, D), (E // 16) ** -0.5, 0.5, ((0, 4),))
    return dict(inputs=inputs, lengths=lengths, out_grad=out_grad, norm_gain=norm_gain, input_projection_weight=input_projection_weight, conv_weight=conv_weight, conv_bias=conv_bias, x_weight=x_weight, dt_weight=dt_weight, dt_bias=dt_bias, log_decay=log_decay, skip_gain=skip_gain, output_projection_weight=output_projection_weight)


epsilon = 1e-05
highest = lax.Precision.HIGHEST

@jax.custom_vjp
def low(v):
    return lax.optimization_barrier(v.astype(jnp.bfloat16)).astype(jnp.float32)

@jax.custom_vjp
def low_back(v):
    return v

def low_keep(v):
    return (low(v), None)

def low_pass(kept, grad):
    return (grad,)

def back_keep(v):
    return (v, None)

def back_low(kept, grad):
    return (low(grad),)
low.defvjp(low_keep, low_pass)
low_back.defvjp(back_keep, back_low)

def conv_apply(inner_act, conv_weight, conv_bias):
    tap_count = conv_weight.shape[0]
    length = inner_act.shape[0]
    padded = jnp.pad(inner_act, ((tap_count - 1, 0), (0, 0)))
    running = conv_bias + jnp.zeros_like(inner_act)
    for offset in range(tap_count):
        running = running + conv_weight[offset] * padded[offset:offset + length]
    return running

def token_step(decay_rate, state_now, token_item):
    step_size, input_map, output_map, activated = token_item
    state_now = jnp.exp(step_size * decay_rate) * state_now + input_map[:, None] * (step_size * activated)
    return (state_now, lax.optimization_barrier(jnp.sum(output_map[:, None] * state_now, axis=0)))

def block_scan(decay_rate, state_now, block_item):
    return lax.scan(partial(token_step, decay_rate), state_now, block_item)

def selective_scan(step_size, input_map, output_map, activated, decay_rate):
    length, channels = step_size.shape
    span_len = math.gcd(128, length)
    blocks = tuple((tensor.reshape((length // span_len, span_len) + tensor.shape[1:]) for tensor in (step_size, input_map, output_map, activated)))
    runner = jax.checkpoint(partial(block_scan, decay_rate))
    start_state = jnp.zeros((input_map.shape[1], channels), jnp.float32)
    _, emitted = lax.scan(runner, start_state, blocks)
    return emitted.reshape(length, channels)

def forward(values, token_mask, norm_gain, input_projection_weight, conv_weight, conv_bias, x_weight, dt_weight, dt_bias, log_decay, skip_gain, output_projection_weight):
    root_scale = lax.rsqrt(lax.optimization_barrier(jnp.mean(values * values, axis=-1, keepdims=True)) + epsilon)
    normalized_rows = low(values * root_scale * norm_gain)
    inner_pre = jnp.dot(normalized_rows, input_projection_weight[0], precision=highest)
    gate_pre = low_back(jnp.dot(normalized_rows, input_projection_weight[1], precision=highest))
    inner_act = low(low_back(inner_pre)) * token_mask
    conv_pre = low_back(conv_apply(inner_act, conv_weight, conv_bias))
    activated = low(jax.nn.silu(conv_pre))
    projected = low_back(jnp.dot(activated, x_weight.T, precision=highest))
    low_rank = dt_weight.shape[0]
    state_count = log_decay.shape[0]
    delta_low = low(projected[:, :low_rank])
    input_map = projected[:, low_rank:low_rank + state_count]
    output_map = projected[:, low_rank + state_count:]
    step_size = jax.nn.softplus(low_back(jnp.dot(delta_low, dt_weight, precision=highest)) + dt_bias)
    scanned = selective_scan(step_size, input_map, output_map, activated, -jnp.exp(log_decay))
    mixer_activation = low((scanned + skip_gain * activated) * jax.nn.silu(gate_pre))
    return values + jnp.dot(mixer_activation, output_projection_weight, precision=highest)

def reference(inputs, lengths, out_grad, norm_gain, input_projection_weight, conv_weight, conv_bias, x_weight, dt_weight, dt_bias, log_decay, skip_gain, output_projection_weight):
    weights = tuple((tensor.astype(jnp.float32) for tensor in (norm_gain, input_projection_weight, conv_weight, conv_bias, x_weight, dt_weight, dt_bias, log_decay, skip_gain, output_projection_weight)))
    positions = jnp.arange(inputs.shape[1], dtype=jnp.int32)

    def per_sequence(grad_totals, sequence):
        seq_in, seq_len, seq_grad = sequence
        token_mask = (positions < seq_len).astype(jnp.float32)[:, None]
        result, pullback = jax.vjp(lambda values, *params: forward(values, token_mask, *params), seq_in.astype(jnp.float32), *weights)
        gradients = pullback(seq_grad.astype(jnp.float32) * token_mask)
        grad_totals = tuple((acc_total + new_term for acc_total, new_term in zip(grad_totals, gradients[1:])))
        return (grad_totals, (result.astype(jnp.bfloat16), gradients[0].astype(jnp.bfloat16)))
    grad_sums, (outputs, input_grads) = lax.scan(per_sequence, tuple((jnp.zeros_like(tensor) for tensor in weights)), (inputs, lengths, out_grad))
    return (outputs, input_grads, grad_sums[0], grad_sums[1], grad_sums[2], grad_sums[3], grad_sums[4], grad_sums[5], grad_sums[6], grad_sums[7], grad_sums[8], grad_sums[9])
```

```python
from functools import partial
import jax
import jax.numpy as jnp
from jax import lax
from jax.experimental import pallas as pl
from jax.experimental.pallas import tpu as pltpu
from jax.sharding import PartitionSpec as P

epsilon = 1e-05


def from_behind(value, axis, steps):
    count = lax.axis_size(axis)
    first, last = (max(0, -steps), min(count, count - steps))
    return lax.ppermute(value, axis, [(source, source + steps) for source in range(first, last)])


def carried_in(totals, rate2, ends, leaves):
    count, mine = (lax.axis_size("seq"), lax.axis_index("seq"))
    all_totals, all_ends, all_leaves = (
        lax.all_gather(part, "seq") for part in (totals, ends, leaves)
    )
    entering, leaving = (jnp.zeros_like(ends), jnp.zeros_like(leaves))

    def turn(step, pair):
        entering, leaving = pair
        earlier, later = (step, count - 1 - step)
        forward = jnp.exp2(all_totals[earlier][:, None, :] * rate2) * entering + all_ends[earlier]
        backward = jnp.exp2(all_totals[later][:, None, :] * rate2) * leaving + all_leaves[later]
        return (
            jnp.where(earlier < mine, forward, entering),
            jnp.where(later > mine, backward, leaving),
        )

    return lax.fori_loop(0, count - 1, turn, (entering, leaving))


def silu_slope(values):
    sigmoid_val = jax.nn.sigmoid(values)
    return sigmoid_val * (1.0 + values * (1.0 - sigmoid_val))


LANES = 128
LOG2E = 1.4426950408889634


def lane_chunks(width):
    return [slice(k * LANES, (k + 1) * LANES) for k in range(width // LANES)]


def spread_maps(maps_ref, b_ref, c_ref, states, first, tokens):
    def block(index, _):
        start = index * 8
        rolled = pltpu.roll(maps_ref[:, first : first + tokens], lax.rem(tokens - start, tokens), 1)
        for j in range(8):
            column = jnp.broadcast_to(rolled[:, j : j + 1], (2 * states, LANES))
            b_ref[first + start + j] = column[:states]
            c_ref[first + start + j] = column[states:]
        return 0

    lax.fori_loop(0, tokens // 8, block, 0)


def local_states(decay_ref, step_ref, drive_ref, b_ref, rate_ref, first, tokens):
    states, width = rate_ref.shape
    chunks = lane_chunks(width)

    def block(index, held):
        held = list(held)
        rows = pl.ds(pl.multiple_of(first + index * 8, 8), 8)
        steps = [step_ref[rows, lanes] for lanes in chunks]
        drives = [drive_ref[rows, lanes] for lanes in chunks]
        for j in range(8):
            token = first + index * 8 + j
            b = b_ref[token]
            for k, lanes in enumerate(chunks):
                decay = jnp.exp2(steps[k][j : j + 1] * rate_ref[:, lanes])
                decay_ref[token, :, lanes] = decay
                held[k] = decay * held[k] + drives[k][j : j + 1] * b
        return tuple(held)

    zero = tuple(jnp.zeros((states, LANES), jnp.float32) for _ in chunks)
    return lax.fori_loop(0, tokens // 8, block, zero)


def local_adjoints(decay_ref, up_ref, c_ref, first, tokens):
    _, states, width = decay_ref.shape
    chunks = lane_chunks(width)

    def block(index, held):
        held = list(held)
        start = first + (tokens // 8 - 1 - index) * 8
        ups = [up_ref[pl.ds(pl.multiple_of(start, 8), 8), lanes] for lanes in chunks]
        for j in range(7, -1, -1):
            token = start + j
            c = c_ref[token]
            for k, lanes in enumerate(chunks):
                adjoint = c * ups[k][j : j + 1] + held[k]
                held[k] = decay_ref[token, :, lanes] * adjoint
        return tuple(held)

    zero = tuple(jnp.zeros((states, LANES), jnp.float32) for _ in chunks)
    return lax.fori_loop(0, tokens // 8, block, zero)


def run_states(decay_ref, drive_ref, b_ref, c_ref, enter_ref, state_ref, out_ref, which, first, tokens):
    _, states, width = decay_ref.shape
    chunks = lane_chunks(width)

    def block(index, held):
        held = list(held)
        rows = pl.ds(pl.multiple_of(first + index * 8, 8), 8)
        drives = [drive_ref[rows, lanes] for lanes in chunks]
        outs = [[] for _ in chunks]
        for j in range(8):
            token = first + index * 8 + j
            b, c = b_ref[token], c_ref[token]
            for k, lanes in enumerate(chunks):
                held[k] = decay_ref[token, :, lanes] * held[k] + drives[k][j : j + 1] * b
                state_ref[token, :, lanes] = held[k].astype(jnp.bfloat16)
                outs[k].append(jnp.sum(c * held[k], axis=0, keepdims=True))
        for k, lanes in enumerate(chunks):
            out_ref[rows, lanes] = jnp.concatenate(outs[k], axis=0)
        return tuple(held)

    start = tuple(enter_ref[which, :, lanes] for lanes in chunks)
    lax.fori_loop(0, tokens // 8, block, start)


def run_adjoints(
    decay_ref, step_ref, up_ref, b_ref, c_ref, rate_ref, enter_ref, leave_ref, state_ref,
    adjoint_ref, first_sum_ref, second_sum_ref, which, first, tokens,
):
    _, states, width = decay_ref.shape
    chunks = lane_chunks(width)

    def block(index, carried):
        held, total = list(carried[0]), list(carried[1])
        ones = [[None] * 8 for _ in chunks]
        twos = [[None] * 8 for _ in chunks]
        start = first + (tokens // 8 - 1 - index) * 8
        rows = pl.ds(pl.multiple_of(start, 8), 8)
        ups = [up_ref[rows, lanes] for lanes in chunks]
        steps = [step_ref[rows, lanes] for lanes in chunks]
        for j in range(7, -1, -1):
            token = start + j
            b, c = b_ref[token], c_ref[token]
            for k, lanes in enumerate(chunks):
                adjoint = c * ups[k][j : j + 1] + held[k]
                adjoint_ref[token, :, lanes] = adjoint.astype(jnp.bfloat16)
                held[k] = decay_ref[token, :, lanes] * adjoint
                if j > 0:
                    before = state_ref[token - 1, :, lanes].astype(jnp.float32)
                else:
                    before = state_ref[jnp.maximum(token - 1, first), :, lanes].astype(jnp.float32)
                    before = jnp.where(token == first, enter_ref[which, :, lanes], before)
                pulled = held[k] * before
                ones[k][j] = jnp.sum(pulled * rate_ref[:, lanes], axis=0, keepdims=True)
                twos[k][j] = jnp.sum(adjoint * b, axis=0, keepdims=True)
                total[k] = total[k] + pulled * steps[k][j : j + 1]
        for k, lanes in enumerate(chunks):
            first_sum_ref[rows, lanes] = jnp.concatenate(ones[k], axis=0)
            second_sum_ref[rows, lanes] = jnp.concatenate(twos[k], axis=0)
        return tuple(held), tuple(total)

    begin = tuple(leave_ref[which, :, lanes] for lanes in chunks)
    zero = tuple(jnp.zeros((states, LANES), jnp.float32) for _ in chunks)
    return lax.fori_loop(0, tokens // 8, block, (begin, zero))[1]


def map_sums(values_ref, rows, states, first, tokens):
    width = rows.shape[1]
    flat = values_ref[first : first + tokens].reshape(tokens * states, width)
    all_pairs = lax.dot_general(
        flat, rows.astype(jnp.bfloat16), (((1,), (1,)), ((), ())), preferred_element_type=jnp.float32
    )
    row_token = lax.broadcasted_iota(jnp.int32, (tokens * states, tokens), 0) // states
    column_token = lax.broadcasted_iota(jnp.int32, (tokens * states, tokens), 1)
    kept = jnp.where(row_token == column_token, all_pairs, 0.0).astype(jnp.bfloat16)
    state = lax.broadcasted_iota(jnp.int32, (states, tokens * states), 0)
    row_state = lax.broadcasted_iota(jnp.int32, (states, tokens * states), 1) % states
    pick = (state == row_state).astype(jnp.bfloat16)
    return jnp.dot(pick, kept, preferred_element_type=jnp.float32)


def summary_kernel(seqs, step_ref, drive_ref, up_ref, maps_ref, rate_ref, end_ref, leave_ref, decay_ref, b_ref, c_ref):
    states, width = rate_ref.shape
    tokens = step_ref.shape[0] // seqs
    for s in range(seqs):
        spread_maps(maps_ref, b_ref, c_ref, states, s * tokens, tokens)
        ends = local_states(decay_ref, step_ref, drive_ref, b_ref, rate_ref, s * tokens, tokens)
        for k, lanes in enumerate(lane_chunks(width)):
            end_ref[s, :, lanes] = ends[k]
        leaves = local_adjoints(decay_ref, up_ref, c_ref, s * tokens, tokens)
        for k, lanes in enumerate(lane_chunks(width)):
            leave_ref[s, :, lanes] = leaves[k]


def scan_kernel(
    seqs, step_ref, drive_ref, up_ref, maps_ref, rate2_ref, rate_ref, enter_ref, leave_ref,
    out_ref, first_sum_ref, second_sum_ref, maps_grad_ref, rate_sum_ref,
    decay_ref, b_ref, c_ref, state_ref, adjoint_ref,
):
    states, width = rate_ref.shape
    tokens = step_ref.shape[0] // seqs
    for s in range(seqs):
        first = s * tokens
        spread_maps(maps_ref, b_ref, c_ref, states, first, tokens)
        local_states(decay_ref, step_ref, drive_ref, b_ref, rate2_ref, first, tokens)
        run_states(decay_ref, drive_ref, b_ref, c_ref, enter_ref, state_ref, out_ref, s, first, tokens)
        sums = run_adjoints(
            decay_ref, step_ref, up_ref, b_ref, c_ref, rate_ref, enter_ref, leave_ref, state_ref,
            adjoint_ref, first_sum_ref, second_sum_ref, s, first, tokens,
        )
        for k, lanes in enumerate(lane_chunks(width)):
            if s == 0:
                rate_sum_ref[:, lanes] = sums[k]
            else:
                rate_sum_ref[:, lanes] += sums[k]
        maps_grad_ref[:states, first : first + tokens] = map_sums(
            adjoint_ref, drive_ref[first : first + tokens], states, first, tokens
        )
        maps_grad_ref[states:, first : first + tokens] = map_sums(
            state_ref, up_ref[first : first + tokens], states, first, tokens
        )


VMEM_LIMIT = 60 * 2**20


def whole(count):
    return [pl.BlockSpec(memory_space=pltpu.VMEM)] * count


def scan_summary(step, drive, up, maps, rate2, seqs):
    states, width = rate2.shape
    rows = step.shape[0]
    small = jax.ShapeDtypeStruct((seqs, states, width), jnp.float32)
    return pl.pallas_call(
        partial(summary_kernel, seqs),
        out_shape=(small, small),
        in_specs=whole(5),
        out_specs=tuple(whole(2)),
        scratch_shapes=[
            pltpu.VMEM((rows, states, width), jnp.float32),
            pltpu.VMEM((rows, states, LANES), jnp.float32),
            pltpu.VMEM((rows, states, LANES), jnp.float32),
        ],
        compiler_params=pltpu.CompilerParams(vmem_limit_bytes=VMEM_LIMIT),
    )(step, drive, up, maps, rate2)


def scan_full(step, drive, up, maps, rate2, rate, entering, leaving, seqs):
    states, width = rate2.shape
    rows = step.shape[0]
    wide = jax.ShapeDtypeStruct((rows, width), jnp.float32)
    return pl.pallas_call(
        partial(scan_kernel, seqs),
        out_shape=(
            wide, wide, wide,
            jax.ShapeDtypeStruct((2 * states, rows), jnp.float32),
            jax.ShapeDtypeStruct((states, width), jnp.float32),
        ),
        in_specs=whole(8),
        out_specs=tuple(whole(5)),
        scratch_shapes=[
            pltpu.VMEM((rows, states, width), jnp.float32),
            pltpu.VMEM((rows, states, LANES), jnp.float32),
            pltpu.VMEM((rows, states, LANES), jnp.float32),
            pltpu.VMEM((rows, states, width), jnp.bfloat16),
            pltpu.VMEM((rows, states, width), jnp.bfloat16),
        ],
        compiler_params=pltpu.CompilerParams(vmem_limit_bytes=VMEM_LIMIT),
    )(step, drive, up, maps, rate2, rate, entering, leaving)


def body(
    inputs,
    lengths,
    out_grad,
    norm_gain,
    input_projection_weight,
    conv_weight,
    conv_bias,
    x_weight,
    dt_weight,
    dt_bias,
    log_decay,
    skip_gain,
    output_projection_weight,
):
    seq_count, local_len, shard_width = inputs.shape
    low_rank = dt_weight.shape[0]
    tap_count = conv_weight.shape[0]
    positions = lax.axis_index("seq") * local_len + jnp.arange(local_len, dtype=jnp.int32)
    token_mask = (positions[None, :] < lengths[:, None]).astype(jnp.float32)[:, :, None]
    full_in, full_gain = (
        lax.all_gather(inputs, "chan", axis=2, tiled=True),
        lax.all_gather(norm_gain, "chan", axis=0, tiled=True),
    )
    full_vals = full_in.astype(jnp.float32)
    model_width = full_vals.shape[2]
    root_scale = lax.rsqrt(jnp.mean(full_vals * full_vals, axis=2, keepdims=True) + epsilon)
    gain_vals = full_gain.astype(jnp.float32)
    normalized_rows = (full_vals * root_scale * gain_vals).astype(jnp.bfloat16)
    projected_xz = jnp.einsum(
        "zim,fmn->fzin",
        normalized_rows,
        input_projection_weight,
        preferred_element_type=jnp.float32,
    )
    inner_act = projected_xz[0].astype(jnp.bfloat16) * token_mask.astype(jnp.bfloat16)
    gate_pre = projected_xz[1]
    left_rim = from_behind(inner_act[:, local_len - tap_count + 1 :], "seq", 1)
    padded = jnp.concatenate([left_rim, inner_act], axis=1).astype(jnp.float32)
    conv_pre = conv_bias + sum(
        (
            conv_weight[offset] * padded[:, offset : offset + local_len]
            for offset in range(tap_count)
        )
    )
    activated = jax.nn.silu(conv_pre).astype(jnp.bfloat16)
    all_act, all_rows = (
        lax.all_gather(activated, "chan", axis=2, tiled=True),
        lax.all_gather(x_weight, "chan", axis=1, tiled=True),
    )
    projected = jnp.einsum("sle,re->slr", all_act, all_rows, preferred_element_type=jnp.float32)
    delta_low = projected[:, :, :low_rank].astype(jnp.bfloat16)
    step_pre = (
        jnp.einsum("slr,re->sle", delta_low, dt_weight, preferred_element_type=jnp.float32)
        + dt_bias
    )
    step_size = jax.nn.softplus(step_pre)
    decay_rate = -jnp.exp(log_decay)
    act_vals = activated.astype(jnp.float32)
    width = step_size.shape[2]
    rate2 = decay_rate * LOG2E
    flat = lambda values: values.reshape(seq_count * local_len, values.shape[-1])
    step_rows = flat(step_size)
    drive_rows = flat(step_size * act_vals)
    maps = flat(projected[:, :, low_rank:]).T
    gate_act = jax.nn.silu(gate_pre)
    grad_full = lax.all_gather(out_grad, "chan", axis=2, tiled=True)
    cotangent_rows = grad_full * token_mask.astype(jnp.bfloat16)
    mixer_output_gradient = jnp.einsum(
        "gtb,rb->gtr", cotangent_rows, output_projection_weight, preferred_element_type=jnp.float32
    )
    grad_scanned = mixer_output_gradient * gate_act
    up_rows = flat(grad_scanned)
    ends, leaves = scan_summary(step_rows, drive_rows, up_rows, maps, rate2, seq_count)
    entering, leaving = carried_in(jnp.sum(step_size, axis=1), rate2, ends, leaves)
    scanned, first_sum, second_sum, maps_grad, rate_sum = scan_full(
        step_rows, drive_rows, up_rows, maps, rate2, decay_rate, entering, leaving, seq_count
    )
    unflat = lambda values: values.reshape(seq_count, local_len, values.shape[-1])
    scanned, first_sum, second_sum = (unflat(part) for part in (scanned, first_sum, second_sum))
    with_skip = scanned + skip_gain * act_vals
    mixer_activation = (with_skip * gate_act).astype(jnp.bfloat16)
    partial_out = jnp.einsum(
        "soj,jp->sop",
        mixer_activation,
        output_projection_weight,
        preferred_element_type=jnp.float32,
    )
    reduced = lax.psum_scatter(partial_out, "chan", scatter_dimension=2, tiled=True)
    mixed_out = (inputs.astype(jnp.float32) + reduced).astype(jnp.bfloat16)
    grad_out_weight = jnp.einsum(
        "bzw,bzy->wy", mixer_activation, cotangent_rows, preferred_element_type=jnp.float32
    )
    grad_gate = (mixer_output_gradient * with_skip * silu_slope(gate_pre)).astype(jnp.bfloat16)
    grad_skip_gain = jnp.sum(grad_scanned * act_vals, axis=(0, 1))
    grad_step = first_sum + act_vals * second_sum
    grad_act = step_size * second_sum + grad_scanned * skip_gain
    maps_grad_rows = unflat(maps_grad.T)
    grad_log_decay = rate_sum * decay_rate
    grad_step_pre = grad_step * jax.nn.sigmoid(step_pre)
    grad_dt_bias = jnp.sum(grad_step_pre, axis=(0, 1))
    grad_step_low = grad_step_pre.astype(jnp.bfloat16)
    grad_dt_weight = jnp.einsum(
        "slr,sle->re", delta_low, grad_step_low, preferred_element_type=jnp.float32
    )
    grad_low_part = jnp.einsum(
        "sle,re->slr", grad_step_low, dt_weight, preferred_element_type=jnp.float32
    )
    partial_grads = jnp.concatenate([grad_low_part, maps_grad_rows], axis=2)
    grad_projected = lax.psum(partial_grads, "chan").astype(jnp.bfloat16)
    grad_x_weight = jnp.einsum(
        "slr,sle->re", grad_projected, activated, preferred_element_type=jnp.float32
    )
    grad_act = grad_act + jnp.einsum(
        "slr,re->sle", grad_projected, x_weight, preferred_element_type=jnp.float32
    )
    grad_conv = (grad_act * silu_slope(conv_pre)).astype(jnp.bfloat16)
    grad_conv_vals = grad_conv.astype(jnp.float32)
    grad_conv_bias = jnp.sum(grad_conv_vals, axis=(0, 1))
    grad_conv_weight = jnp.stack(
        [
            jnp.sum(grad_conv_vals * padded[:, offset : offset + local_len], axis=(0, 1))
            for offset in range(tap_count)
        ]
    )
    next_rim = from_behind(grad_conv[:, : tap_count - 1], "seq", -1)
    extended = jnp.concatenate([grad_conv, next_rim], axis=1).astype(jnp.float32)
    grad_inner_vals = sum(
        (
            conv_weight[offset]
            * extended[:, tap_count - 1 - offset : tap_count - 1 - offset + local_len]
            for offset in range(tap_count)
        )
    )
    grad_inner = (grad_inner_vals * token_mask).astype(jnp.bfloat16)
    inner_gate_gradient = jnp.stack([grad_inner, grad_gate])
    grad_in_weight = jnp.einsum(
        "gpt,vgpr->vtr", normalized_rows, inner_gate_gradient, preferred_element_type=jnp.float32
    )
    grad_normed_part = jnp.einsum(
        "wrvc,wic->rvi",
        inner_gate_gradient,
        input_projection_weight,
        preferred_element_type=jnp.float32,
    )
    chan_index = lax.axis_index("chan")
    grad_normed = lax.psum(grad_normed_part, "chan")
    weighted = grad_normed * gain_vals
    moment = jnp.sum(weighted * full_vals, axis=2, keepdims=True)
    full_back = (
        root_scale * weighted
        - full_vals * (root_scale * root_scale * root_scale) * moment / model_width
    )
    grad_norm_part = lax.dynamic_slice_in_dim(full_back, chan_index * shard_width, shard_width, 2)
    gain_full = jnp.sum(grad_normed * full_vals * root_scale, axis=(0, 1))
    grad_norm_gain = lax.dynamic_slice_in_dim(gain_full, chan_index * shard_width, shard_width, 0)
    grad_inputs = (out_grad.astype(jnp.float32) * token_mask + grad_norm_part).astype(jnp.bfloat16)
    summed = lax.psum(
        (
            grad_norm_gain,
            grad_in_weight,
            grad_conv_weight,
            grad_conv_bias,
            grad_x_weight,
            grad_dt_weight,
            grad_dt_bias,
            grad_log_decay,
            grad_skip_gain,
            grad_out_weight,
        ),
        "seq",
    )
    return (
        mixed_out,
        grad_inputs,
        summed[0],
        summed[1],
        summed[2],
        summed[3],
        summed[4],
        summed[5],
        summed[6],
        summed[7],
        summed[8],
        summed[9],
    )


def solution(mesh):
    in_specs = (
        P(None, "seq", "chan"),
        P(),
        P(None, "seq", "chan"),
        P("chan"),
        P(None, None, "chan"),
        P(None, "chan"),
        P("chan"),
        P(None, "chan"),
        P(None, "chan"),
        P("chan"),
        P(None, "chan"),
        P("chan"),
        P("chan", None),
    )
    out_specs = (
        P(None, "seq", "chan"),
        P(None, "seq", "chan"),
        P("chan"),
        P(None, None, "chan"),
        P(None, "chan"),
        P("chan"),
        P(None, "chan"),
        P(None, "chan"),
        P("chan"),
        P(None, "chan"),
        P("chan"),
        P("chan", None),
    )
    return jax.shard_map(body, mesh=mesh, in_specs=in_specs, out_specs=out_specs, check_vma=False)
```

```python
from functools import partial
from types import SimpleNamespace

import jax
import jax.numpy as jnp
from jax import lax
from jax.experimental import pallas as pl
from jax.experimental.pallas import tpu as pltpu
from jax.sharding import PartitionSpec as P

EPSILON = 1e-05
LANES = 128
LOG2E = 1.4426950408889634
VMEM_LIMIT = 60 * 2**20
HALO = 16
MESH = pl.DeviceIdType.MESH
F32 = jnp.float32
BF16 = jnp.bfloat16


def lane_chunks(width):
    return [slice(k * LANES, (k + 1) * LANES) for k in range(width // LANES)]


def flip(index, bit):
    return index + bit - 2 * bit * lax.rem(lax.div(index, bit), 2)


def dot(a, b, contract=((1,), (0,))):
    return lax.dot_general(a, b, (contract, ((), ())), preferred_element_type=F32)


def silu_slope(values, sigmoid):
    return sigmoid * (1.0 + values * (1.0 - sigmoid))


def softplus(values):
    return jnp.maximum(values, 0.0) + jnp.log1p(jnp.exp(-jnp.abs(values)))


def spread_maps(maps, b_ref, c_ref, first, tokens):
    states = maps.shape[0] // 2

    def block(index, _):
        start = index * 8
        rolled = pltpu.roll(maps, lax.rem(tokens - start, tokens), 1)
        for j in range(8):
            column = jnp.broadcast_to(rolled[:, j : j + 1], (2 * states, LANES))
            b_ref[first + start + j] = column[:states]
            c_ref[first + start + j] = column[states:]
        return 0

    lax.fori_loop(0, tokens // 8, block, 0)


def zero_states(rate_ref):
    states, width = rate_ref.shape
    return tuple(jnp.zeros((states, LANES), F32) for _ in lane_chunks(width))


def local_states(decay_ref, step_ref, drive_ref, b_ref, rate_ref, first, tokens):
    chunks = lane_chunks(rate_ref.shape[1])

    def block(index, held):
        held = list(held)
        rows = pl.ds(pl.multiple_of(first + index * 8, 8), 8)
        steps = [step_ref[rows, lanes] for lanes in chunks]
        drives = [drive_ref[rows, lanes] for lanes in chunks]
        for j in range(8):
            token = first + index * 8 + j
            b = b_ref[token]
            for k, lanes in enumerate(chunks):
                decay = jnp.exp2(steps[k][j : j + 1] * rate_ref[:, lanes])
                decay_ref[token, :, lanes] = decay
                held[k] = decay * held[k] + drives[k][j : j + 1] * b
        return tuple(held)

    return lax.fori_loop(0, tokens // 8, block, zero_states(rate_ref))


def local_adjoints(decay_ref, up_ref, c_ref, rate_ref, first, tokens):
    chunks = lane_chunks(rate_ref.shape[1])

    def block(index, held):
        held = list(held)
        start = first + (tokens // 8 - 1 - index) * 8
        rows = pl.ds(pl.multiple_of(start, 8), 8)
        ups = [up_ref[rows, lanes] for lanes in chunks]
        for j in range(7, -1, -1):
            token = start + j
            c = c_ref[token]
            for k, lanes in enumerate(chunks):
                adjoint = c * ups[k][j : j + 1] + held[k]
                held[k] = decay_ref[token, :, lanes] * adjoint
        return tuple(held)

    return lax.fori_loop(0, tokens // 8, block, zero_states(rate_ref))


def run_states(decay_ref, drive_ref, b_ref, c_ref, enter_ref, state_ref, out_ref, which, first, tokens):
    chunks = lane_chunks(decay_ref.shape[2])

    def block(index, held):
        held = list(held)
        rows = pl.ds(pl.multiple_of(first + index * 8, 8), 8)
        drives = [drive_ref[rows, lanes] for lanes in chunks]
        outs = [[] for _ in chunks]
        for j in range(8):
            token = first + index * 8 + j
            b, c = b_ref[token], c_ref[token]
            for k, lanes in enumerate(chunks):
                held[k] = decay_ref[token, :, lanes] * held[k] + drives[k][j : j + 1] * b
                state_ref[token, :, lanes] = held[k].astype(BF16)
                outs[k].append(jnp.sum(c * held[k], axis=0, keepdims=True))
        for k, lanes in enumerate(chunks):
            out_ref[rows, lanes] = jnp.concatenate(outs[k], axis=0)
        return tuple(held)

    lax.fori_loop(0, tokens // 8, block, tuple(enter_ref[which, :, lanes] for lanes in chunks))


def run_adjoints(
    decay_ref, step_ref, up_ref, b_ref, c_ref, rate_ref, enter_ref, state_ref, adjoint_ref,
    first_sum_ref, second_sum_ref, which, first, tokens, span, carried,
):
    chunks = lane_chunks(rate_ref.shape[1])

    def block(index, carried):
        held, total = list(carried[0]), list(carried[1])
        ones = [[None] * 8 for _ in chunks]
        twos = [[None] * 8 for _ in chunks]
        start = first + (tokens // 8 - 1 - index) * 8
        rows = pl.ds(pl.multiple_of(start, 8), 8)
        ups = [up_ref[rows, lanes] for lanes in chunks]
        steps = [step_ref[rows, lanes] for lanes in chunks]
        for j in range(7, -1, -1):
            token = start + j
            b, c = b_ref[token], c_ref[token]
            for k, lanes in enumerate(chunks):
                adjoint = c * ups[k][j : j + 1] + held[k]
                adjoint_ref[token, :, lanes] = adjoint.astype(BF16)
                held[k] = decay_ref[token, :, lanes] * adjoint
                if j > 0:
                    before = state_ref[token - 1, :, lanes].astype(F32)
                else:
                    before = state_ref[jnp.maximum(token - 1, first), :, lanes].astype(F32)
                    before = jnp.where(token == first, enter_ref[which, :, lanes], before)
                pulled = held[k] * before
                ones[k][j] = jnp.sum(pulled * rate_ref[:, lanes], axis=0, keepdims=True)
                twos[k][j] = jnp.sum(adjoint * b, axis=0, keepdims=True)
                total[k] = total[k] + pulled * steps[k][j : j + 1]
        for k, lanes in enumerate(chunks):
            first_sum_ref[rows, lanes] = jnp.concatenate(ones[k], axis=0)
            second_sum_ref[rows, lanes] = jnp.concatenate(twos[k], axis=0)
        return tuple(held), tuple(total)

    return lax.fori_loop(span[0], span[1], block, carried)


def map_sums(values_ref, rows, states, first, tokens):
    width = rows.shape[1]
    flat = values_ref[first : first + tokens].reshape(tokens * states, width)
    all_pairs = dot(flat, rows.astype(BF16), ((1,), (1,)))
    row_token = lax.broadcasted_iota(jnp.int32, (tokens * states, tokens), 0) // states
    column_token = lax.broadcasted_iota(jnp.int32, (tokens * states, tokens), 1)
    kept = jnp.where(row_token == column_token, all_pairs, 0.0).astype(BF16)
    state = lax.broadcasted_iota(jnp.int32, (states, tokens * states), 0)
    row_state = lax.broadcasted_iota(jnp.int32, (states, tokens * states), 1) % states
    return dot((state == row_state).astype(BF16), kept)


def send(src, dst, send_sem, recv_sem, device):
    copy = pltpu.make_async_remote_copy(
        src_ref=src, dst_ref=dst, send_sem=send_sem, recv_sem=recv_sem,
        device_id=device, device_id_type=MESH,
    )
    copy.start()
    return copy


class ChanGather:
    def __init__(self, src, dst, sems, mine, core_peer, x_peer):
        self.dst, self.sems, self.mine, self.core_peer = (dst, sems, mine, core_peer)
        self.over_x = send(src, dst.at[mine], sems.at[0], sems.at[1], x_peer)
        self.over_core = send(src, dst.at[mine], sems.at[2], sems.at[3], core_peer)

    def relay(self):
        self.over_x.wait_recv()
        block = self.dst.at[flip(self.mine, 2)]
        self.onward = send(block, block, self.sems.at[4], self.sems.at[5], self.core_peer)

    def finish(self):
        self.over_core.wait_recv()
        self.onward.wait_recv()
        for copy in (self.over_x, self.over_core, self.onward):
            copy.wait_send()


class ChanSum:
    def __init__(self, own, first, second, middle, sems, core_peer, x_peer):
        self.own, self.first, self.second, self.middle = (own, first, second, middle)
        self.sems, self.x_peer = (sems, x_peer)
        self.copies = [send(own, first, sems.at[0], sems.at[1], core_peer)]

    def cross(self):
        self.copies[0].wait_recv()
        self.middle[...] = self.own[...] + self.first[...]
        self.copies.append(send(self.middle, self.second, self.sems.at[2], self.sems.at[3], self.x_peer))

    def finish(self):
        self.copies[1].wait_recv()
        for copy in self.copies:
            copy.wait_send()
        return self.middle[...] + self.second[...]


class ChanScatter:
    def __init__(self, blocks, first, second, sems, mine, core_peer, x_peer, extra=None):
        self.blocks, self.first, self.second, self.sems = (blocks, first, second, sems)
        self.mine, self.x_peer, self.extra = (mine, x_peer, extra)
        other = flip(mine, 1)
        self.copies = [
            send(blocks.at[other], first.at[0], sems.at[0], sems.at[1], core_peer),
            send(blocks.at[flip(other, 2)], first.at[1], sems.at[2], sems.at[3], core_peer),
        ]
        if extra is not None:
            self.copies.append(send(extra[0], extra[1], sems.at[6], sems.at[7], core_peer))

    def cross(self):
        for copy in self.copies:
            copy.wait_recv()
        far = flip(self.mine, 2)
        self.blocks[far] = (self.blocks[far].astype(F32) + self.first[1].astype(F32)).astype(BF16)
        self.last = [send(self.blocks.at[far], self.second, self.sems.at[4], self.sems.at[5], self.x_peer)]
        if self.extra is not None:
            own, near, middle, across = self.extra
            middle[...] = own[...] + near[...]
            self.last.append(send(middle, across, self.sems.at[8], self.sems.at[9], self.x_peer))

    def finish(self):
        for copy in self.last:
            copy.wait_recv()
        for copy in self.copies + self.last:
            copy.wait_send()
        total = self.blocks[self.mine].astype(F32) + self.first[0].astype(F32) + self.second[...].astype(F32)
        if self.extra is None:
            return total
        return total, self.extra[2][...] + self.extra[3][...]


class SeqSum:
    def __init__(self, held, landing, full, sems, bits, mine, chan):
        self.held, self.landing, self.full, self.sems, self.bits = (held, landing, full, sems, bits)
        self.mine, self.chan = (mine, chan)
        self.regions = []
        self.copies = []
        start, size, place = (0, held.shape[0], 0)
        for bit in bits:
            half = size // 2
            mine_bit = lax.rem(lax.div(mine, bit), 2)
            keep = pl.multiple_of(start + mine_bit * half, 16)
            give = pl.multiple_of(start + (1 - mine_bit) * half, 16)
            self.regions.append((keep, give, half, place))
            start, size, place = (keep, half, place + half)
        self.step = 0
        self.total = 2 * len(bits)
        self.launch()

    def launch(self):
        step, count = (self.step, len(self.bits))
        sems = (self.sems.at[2 * step], self.sems.at[2 * step + 1])
        if step < count:
            _, give, half, place = self.regions[step]
            src, dst = (self.held.at[pl.ds(give, half)], self.landing.at[pl.ds(place, half)])
            bit = self.bits[step]
        else:
            keep, _, half, _ = self.regions[self.total - 1 - step]
            src = dst = self.full.at[pl.ds(keep, half)]
            bit = self.bits[self.total - 1 - step]
        self.copies.append(send(src, dst, *sems, (flip(self.mine, bit), self.chan)))

    def advance(self):
        if self.step == self.total:
            return
        self.copies[-1].wait_recv()
        if self.step < len(self.bits):
            keep, _, half, place = self.regions[self.step]
            rows = pl.ds(keep, half)
            got = self.landing[pl.ds(place, half)].astype(F32)
            into = self.held if self.step < len(self.bits) - 1 else self.full
            into[rows] = (self.held[rows].astype(F32) + got).astype(BF16)
        self.step += 1
        if self.step < self.total:
            self.launch()

    def finish(self):
        while self.step < self.total:
            self.advance()
        for copy in self.copies:
            copy.wait_send()


def layer_kernel(names, seq_devices, *refs):
    r = SimpleNamespace(**dict(zip(names, refs)))
    x_ref, og_ref, win_ref, wout_ref = (r.inputs, r.out_grad, r.w_in, r.w_out)
    xw_ref, dtw_ref = (r.x_weight, r.dt_weight)
    seqs, tokens, shard = x_ref.shape
    model, width = win_ref.shape[1:]
    states = r.log_decay.shape[0]
    low_rank = dtw_ref.shape[0]
    taps = r.conv_weight.shape[0]
    proj = xw_ref.shape[0]
    me_s, me_c = (lax.axis_index("seq"), lax.axis_index("chan"))
    core_peer, x_peer = ((me_s, flip(me_c, 1)), (me_s, flip(me_c, 2)))
    right, left = (lax.rem(me_s + 1, seq_devices), lax.rem(me_s + seq_devices - 1, seq_devices))
    other_chans = [lax.rem(me_c + k, 4) for k in range(1, 4)]

    barrier = pltpu.get_barrier_semaphore()

    def greet(device):
        pl.semaphore_signal(barrier, inc=1, device_id=device, device_id_type=MESH)

    for chan in other_chans:
        greet((me_s, chan))
        greet((right, chan))
        greet((left, chan))

    def greet_seq(k, _):
        greet((lax.rem(me_s + k, seq_devices), me_c))
        return 0

    lax.fori_loop(1, seq_devices, greet_seq, 0)
    pl.semaphore_wait(barrier, 9 + seq_devices - 1)

    gain_ref = r.gain
    gain_ref[me_c] = jnp.broadcast_to(r.norm_gain[...].astype(F32), (8, shard))
    xg_ref, og_all_ref, halo_ref = (r.x_all, r.og_all, r.halo)
    gather_x = ChanGather(x_ref, xg_ref, r.x_sems, me_c, core_peer, x_peer)
    xg_ref[me_c] = x_ref[...]
    og_all_ref[me_c] = og_ref[...]
    last_rows = x_ref.at[:, pl.ds(tokens - HALO, HALO), :]
    halo_copies = []
    for k in range(4):
        device = (right, lax.rem(me_c + k, 4))
        halo_copies.append(
            send(last_rows, halo_ref.at[me_c], r.halo_send.at[k], r.halo_recv.at[me_c], device)
        )
    gain_copies = []
    for k, chan in enumerate(other_chans):
        gain_copies.append(
            send(gain_ref.at[me_c], gain_ref.at[me_c], r.gain_send.at[k], r.gain_recv.at[me_c], (me_s, chan))
        )
    gather_og = ChanGather(og_ref, og_all_ref, r.og_sems, me_c, core_peer, x_peer)
    gather_x.relay()
    gather_x.finish()

    def wait_block(ref, sem, block):
        pltpu.make_async_remote_copy(
            src_ref=ref.at[block], dst_ref=ref.at[block], send_sem=sem.at[block], recv_sem=sem.at[block],
            device_id=core_peer, device_id_type=MESH,
        ).wait_recv()

    for chan in other_chans:
        wait_block(gain_ref, r.gain_recv, chan)
    for chan in range(4):
        wait_block(halo_ref, r.halo_recv, chan)
    for copy in halo_copies + gain_copies:
        copy.wait_send()

    rate_ref, rate2_ref = (r.rate, r.rate2)
    rate_ref[...] = -jnp.exp(r.log_decay[...])
    rate2_ref[...] = rate_ref[...] * LOG2E

    def mask_of(s, rows, begin):
        positions = me_s * tokens + begin + lax.broadcasted_iota(jnp.int32, (rows, 1), 0)
        return (positions < r.lengths[s]).astype(F32)

    def normalize(blocks):
        squares = sum(jnp.sum(b * b, axis=1, keepdims=True) for b in blocks)
        root = lax.rsqrt(squares * (1.0 / model) + EPSILON)
        return root, [(b * root * gain_ref[q, 0:1]).astype(BF16) for q, b in enumerate(blocks)]

    conv_sum = []
    has_left = (me_s > 0).astype(F32)
    for s in range(seqs):
        mine = pl.ds(s * tokens, tokens)
        root, rows = normalize([xg_ref[q, s].astype(F32) for q in range(4)])
        _, before = normalize([halo_ref[q, s].astype(F32) for q in range(4)])
        r.root[mine, :] = jnp.broadcast_to(root, (tokens, LANES))
        normed, normed_before = (jnp.concatenate(rows, axis=1), jnp.concatenate(before, axis=1))
        r.normed[mine, :] = normed
        inner = dot(normed, win_ref[0]).astype(BF16).astype(F32) * mask_of(s, tokens, 0)
        inner_before = dot(normed_before, win_ref[0]).astype(BF16).astype(F32)
        inner_before = inner_before * (mask_of(s, HALO, -HALO) * has_left)
        r.inner[s, HALO:, :] = inner
        r.inner[s, :HALO, :] = inner_before
        conv_pre = r.conv_bias[...] + sum(
            r.conv_weight[k : k + 1, :] * r.inner[s, HALO - taps + 1 + k : HALO - taps + 1 + k + tokens, :]
            for k in range(taps)
        )
        r.conv_pre[mine, :] = conv_pre
        act = (conv_pre * jax.nn.sigmoid(conv_pre)).astype(BF16)
        r.act[mine, :] = act.astype(F32)
        r.proj_own[s] = dot(xw_ref[...], act, ((1,), (1,)))
        conv_sum.append(
            ChanSum(
                r.proj_own.at[s], r.proj_first.at[s], r.proj_second.at[s], r.proj_mid.at[s],
                r.proj_sems.at[s], core_peer, x_peer,
            )
        )
    for s in range(seqs):
        conv_sum[s].cross()
    gather_og.relay()
    for s in range(seqs):
        mine = pl.ds(s * tokens, tokens)
        r.gate_pre[mine, :] = dot(r.normed[mine, :], win_ref[1])
    gather_og.finish()
    for s in range(seqs):
        mine = pl.ds(s * tokens, tokens)
        mask = mask_of(s, tokens, 0).astype(BF16)
        cot = jnp.concatenate([og_all_ref[q, s] * mask for q in range(4)], axis=1)
        r.cot[mine, :] = cot
        grad_mixed = dot(cot, wout_ref[...], ((1,), (1,)))
        gate = r.gate_pre[mine, :]
        r.grad_mixed[mine, :] = grad_mixed
        r.up[mine, :] = grad_mixed * (gate * jax.nn.sigmoid(gate))

    totals_ref = r.totals
    step_totals = []
    for s in range(seqs):
        mine = pl.ds(s * tokens, tokens)
        projected = conv_sum[s].finish()
        low = projected[:low_rank].astype(BF16)
        r.low[:, s * tokens : (s + 1) * tokens] = low
        step_pre = dot(projected[:low_rank].T.astype(BF16), dtw_ref[...]) + r.dt_bias[...]
        r.step_pre[mine, :] = step_pre
        step = softplus(step_pre)
        r.step[mine, :] = step
        r.drive[mine, :] = step * r.act[mine, :]
        step_totals.append(jnp.sum(step, axis=0, keepdims=True))
        spread_maps(projected[low_rank:], r.b, r.c, s * tokens, tokens)
    totals_ref[me_s] = jnp.concatenate(step_totals + [jnp.zeros((8 - seqs, width), F32)], axis=0)

    def seq_device(k):
        return (k, me_c)

    def totals_copy(k):
        peer = lax.rem(me_s + k, seq_devices)
        return pltpu.make_async_remote_copy(
            src_ref=totals_ref.at[me_s], dst_ref=totals_ref.at[me_s],
            send_sem=r.totals_send.at[k], recv_sem=r.totals_recv.at[me_s],
            device_id=seq_device(peer), device_id_type=MESH,
        )

    def start_totals(k, _):
        totals_copy(k).start()
        return 0

    lax.fori_loop(1, seq_devices, start_totals, 0)

    ends_refs = (r.ends, r.ends_send, r.ends_recv)
    leaves_refs = (r.leaves, r.leaves_send, r.leaves_recv)

    def carried_copy(which, s, peer):
        ref, send_sem, recv_sem = which
        return pltpu.make_async_remote_copy(
            src_ref=ref.at[s, me_s], dst_ref=ref.at[s, me_s],
            send_sem=send_sem.at[s, peer], recv_sem=recv_sem.at[s, me_s],
            device_id=seq_device(peer), device_id_type=MESH,
        )

    def start_carried(which, s, begin, end):
        def start(peer, _):
            carried_copy(which, s, peer).start()
            return 0

        lax.fori_loop(begin, end, start, 0)

    def wait_carried(which, s, begin, end):
        def wait(peer, _):
            carried_copy(which, s, peer).wait_send()
            return 0

        lax.fori_loop(begin, end, wait, 0)

    for s in range(seqs):
        ends = local_states(r.decay, r.step, r.drive, r.b, rate2_ref, s * tokens, tokens)
        for k, lanes in enumerate(lane_chunks(width)):
            r.ends[s, me_s, :, lanes] = ends[k].astype(BF16)
        start_carried(ends_refs, s, me_s + 1, seq_devices)
    for s in range(seqs):
        leaves = local_adjoints(r.decay, r.up, r.c, rate_ref, s * tokens, tokens)
        for k, lanes in enumerate(lane_chunks(width)):
            r.leaves[s, me_s, :, lanes] = leaves[k].astype(BF16)
        start_carried(leaves_refs, s, 0, me_s)

    def wait_totals(k, _):
        peer = lax.rem(me_s + k, seq_devices)
        pltpu.make_async_remote_copy(
            src_ref=totals_ref.at[peer], dst_ref=totals_ref.at[peer],
            send_sem=r.totals_send.at[k], recv_sem=r.totals_recv.at[peer],
            device_id=seq_device(peer), device_id_type=MESH,
        ).wait_recv()
        return 0

    lax.fori_loop(1, seq_devices, wait_totals, 0)

    def combine(which, s, count, place):
        ref, send_sem, recv_sem = which

        def turn(k, held):
            peer = place(k)
            pltpu.make_async_remote_copy(
                src_ref=ref.at[s, peer], dst_ref=ref.at[s, peer],
                send_sem=send_sem.at[s, peer], recv_sem=recv_sem.at[s, peer],
                device_id=seq_device(peer), device_id_type=MESH,
            ).wait_recv()
            total = totals_ref[peer][s : s + 1]
            return jnp.exp2(total * rate2_ref[...]) * held + ref[s, peer].astype(F32)

        return lax.fori_loop(0, count, turn, jnp.zeros((states, width), F32))

    for s in range(seqs):
        mine = pl.ds(s * tokens, tokens)
        r.entering[s] = combine(ends_refs, s, me_s, lambda k: k)
        run_states(
            r.decay, r.drive, r.b, r.c, r.entering, r.state, r.scanned, s, s * tokens, tokens
        )
        gate = r.gate_pre[mine, :]
        sigmoid = jax.nn.sigmoid(gate)
        with_skip = r.scanned[mine, :] + r.skip_gain[...] * r.act[mine, :]
        mixed = (with_skip * (gate * sigmoid)).astype(BF16)
        r.mixed[mine, :] = mixed
        r.grad_gate[mine, :] = (r.grad_mixed[mine, :] * with_skip * silu_slope(gate, sigmoid)).astype(BF16)
    out_part = dot(r.mixed[...], wout_ref[...])
    for q in range(4):
        r.out_blocks[q] = out_part[:, q * shard : (q + 1) * shard].astype(BF16)
    scatter_out = ChanScatter(
        r.out_blocks, r.out_first, r.out_second, r.out_sems, me_c, core_peer, x_peer
    )
    bits = [1 << k for k in range(seq_devices.bit_length() - 1)]
    turned = bits[1:] + bits[:1]
    grad_out = dot(r.mixed[...], r.cot[...], ((0,), (0,))).astype(BF16)
    r.grad_w_out[:width, :] = grad_out[:, : model // 2]
    r.grad_w_out[width:, :] = grad_out[:, model // 2 :]
    sums = [SeqSum(r.grad_w_out, r.land_w_out, r.out_w_out, r.w_out_sems, bits, me_s, me_c)]
    r.grad_w_gate[...] = dot(r.normed[...], r.grad_gate[...], ((0,), (0,))).astype(BF16)
    sums.append(SeqSum(r.grad_w_gate, r.land_w_gate, r.out_w_gate, r.w_gate_sems, turned, me_s, me_c))

    blocks = tokens // 8
    rate_sums = None
    small = r.small
    small[...] = jnp.zeros_like(small)
    low_sum = []
    act_part = []
    for s in range(seqs):
        mine = pl.ds(s * tokens, tokens)
        first = s * tokens
        leaving = combine(leaves_refs, s, seq_devices - 1 - me_s, lambda k: seq_devices - 1 - k)
        carried = (tuple(leaving[:, lanes] for lanes in lane_chunks(width)), zero_states(rate_ref))
        parts = 4
        for part in range(parts):
            carried = run_adjoints(
                r.decay, r.step, r.up, r.b, r.c, rate_ref, r.entering, r.state,
                r.adjoint, r.first_sum, r.second_sum, s, first, tokens,
                (part * blocks // parts, (part + 1) * blocks // parts), carried,
            )
            if s == 0 and part == 0:
                scatter_out.cross()
            elif part % 2 == 1:
                for item in sums:
                    item.advance()
        rate_sums = carried[1] if rate_sums is None else [a + b for a, b in zip(rate_sums, carried[1])]
        act, step, step_pre = (r.act[mine, :], r.step[mine, :], r.step_pre[mine, :])
        second = r.second_sum[mine, :]
        grad_step_pre = (r.first_sum[mine, :] + act * second) * jax.nn.sigmoid(step_pre)
        grad_step_low = grad_step_pre.astype(BF16)
        r.grad_step_low[mine, :] = grad_step_low
        small[proj + low_rank + states + taps + 1, :] += jnp.sum(grad_step_pre, axis=0)
        small[proj + low_rank + states + taps + 2, :] += jnp.sum(r.up[mine, :] * act, axis=0)
        r.grad_act[mine, :] = step * second + r.up[mine, :] * r.skip_gain[...]
        own = r.proj_own.at[s]
        own[:low_rank, :] = dot(dtw_ref[...], grad_step_low, ((1,), (1,)))
        own[low_rank : low_rank + states, :] = map_sums(r.adjoint, r.drive[mine, :], states, first, tokens)
        own[low_rank + states :, :] = map_sums(r.state, r.up[mine, :], states, first, tokens)
        low_sum.append(
            ChanSum(
                own, r.back_first.at[s], r.back_second.at[s], r.back_mid.at[s],
                r.back_sems.at[s], core_peer, x_peer,
            )
        )
        if s > 0:
            low_sum[s - 1].cross()
    out_sum = scatter_out.finish()
    for s in range(seqs):
        r.mixed_out[s] = (x_ref[s].astype(F32) + out_sum[s * tokens : (s + 1) * tokens]).astype(BF16)
    low_sum[seqs - 1].cross()
    for k, lanes in enumerate(lane_chunks(width)):
        small[proj + low_rank : proj + low_rank + states, lanes] = rate_sums[k] * rate_ref[:, lanes]
    small[proj : proj + low_rank, :] = dot(r.low[...], r.grad_step_low[...])
    for item in sums:
        item.advance()

    rim_copies = []
    for s in range(seqs):
        mine = pl.ds(s * tokens, tokens)
        grad_projected = low_sum[s].finish()
        r.grad_proj[:, s * tokens : (s + 1) * tokens] = grad_projected.astype(BF16)
        grad_act = r.grad_act[mine, :] + dot(grad_projected.T.astype(BF16), xw_ref[...])
        conv_pre = r.conv_pre[mine, :]
        grad_conv = (grad_act * silu_slope(conv_pre, jax.nn.sigmoid(conv_pre))).astype(BF16)
        r.rim_own[s] = grad_conv[:HALO]
        r.grad_conv[s, :tokens, :] = grad_conv.astype(F32)
        rim_copies.append(
            send(r.rim_own.at[s], r.rim.at[s], r.rim_sems.at[2 * s], r.rim_sems.at[2 * s + 1], (left, me_c))
        )
        small[proj + low_rank + states + taps, :] += jnp.sum(grad_conv.astype(F32), axis=0)
        for k in range(taps):
            shifted = r.inner[s, HALO - taps + 1 + k : HALO - taps + 1 + k + tokens, :]
            small[proj + low_rank + states + k, :] += jnp.sum(grad_conv.astype(F32) * shifted, axis=0)
    small[:proj, :] = dot(r.grad_proj[...], r.act[...].astype(BF16))
    for item in sums:
        item.advance()
    has_right = (me_s < seq_devices - 1).astype(F32)
    for s in range(seqs):
        mine = pl.ds(s * tokens, tokens)
        rim_copies[s].wait_recv()
        rim_copies[s].wait_send()
        r.grad_conv[s, tokens:, :] = r.rim[s].astype(F32) * has_right
        grad_inner = sum(
            r.conv_weight[k : k + 1, :] * r.grad_conv[s, taps - 1 - k : taps - 1 - k + tokens, :]
            for k in range(taps)
        )
        r.grad_inner[mine, :] = (grad_inner * mask_of(s, tokens, 0)).astype(BF16)

    late = r.grad_w_inner
    late[:model, :] = dot(r.normed[...], r.grad_inner[...], ((0,), (0,))).astype(BF16)
    late[model:, :] = small[...].astype(BF16)
    sums.append(SeqSum(late, r.land_w_inner, r.out_w_inner, r.w_inner_sems, bits, me_s, me_c))
    moment = None
    for q in range(4):
        cols = pl.ds(q * shard, shard)
        part = dot(r.grad_inner[...], win_ref[0, q * shard : (q + 1) * shard, :], ((1,), (1,)))
        part = part + dot(r.grad_gate[...], win_ref[1, q * shard : (q + 1) * shard, :], ((1,), (1,)))
        values = xg_ref[q].reshape(seqs * tokens, shard).astype(F32)
        term = jnp.sum(part * gain_ref[q, 0:1] * values, axis=1, keepdims=True)
        moment = term if moment is None else moment + term
        r.gn_blocks[q] = part.astype(BF16)
    r.moment[...] = jnp.broadcast_to(moment, (seqs * tokens, LANES)).T[:8]
    scatter_gn = ChanScatter(
        r.gn_blocks, r.gn_first, r.gn_second, r.gn_sems, me_c, core_peer, x_peer,
        (r.moment, r.moment_first, r.moment_mid, r.moment_second),
    )
    for item in sums:
        item.advance()
    scatter_gn.cross()
    for item in sums:
        item.advance()
    grad_normed, moment_row = scatter_gn.finish()
    moment = jnp.broadcast_to(moment_row[:1], (LANES, seqs * tokens)).T[:, :1]
    root = r.root[:, :1]
    values = x_ref[...].reshape(seqs * tokens, shard).astype(F32)
    gains = r.norm_gain[...].astype(F32)
    back = root * (grad_normed * gains) - values * (root * root * root) * moment * (1.0 / model)
    for s in range(seqs):
        mine = slice(s * tokens, (s + 1) * tokens)
        cot = og_ref[s].astype(F32) * mask_of(s, tokens, 0)
        r.grad_inputs[s] = (cot + back[mine]).astype(BF16)
    gain_sums_ref = r.gain_sums
    gain_sums_ref[me_s] = jnp.broadcast_to(jnp.sum(grad_normed * values * root, axis=0, keepdims=True), (8, shard))

    def gain_copy(k):
        peer = lax.rem(me_s + k, seq_devices)
        return pltpu.make_async_remote_copy(
            src_ref=gain_sums_ref.at[me_s], dst_ref=gain_sums_ref.at[me_s],
            send_sem=r.gain_sums_send.at[k], recv_sem=r.gain_sums_recv.at[me_s],
            device_id=seq_device(peer), device_id_type=MESH,
        )

    def start_gain(k, _):
        gain_copy(k).start()
        return 0

    lax.fori_loop(1, seq_devices, start_gain, 0)
    for step in range(max(item.total for item in sums)):
        for item in sums:
            item.advance()

    def take_gain(k, _):
        peer = lax.rem(me_s + k, seq_devices)
        pltpu.make_async_remote_copy(
            src_ref=gain_sums_ref.at[peer], dst_ref=gain_sums_ref.at[peer],
            send_sem=r.gain_sums_send.at[k], recv_sem=r.gain_sums_recv.at[peer],
            device_id=seq_device(peer), device_id_type=MESH,
        ).wait_recv()
        gain_copy(k).wait_send()
        totals_copy(k).wait_send()
        return 0

    lax.fori_loop(1, seq_devices, take_gain, 0)
    r.grad_gain[...] = jnp.sum(gain_sums_ref[...], axis=0)
    for item in sums:
        item.finish()
    for s in range(seqs):
        wait_carried(ends_refs, s, me_s + 1, seq_devices)
        wait_carried(leaves_refs, s, 0, me_s)


def layer(
    seq_devices,
    inputs, lengths, out_grad, norm_gain, w_in, conv_weight, conv_bias, x_weight, dt_weight,
    dt_bias, log_decay, skip_gain, w_out,
):
    seqs, tokens, shard = inputs.shape
    _, model, width = w_in.shape
    states, low_rank, taps, proj = (log_decay.shape[0], dt_weight.shape[0], conv_weight.shape[0], x_weight.shape[0])
    rows = seqs * tokens
    small_rows = proj + low_rank + states + taps + 3
    grain = 16 * seq_devices
    small_rows = -(-small_rows // grain) * grain
    steps = 4 * (seq_devices.bit_length() - 1)
    dma = pltpu.SemaphoreType.DMA
    vmem = pltpu.VMEM
    operands = dict(
        inputs=inputs, lengths=lengths, out_grad=out_grad, norm_gain=norm_gain.reshape(1, shard),
        w_in=w_in, conv_weight=conv_weight, conv_bias=conv_bias.reshape(1, width),
        x_weight=x_weight, dt_weight=dt_weight, dt_bias=dt_bias.reshape(1, width),
        log_decay=log_decay, skip_gain=skip_gain.reshape(1, width), w_out=w_out,
    )
    outputs = dict(
        mixed_out=(inputs.shape, BF16), grad_inputs=(inputs.shape, BF16), grad_gain=((8, shard), F32),
        out_w_out=((2 * width, model // 2), BF16), out_w_gate=((model, width), BF16),
        out_w_inner=((model + small_rows, width), BF16),
    )
    wide = (rows, width)
    scratch = dict(
        x_all=vmem((4,) + inputs.shape, BF16), og_all=vmem((4,) + inputs.shape, BF16),
        halo=vmem((4, seqs, HALO, shard), BF16), gain=vmem((4, 8, shard), F32),
        x_sems=dma((6,)), og_sems=dma((6,)), halo_send=dma((4,)), halo_recv=dma((4,)),
        gain_send=dma((3,)), gain_recv=dma((4,)),
        rate=vmem((states, width), F32), rate2=vmem((states, width), F32),
        root=vmem((rows, LANES), F32), normed=vmem((rows, model), BF16),
        inner=vmem((seqs, HALO + tokens, width), F32),
        conv_pre=vmem(wide, F32), act=vmem(wide, F32), gate_pre=vmem(wide, F32),
        cot=vmem((rows, model), BF16), grad_mixed=vmem(wide, F32), up=vmem(wide, F32),
        proj_own=vmem((seqs, proj, tokens), F32), proj_first=vmem((seqs, proj, tokens), F32),
        proj_second=vmem((seqs, proj, tokens), F32), proj_mid=vmem((seqs, proj, tokens), F32),
        proj_sems=dma((seqs, 4)),
        back_first=vmem((seqs, proj, tokens), F32), back_second=vmem((seqs, proj, tokens), F32),
        back_mid=vmem((seqs, proj, tokens), F32), back_sems=dma((seqs, 4)),
        low=vmem((low_rank, rows), BF16), step_pre=vmem(wide, F32), step=vmem(wide, F32),
        drive=vmem(wide, F32), b=vmem((rows, states, LANES), F32), c=vmem((rows, states, LANES), F32),
        decay=vmem((rows, states, width), F32),
        totals=vmem((seq_devices, 8, width), F32), totals_send=dma((seq_devices,)),
        totals_recv=dma((seq_devices,)),
        ends=vmem((seqs, seq_devices, states, width), BF16), ends_send=dma((seqs, seq_devices)),
        ends_recv=dma((seqs, seq_devices)),
        leaves=vmem((seqs, seq_devices, states, width), BF16), leaves_send=dma((seqs, seq_devices)),
        leaves_recv=dma((seqs, seq_devices)),
        entering=vmem((seqs, states, width), F32),
        state=vmem((rows, states, width), BF16), adjoint=vmem((rows, states, width), BF16),
        scanned=vmem(wide, F32), first_sum=vmem(wide, F32), second_sum=vmem(wide, F32),
        mixed=vmem(wide, BF16), grad_gate=vmem(wide, BF16), grad_step_low=vmem(wide, BF16),
        grad_act=vmem(wide, F32), grad_proj=vmem((proj, rows), BF16),
        grad_conv=vmem((seqs, tokens + HALO, width), F32), rim_own=vmem((seqs, HALO, width), BF16),
        rim=vmem((seqs, HALO, width), BF16), rim_sems=dma((2 * seqs,)),
        grad_inner=vmem(wide, BF16),
        out_blocks=vmem((4, rows, shard), BF16), out_first=vmem((2, rows, shard), BF16),
        out_second=vmem((rows, shard), BF16), out_sems=dma((6,)),
        gn_blocks=vmem((4, rows, shard), BF16), gn_first=vmem((2, rows, shard), BF16),
        gn_second=vmem((rows, shard), BF16), gn_sems=dma((10,)),
        moment=vmem((8, rows), F32), moment_first=vmem((8, rows), F32),
        moment_mid=vmem((8, rows), F32), moment_second=vmem((8, rows), F32),
        small=vmem((small_rows, width), F32),
        grad_w_out=vmem((2 * width, model // 2), BF16), land_w_out=vmem((2 * width, model // 2), BF16),
        w_out_sems=dma((steps,)),
        grad_w_gate=vmem((model, width), BF16), land_w_gate=vmem((model, width), BF16),
        w_gate_sems=dma((steps,)),
        grad_w_inner=vmem((model + small_rows, width), BF16),
        land_w_inner=vmem((model + small_rows, width), BF16), w_inner_sems=dma((steps,)),
        gain_sums=vmem((seq_devices, 8, shard), F32), gain_sums_send=dma((seq_devices,)),
        gain_sums_recv=dma((seq_devices,)),
    )
    names = list(operands) + list(outputs) + list(scratch)
    spaces = dict(lengths=pltpu.SMEM)
    mixed_out, grad_inputs, gain, w_out_grad, w_gate_grad, late = pl.pallas_call(
        partial(layer_kernel, names, seq_devices),
        out_shape=tuple(jax.ShapeDtypeStruct(*item) for item in outputs.values()),
        in_specs=[pl.BlockSpec(memory_space=spaces.get(name, pltpu.VMEM)) for name in operands],
        out_specs=tuple(pl.BlockSpec(memory_space=pltpu.VMEM) for _ in outputs),
        scratch_shapes=list(scratch.values()),
        compiler_params=pltpu.CompilerParams(
            collective_id=0, has_side_effects=True, vmem_limit_bytes=VMEM_LIMIT
        ),
    )(*operands.values())
    grad_w_out = jnp.concatenate([w_out_grad[:width], w_out_grad[width:]], axis=1).astype(F32)
    grad_w_in = jnp.stack([late[:model], w_gate_grad]).astype(F32)
    small = late[model:].astype(F32)
    at = proj + low_rank + states
    return (
        mixed_out, grad_inputs, gain[0], grad_w_in, small[at : at + taps], small[at + taps],
        small[:proj], small[proj : proj + low_rank], small[at + taps + 1],
        small[proj + low_rank : at], small[at + taps + 2], grad_w_out,
    )


def solution(mesh):
    in_specs = (
        P(None, "seq", "chan"), P(), P(None, "seq", "chan"), P("chan"), P(None, None, "chan"),
        P(None, "chan"), P("chan"), P(None, "chan"), P(None, "chan"), P("chan"), P(None, "chan"),
        P("chan"), P("chan", None),
    )
    out_specs = (
        P(None, "seq", "chan"), P(None, "seq", "chan"), P("chan"), P(None, None, "chan"),
        P(None, "chan"), P("chan"), P(None, "chan"), P(None, "chan"), P("chan"), P(None, "chan"),
        P("chan"), P("chan", None),
    )
    body = partial(layer, mesh.shape["seq"])
    return jax.shard_map(body, mesh=mesh, in_specs=in_specs, out_specs=out_specs, check_vma=False)
```

```python
from functools import partial
from types import SimpleNamespace

import jax
import jax.numpy as jnp
from jax import lax
from jax.experimental import pallas as pl
from jax.experimental.pallas import tpu as pltpu
from jax.sharding import PartitionSpec as P

EPSILON = 1e-05
LANES = 128
LOG2E = 1.4426950408889634
VMEM_LIMIT = 60 * 2**20
HALO = 16
MOST_GATHERED = 8
MESH = pl.DeviceIdType.MESH
F32 = jnp.float32
BF16 = jnp.bfloat16


def lane_chunks(width):
    return [slice(k * LANES, (k + 1) * LANES) for k in range(width // LANES)]


def flip(index, bit):
    return index + bit - 2 * bit * lax.rem(lax.div(index, bit), 2)


def dot(a, b, contract=((1,), (0,))):
    return lax.dot_general(a, b, (contract, ((), ())), preferred_element_type=F32)


def silu_slope(values, sigmoid):
    return sigmoid * (1.0 + values * (1.0 - sigmoid))


def softplus(values):
    return jnp.maximum(values, 0.0) + jnp.log1p(jnp.exp(-jnp.abs(values)))


def spread_maps(maps, b_ref, c_ref, first, tokens):
    states = maps.shape[0] // 2

    def block(index, _):
        start = index * 8
        rolled = pltpu.roll(maps, lax.rem(tokens - start, tokens), 1)
        for j in range(8):
            column = jnp.broadcast_to(rolled[:, j : j + 1], (2 * states, LANES))
            b_ref[first + start + j] = column[:states]
            c_ref[first + start + j] = column[states:]
        return 0

    lax.fori_loop(0, tokens // 8, block, 0)


def zero_states(rate_ref):
    states, width = rate_ref.shape
    return tuple(jnp.zeros((states, LANES), F32) for _ in lane_chunks(width))


def local_states(decay_ref, step_ref, drive_ref, b_ref, rate_ref, first, tokens):
    chunks = lane_chunks(rate_ref.shape[1])

    def block(index, held):
        held = list(held)
        rows = pl.ds(pl.multiple_of(first + index * 8, 8), 8)
        steps = [step_ref[rows, lanes] for lanes in chunks]
        drives = [drive_ref[rows, lanes] for lanes in chunks]
        for j in range(8):
            token = first + index * 8 + j
            b = b_ref[token]
            for k, lanes in enumerate(chunks):
                decay = jnp.exp2(steps[k][j : j + 1] * rate_ref[:, lanes])
                decay_ref[token, :, lanes] = decay
                held[k] = decay * held[k] + drives[k][j : j + 1] * b
        return tuple(held)

    return lax.fori_loop(0, tokens // 8, block, zero_states(rate_ref))


def local_adjoints(decay_ref, up_ref, c_ref, rate_ref, first, tokens):
    chunks = lane_chunks(rate_ref.shape[1])

    def block(index, held):
        held = list(held)
        start = first + (tokens // 8 - 1 - index) * 8
        rows = pl.ds(pl.multiple_of(start, 8), 8)
        ups = [up_ref[rows, lanes] for lanes in chunks]
        for j in range(7, -1, -1):
            token = start + j
            c = c_ref[token]
            for k, lanes in enumerate(chunks):
                adjoint = c * ups[k][j : j + 1] + held[k]
                held[k] = decay_ref[token, :, lanes] * adjoint
        return tuple(held)

    return lax.fori_loop(0, tokens // 8, block, zero_states(rate_ref))


def run_states(decay_ref, drive_ref, b_ref, c_ref, enter_ref, state_ref, out_ref, which, first, tokens):
    chunks = lane_chunks(decay_ref.shape[2])

    def block(index, held):
        held = list(held)
        rows = pl.ds(pl.multiple_of(first + index * 8, 8), 8)
        drives = [drive_ref[rows, lanes] for lanes in chunks]
        outs = [[] for _ in chunks]
        for j in range(8):
            token = first + index * 8 + j
            b, c = b_ref[token], c_ref[token]
            for k, lanes in enumerate(chunks):
                held[k] = decay_ref[token, :, lanes] * held[k] + drives[k][j : j + 1] * b
                state_ref[token, :, lanes] = held[k].astype(BF16)
                outs[k].append(jnp.sum(c * held[k], axis=0, keepdims=True))
        for k, lanes in enumerate(chunks):
            out_ref[pl.ds(pl.multiple_of(index * 8, 8), 8), lanes] = jnp.concatenate(outs[k], axis=0)
        return tuple(held)

    lax.fori_loop(0, tokens // 8, block, tuple(enter_ref[which, :, lanes] for lanes in chunks))


def run_adjoints(
    decay_ref, step_ref, up_ref, b_ref, c_ref, rate_ref, enter_ref, state_ref, adjoint_ref,
    first_sum_ref, second_sum_ref, which, first, tokens, span, carried,
):
    chunks = lane_chunks(rate_ref.shape[1])

    def block(index, carried):
        held, total = list(carried[0]), list(carried[1])
        ones = [[None] * 8 for _ in chunks]
        twos = [[None] * 8 for _ in chunks]
        start = first + (tokens // 8 - 1 - index) * 8
        rows = pl.ds(pl.multiple_of(start, 8), 8)
        ups = [up_ref[rows, lanes] for lanes in chunks]
        steps = [step_ref[rows, lanes] for lanes in chunks]
        for j in range(7, -1, -1):
            token = start + j
            b, c = b_ref[token], c_ref[token]
            for k, lanes in enumerate(chunks):
                adjoint = c * ups[k][j : j + 1] + held[k]
                adjoint_ref[token - first, :, lanes] = adjoint.astype(BF16)
                held[k] = decay_ref[token, :, lanes] * adjoint
                if j > 0:
                    before = state_ref[token - 1, :, lanes].astype(F32)
                else:
                    before = state_ref[jnp.maximum(token - 1, first), :, lanes].astype(F32)
                    before = jnp.where(token == first, enter_ref[which, :, lanes], before)
                pulled = held[k] * before
                ones[k][j] = jnp.sum(pulled * rate_ref[:, lanes], axis=0, keepdims=True)
                twos[k][j] = jnp.sum(adjoint * b, axis=0, keepdims=True)
                total[k] = total[k] + pulled * steps[k][j : j + 1]
        own_rows = pl.ds(pl.multiple_of(start - first, 8), 8)
        for k, lanes in enumerate(chunks):
            first_sum_ref[own_rows, lanes] = jnp.concatenate(ones[k], axis=0)
            second_sum_ref[own_rows, lanes] = jnp.concatenate(twos[k], axis=0)
        return tuple(held), tuple(total)

    return lax.fori_loop(span[0], span[1], block, carried)


def map_sums(values_ref, rows, states, first, tokens):
    width = rows.shape[1]
    flat = values_ref[first : first + tokens].reshape(tokens * states, width)
    all_pairs = dot(flat, rows.astype(BF16), ((1,), (1,)))
    row_token = lax.broadcasted_iota(jnp.int32, (tokens * states, tokens), 0) // states
    column_token = lax.broadcasted_iota(jnp.int32, (tokens * states, tokens), 1)
    kept = jnp.where(row_token == column_token, all_pairs, 0.0).astype(BF16)
    state = lax.broadcasted_iota(jnp.int32, (states, tokens * states), 0)
    row_state = lax.broadcasted_iota(jnp.int32, (states, tokens * states), 1) % states
    return dot((state == row_state).astype(BF16), kept)


def send(src, dst, send_sem, recv_sem, device):
    copy = pltpu.make_async_remote_copy(
        src_ref=src, dst_ref=dst, send_sem=send_sem, recv_sem=recv_sem,
        device_id=device, device_id_type=MESH,
    )
    copy.start()
    return copy


class ChanGather:
    def __init__(self, src, place, sems, mine, core_peer, x_peer):
        self.place, self.sems, self.mine, self.core_peer = (place, sems, mine, core_peer)
        self.over_x = send(src, place(mine), sems.at[0], sems.at[1], x_peer)
        self.over_core = send(src, place(mine), sems.at[2], sems.at[3], core_peer)

    def relay(self):
        self.over_x.wait_recv()
        block = self.place(flip(self.mine, 2))
        self.onward = send(block, block, self.sems.at[4], self.sems.at[5], self.core_peer)

    def finish(self):
        self.over_core.wait_recv()
        self.onward.wait_recv()
        for copy in (self.over_x, self.over_core, self.onward):
            copy.wait_send()


def ring_position(index, count):
    return lax.div(index, 2) + lax.rem(index, 2) * (count - 1 - 2 * lax.div(index, 2))


def ring_device(position, count):
    position = lax.rem(position + 2 * count, count)
    back = lax.div(position, count // 2)
    return 2 * position + back * (2 * (count - 1 - position) + 1 - 2 * position)


class RingGather:
    def __init__(self, place, sems, count, mine, chan, more_left):
        self.place, self.sems, self.count, self.chan = (place, sems, count, chan)
        self.position = ring_position(mine, count)
        most = count // 2
        self.steps = (most, count - 1 - most) if more_left else (count - 1 - most, most)
        self.length = most
        self.copies = []
        self.step = 0
        self.launch()

    def source(self, side, step):
        return ring_device(self.position + (step if side else -step), self.count)

    def launch(self):
        for side in range(2):
            if self.step < self.steps[side]:
                block = self.place(self.source(side, self.step))
                towards = ring_device(self.position + (-1 if side else 1), self.count)
                sems = self.sems.at[side, self.step]
                self.copies.append(send(block, block, sems.at[0], sems.at[1], (towards, self.chan)))

    def advance(self):
        if self.step == self.length:
            return []
        arrived = []
        for side in range(2):
            if self.step < self.steps[side]:
                source = self.source(side, self.step + 1)
                block = self.place(source)
                sems = self.sems.at[side, self.step]
                pltpu.make_async_remote_copy(
                    src_ref=block, dst_ref=block, send_sem=sems.at[0], recv_sem=sems.at[1],
                    device_id=(source, self.chan), device_id_type=MESH,
                ).wait_recv()
                arrived.append(source)
        self.step += 1
        self.launch()
        return arrived

    def finish(self):
        while self.step < self.length:
            self.advance()
        for copy in self.copies:
            copy.wait_send()


class GridGather:
    def __init__(self, place, ring_sems, chan_sems, count, me_s, me_c, core_peer, x_peer):
        self.place, self.mine, self.sems = (place, me_c, chan_sems)
        self.peers = (core_peer, x_peer)
        self.ring = RingGather(lambda d: place(me_c, d), ring_sems, count, me_s, me_c, True)
        self.gathers = []
        self.relayed = 0

    def advance(self):
        for source in self.ring.advance():
            self.gathers.append(
                ChanGather(
                    self.place(self.mine, source), partial(self.at, source), self.sems.at[len(self.gathers)],
                    self.mine, *self.peers,
                )
            )

    def at(self, source, chan):
        return self.place(chan, source)

    def relay(self, upto):
        while self.relayed < min(upto, len(self.gathers)):
            self.gathers[self.relayed].relay()
            self.relayed += 1

    def finish(self):
        self.ring.finish()
        for gather in self.gathers:
            gather.finish()


class ChanSum:
    def __init__(self, own, first, second, middle, sems, core_peer, x_peer):
        self.own, self.first, self.second, self.middle = (own, first, second, middle)
        self.sems, self.x_peer = (sems, x_peer)
        self.copies = [send(own, first, sems.at[0], sems.at[1], core_peer)]

    def cross(self):
        self.copies[0].wait_recv()
        self.middle[...] = self.own[...] + self.first[...]
        self.copies.append(send(self.middle, self.second, self.sems.at[2], self.sems.at[3], self.x_peer))

    def finish(self):
        self.copies[1].wait_recv()
        for copy in self.copies:
            copy.wait_send()
        return self.middle[...] + self.second[...]


class ChanScatter:
    def __init__(self, blocks, first, second, sems, mine, core_peer, x_peer, extra=None):
        self.blocks, self.first, self.second, self.sems = (blocks, first, second, sems)
        self.mine, self.x_peer, self.extra = (mine, x_peer, extra)
        other = flip(mine, 1)
        self.copies = [
            send(blocks.at[other], first.at[0], sems.at[0], sems.at[1], core_peer),
            send(blocks.at[flip(other, 2)], first.at[1], sems.at[2], sems.at[3], core_peer),
        ]
        if extra is not None:
            self.copies.append(send(extra[0], extra[1], sems.at[6], sems.at[7], core_peer))

    def cross(self):
        for copy in self.copies:
            copy.wait_recv()
        far = flip(self.mine, 2)
        self.blocks[far] = (self.blocks[far].astype(F32) + self.first[1].astype(F32)).astype(BF16)
        self.last = [send(self.blocks.at[far], self.second, self.sems.at[4], self.sems.at[5], self.x_peer)]
        if self.extra is not None:
            own, near, middle, across = self.extra
            middle[...] = own[...] + near[...]
            self.last.append(send(middle, across, self.sems.at[8], self.sems.at[9], self.x_peer))

    def finish(self):
        for copy in self.last:
            copy.wait_recv()
        for copy in self.copies + self.last:
            copy.wait_send()
        total = self.blocks[self.mine].astype(F32) + self.first[0].astype(F32) + self.second[...].astype(F32)
        if self.extra is None:
            return total
        return total, self.extra[2][...] + self.extra[3][...]


class SeqSum:
    def __init__(self, held, landing, full, sems, bits, mine, chan):
        self.held, self.landing, self.full, self.sems, self.bits = (held, landing, full, sems, bits)
        self.mine, self.chan = (mine, chan)
        self.regions = []
        self.copies = []
        start, size, place = (0, held.shape[0], 0)
        for bit in bits:
            half = size // 2
            mine_bit = lax.rem(lax.div(mine, bit), 2)
            keep = pl.multiple_of(start + mine_bit * half, 16)
            give = pl.multiple_of(start + (1 - mine_bit) * half, 16)
            self.regions.append((keep, give, half, place))
            start, size, place = (keep, half, place + half)
        self.step = 0
        self.total = 2 * len(bits)
        self.launch()

    def launch(self):
        step, count = (self.step, len(self.bits))
        sems = (self.sems.at[2 * step], self.sems.at[2 * step + 1])
        if step < count:
            _, give, half, place = self.regions[step]
            src, dst = (self.held.at[pl.ds(give, half)], self.landing.at[pl.ds(place, half)])
            bit = self.bits[step]
        else:
            keep, _, half, _ = self.regions[self.total - 1 - step]
            src = dst = self.full.at[pl.ds(keep, half)]
            bit = self.bits[self.total - 1 - step]
        self.copies.append(send(src, dst, *sems, (flip(self.mine, bit), self.chan)))

    def advance(self):
        if self.step == self.total:
            return
        self.copies[-1].wait_recv()
        if self.step < len(self.bits):
            keep, _, half, place = self.regions[self.step]
            rows = pl.ds(keep, half)
            got = self.landing[pl.ds(place, half)].astype(F32)
            into = self.held if self.step < len(self.bits) - 1 else self.full
            into[rows] = (self.held[rows].astype(F32) + got).astype(BF16)
        self.step += 1
        if self.step < self.total:
            self.launch()

    def finish(self):
        while self.step < self.total:
            self.advance()
        for copy in self.copies:
            copy.wait_send()


def layer_kernel(names, seq_devices, *refs):
    r = SimpleNamespace(**dict(zip(names, refs)))
    x_ref, og_ref, win_ref, wout_ref = (r.inputs, r.out_grad, r.w_in, r.w_out)
    xw_ref, dtw_ref = (r.x_weight, r.dt_weight)
    seqs, tokens, shard = x_ref.shape
    model, width = win_ref.shape[1:]
    states = r.log_decay.shape[0]
    low_rank = dtw_ref.shape[0]
    taps = r.conv_weight.shape[0]
    proj = xw_ref.shape[0]
    me_s, me_c = (lax.axis_index("seq"), lax.axis_index("chan"))
    core_peer, x_peer = ((me_s, flip(me_c, 1)), (me_s, flip(me_c, 2)))
    right, left = (lax.rem(me_s + 1, seq_devices), lax.rem(me_s + seq_devices - 1, seq_devices))
    position = ring_position(me_s, seq_devices)
    gathered = seq_devices <= MOST_GATHERED
    spot = me_s if gathered else 0

    barrier = pltpu.get_barrier_semaphore()

    def greet(semaphore, device):
        pl.semaphore_signal(semaphore, inc=1, device_id=device, device_id_type=MESH)

    ring = [(ring_device(position + step, seq_devices), me_c) for step in (1, -1)]
    first_peers = [core_peer, x_peer, (right, me_c), (left, me_c)] + ring
    for device in first_peers:
        greet(barrier, device)
    pl.semaphore_wait(barrier, len(first_peers))

    xo_ref, halo_ref = (r.xo, r.halo)
    gather_x = ChanGather(x_ref, lambda q: xo_ref.at[q, spot, 0], r.x_sems, me_c, core_peer, x_peer)
    halo_copy = send(
        x_ref.at[:, pl.ds(tokens - HALO, HALO), :], halo_ref.at[me_c, pl.ds(0, seqs)],
        r.halo_sems.at[6], r.halo_sems.at[7], (right, me_c),
    )
    for device in ring:
        greet(r.known.at[0], device)
    gather_og = ChanGather(og_ref, lambda q: xo_ref.at[q, spot, 1], r.og_sems, me_c, core_peer, x_peer)
    xo_ref[me_c, spot, 0] = x_ref[...]
    xo_ref[me_c, spot, 1] = og_ref[...]
    halo_ref[me_c, seqs] = jnp.broadcast_to(r.norm_gain[...], (HALO, shard))
    if gathered:
        gather_all = GridGather(
            lambda q, d: xo_ref.at[q, d], r.xo_ring_sems, r.xo_chan_sems, seq_devices, me_s, me_c, core_peer, x_peer
        )
    halo_copy.wait_recv()
    gather_halo = ChanGather(
        halo_ref.at[me_c], lambda q: halo_ref.at[q], r.halo_sems, me_c, core_peer, x_peer
    )
    gather_x.relay()
    gather_halo.relay()
    gather_x.finish()
    gather_halo.finish()
    halo_copy.wait_send()
    gather_og.relay()

    reaches = [1]
    while 2 * reaches[-1] < seq_devices // 2:
        reaches.append(2 * reaches[-1])

    def hear(k):
        pl.semaphore_wait(r.known.at[k], 2)
        if k + 1 < len(reaches):
            for step in (reaches[k + 1], -reaches[k + 1]):
                greet(r.known.at[k + 1], (ring_device(position + step, seq_devices), me_c))

    hear(0)

    rate_ref, rate2_ref = (r.rate, r.rate2)
    rate_ref[...] = -jnp.exp(r.log_decay[...])
    rate2_ref[...] = rate_ref[...] * LOG2E

    def mask_of(s, rows, begin):
        positions = me_s * tokens + begin + lax.broadcasted_iota(jnp.int32, (rows, 1), 0)
        return (positions < r.lengths[s]).astype(F32)

    def gain_of(q):
        return halo_ref[q, seqs, 0:1, :].astype(F32)

    def normalize(blocks):
        squares = sum(jnp.sum(b * b, axis=1, keepdims=True) for b in blocks)
        root = lax.rsqrt(squares * (1.0 / model) + EPSILON)
        return root, [(b * root * gain_of(q)).astype(BF16) for q, b in enumerate(blocks)]

    conv_sum = []
    normed_rows = []
    has_left = (me_s > 0).astype(F32)
    for s in range(seqs):
        mine = pl.ds(s * tokens, tokens)
        root, rows = normalize([xo_ref[q, spot, 0, s].astype(F32) for q in range(4)])
        _, before = normalize([halo_ref[q, s].astype(F32) for q in range(4)])
        r.root[mine, :] = jnp.broadcast_to(root, (tokens, LANES))
        normed, normed_before = (jnp.concatenate(rows, axis=1), jnp.concatenate(before, axis=1))
        normed_rows.append(pl.ds(pl.multiple_of(spot * seqs * tokens + s * tokens, tokens), tokens))
        r.normed[normed_rows[s], :] = normed
        inner = dot(normed, win_ref[0]).astype(BF16).astype(F32) * mask_of(s, tokens, 0)
        inner_before = dot(normed_before, win_ref[0]).astype(BF16).astype(F32)
        inner_before = inner_before * (mask_of(s, HALO, -HALO) * has_left)
        r.inner[s, HALO:, :] = inner
        r.inner[s, :HALO, :] = inner_before
        conv_pre = r.conv_bias[...] + sum(
            r.conv_weight[k : k + 1, :] * r.inner[s, HALO - taps + 1 + k : HALO - taps + 1 + k + tokens, :]
            for k in range(taps)
        )
        r.conv_pre[mine, :] = conv_pre
        act = (conv_pre * jax.nn.sigmoid(conv_pre)).astype(BF16)
        r.act[mine, :] = act.astype(F32)
        r.proj_own[s] = dot(xw_ref[...], act, ((1,), (1,)))
        conv_sum.append(
            ChanSum(
                r.proj_own.at[s], r.proj_first.at[s], r.proj_second.at[s], r.proj_mid.at[s],
                r.proj_sems.at[s], core_peer, x_peer,
            )
        )
    for s in range(seqs):
        conv_sum[s].cross()
    for s in range(seqs):
        mine = pl.ds(s * tokens, tokens)
        r.gate_pre[mine, :] = dot(r.normed[normed_rows[s], :], win_ref[1])
    gather_og.finish()
    for s in range(seqs):
        mine = pl.ds(s * tokens, tokens)
        cot = jnp.concatenate([xo_ref[q, spot, 1, s] for q in range(4)], axis=1)
        grad_mixed = dot(cot, wout_ref[...], ((1,), (1,))) * mask_of(s, tokens, 0)
        gate = r.gate_pre[mine, :]
        sigmoid = jax.nn.sigmoid(gate)
        r.grad_mixed[mine, :] = grad_mixed
        r.up[mine, :] = grad_mixed * (gate * sigmoid)
        if gathered:
            rows = normed_rows[s]
            r.gate_act_all[rows, :] = (gate * sigmoid * mask_of(s, tokens, 0)).astype(BF16)
            r.gate_slope_all[rows, :] = (grad_mixed * silu_slope(gate, sigmoid)).astype(BF16)
        else:
            r.cot[mine, :] = (cot.astype(F32) * mask_of(s, tokens, 0)).astype(BF16)
    if gathered:
        gather_all.advance()

    totals_ref = r.totals
    step_totals = []
    for s in range(seqs):
        mine = pl.ds(s * tokens, tokens)
        projected = conv_sum[s].finish()
        low = projected[:low_rank].astype(BF16)
        r.low[:, s * tokens : (s + 1) * tokens] = low
        step_pre = dot(projected[:low_rank].T.astype(BF16), dtw_ref[...]) + r.dt_bias[...]
        r.step_pre[mine, :] = step_pre
        step = softplus(step_pre)
        r.step[mine, :] = step
        r.drive[mine, :] = step * r.act[mine, :]
        step_totals.append(jnp.sum(step, axis=0, keepdims=True))
        spread_maps(projected[low_rank:], r.b, r.c, s * tokens, tokens)
    totals_ref[me_s] = jnp.concatenate(step_totals + [jnp.zeros((8 - seqs, width), F32)], axis=0)

    def seq_device(k):
        return (k, me_c)

    def totals_copy(k):
        peer = lax.rem(me_s + k, seq_devices)
        return pltpu.make_async_remote_copy(
            src_ref=totals_ref.at[me_s], dst_ref=totals_ref.at[me_s],
            send_sem=r.totals_send.at[k], recv_sem=r.totals_recv.at[me_s],
            device_id=seq_device(peer), device_id_type=MESH,
        )

    def start_totals(k, _):
        totals_copy(k).start()
        return 0

    for k in range(1, len(reaches)):
        hear(k)
    lax.fori_loop(1, seq_devices, start_totals, 0)

    ends_refs = (r.ends, r.ends_send, r.ends_recv)
    leaves_refs = (r.leaves, r.leaves_send, r.leaves_recv)

    def carried_copy(which, s, peer):
        ref, send_sem, recv_sem = which
        return pltpu.make_async_remote_copy(
            src_ref=ref.at[s, me_s], dst_ref=ref.at[s, me_s],
            send_sem=send_sem.at[s, peer], recv_sem=recv_sem.at[s, me_s],
            device_id=seq_device(peer), device_id_type=MESH,
        )

    def start_carried(which, s, begin, end):
        def start(peer, _):
            carried_copy(which, s, peer).start()
            return 0

        lax.fori_loop(begin, end, start, 0)

    def wait_carried(which, s, begin, end):
        def wait(peer, _):
            carried_copy(which, s, peer).wait_send()
            return 0

        lax.fori_loop(begin, end, wait, 0)

    for s in range(seqs):
        ends = local_states(r.decay, r.step, r.drive, r.b, rate2_ref, s * tokens, tokens)
        for k, lanes in enumerate(lane_chunks(width)):
            r.ends[s, me_s, :, lanes] = ends[k].astype(BF16)
        start_carried(ends_refs, s, me_s + 1, seq_devices)
    if gathered:
        gather_all.advance()
        gather_all.relay(1)
    for s in range(seqs):
        leaves = local_adjoints(r.decay, r.up, r.c, rate_ref, s * tokens, tokens)
        for k, lanes in enumerate(lane_chunks(width)):
            r.leaves[s, me_s, :, lanes] = leaves[k].astype(BF16)
        start_carried(leaves_refs, s, 0, me_s)

    def wait_totals(k, _):
        peer = lax.rem(me_s + k, seq_devices)
        pltpu.make_async_remote_copy(
            src_ref=totals_ref.at[peer], dst_ref=totals_ref.at[peer],
            send_sem=r.totals_send.at[k], recv_sem=r.totals_recv.at[peer],
            device_id=seq_device(peer), device_id_type=MESH,
        ).wait_recv()
        return 0

    lax.fori_loop(1, seq_devices, wait_totals, 0)

    def combine(which, s, count, place):
        ref, send_sem, recv_sem = which

        def turn(k, held):
            peer = place(k)
            pltpu.make_async_remote_copy(
                src_ref=ref.at[s, peer], dst_ref=ref.at[s, peer],
                send_sem=send_sem.at[s, peer], recv_sem=recv_sem.at[s, peer],
                device_id=seq_device(peer), device_id_type=MESH,
            ).wait_recv()
            total = totals_ref[peer][s : s + 1]
            return jnp.exp2(total * rate2_ref[...]) * held + ref[s, peer].astype(F32)

        return lax.fori_loop(0, count, turn, jnp.zeros((states, width), F32))

    skip_gathers, inner_gathers = ([], [])

    def block_of(ref, s, device):
        return ref.at[device, s]

    def foreign(k, _):
        device = lax.rem(me_s + k, seq_devices)
        rows = pl.ds(pl.multiple_of(device * (seqs * tokens), seqs * tokens), seqs * tokens)
        blocks = [xo_ref[q, device, 0].reshape(seqs * tokens, shard).astype(F32) for q in range(4)]
        normed = jnp.concatenate(normalize(blocks)[1], axis=1)
        r.normed[rows, :] = normed
        gate = dot(normed, win_ref[1])
        sigmoid = jax.nn.sigmoid(gate)
        cot = jnp.concatenate([xo_ref[q, device, 1].reshape(seqs * tokens, shard) for q in range(4)], axis=1)
        mask = jnp.concatenate([mask_of(s, tokens, (device - me_s) * tokens) for s in range(seqs)], axis=0)
        grad_mixed = dot(cot, wout_ref[...], ((1,), (1,))) * mask
        r.gate_act_all[rows, :] = (gate * sigmoid * mask).astype(BF16)
        r.gate_slope_all[rows, :] = (grad_mixed * silu_slope(gate, sigmoid)).astype(BF16)
        return 0

    for s in range(seqs):
        mine = pl.ds(s * tokens, tokens)
        r.entering[s] = combine(ends_refs, s, me_s, lambda k: k)
        run_states(
            r.decay, r.drive, r.b, r.c, r.entering, r.state, r.scanned, s, s * tokens, tokens
        )
        gate = r.gate_pre[mine, :]
        sigmoid = jax.nn.sigmoid(gate)
        with_skip = r.scanned[...] + r.skip_gain[...] * r.act[mine, :]
        mixed = (with_skip * (gate * sigmoid)).astype(BF16)
        r.mixed[mine, :] = mixed
        r.grad_gate[mine, :] = (r.grad_mixed[mine, :] * with_skip * silu_slope(gate, sigmoid)).astype(BF16)
        if gathered:
            r.skip_all[me_s, s] = with_skip.astype(BF16)
            skip_gathers.append(
                RingGather(
                    partial(block_of, r.skip_all, s), r.skip_sems.at[s], seq_devices, me_s, me_c, s == 0
                )
            )
    out_part = dot(r.mixed[...], wout_ref[...])
    for q in range(4):
        r.out_blocks[q] = out_part[:, q * shard : (q + 1) * shard].astype(BF16)
    scatter_out = ChanScatter(
        r.out_blocks, r.out_first, r.out_second, r.out_sems, me_c, core_peer, x_peer
    )
    sums = []
    bits = [1 << k for k in range(seq_devices.bit_length() - 1)]
    turned = bits[1:] + bits[:1]
    if gathered:
        gather_all.advance()
        gather_all.relay(3)
    else:
        r.grad_w_out[...] = dot(r.mixed[...], r.cot[...], ((0,), (0,))).astype(BF16)
        sums.append(SeqSum(r.grad_w_out, r.land_w_out, r.out_w_out, r.w_out_sems, bits, me_s, me_c))
        r.grad_w_gate[...] = dot(r.normed[...], r.grad_gate[...], ((0,), (0,))).astype(BF16)
        sums.append(SeqSum(r.grad_w_gate, r.land_w_gate, r.out_w_in.at[1], r.w_gate_sems, turned, me_s, me_c))

    small = r.small
    small[...] = jnp.zeros_like(small)
    decay_row = proj + low_rank
    tap_row = decay_row + states
    low_sum, rim_copies, rate_sums = ([], [], [])
    has_right = (me_s < seq_devices - 1).astype(F32)

    def scan_back(s, services):
        leaving = combine(leaves_refs, s, seq_devices - 1 - me_s, lambda k: seq_devices - 1 - k)
        carried = (tuple(leaving[:, lanes] for lanes in lane_chunks(width)), zero_states(rate_ref))
        parts, blocks = (len(services), tokens // 8)
        for part, service in enumerate(services):
            carried = run_adjoints(
                r.decay, r.step, r.up, r.b, r.c, rate_ref, r.entering, r.state,
                r.adjoint, r.first_sum, r.second_sum, s, s * tokens, tokens,
                (part * blocks // parts, (part + 1) * blocks // parts), carried,
            )
            service()
        rate_sums.append(carried[1])

    def after_scan(s):
        mine = pl.ds(s * tokens, tokens)
        act, step, step_pre = (r.act[mine, :], r.step[mine, :], r.step_pre[mine, :])
        second = r.second_sum[...]
        grad_step_pre = (r.first_sum[...] + act * second) * jax.nn.sigmoid(step_pre)
        grad_step_low = grad_step_pre.astype(BF16)
        own = r.proj_own.at[s]
        own[:low_rank, :] = dot(dtw_ref[...], grad_step_low, ((1,), (1,)))
        own[low_rank : low_rank + states, :] = map_sums(r.adjoint, r.drive[mine, :], states, 0, tokens)
        own[low_rank + states :, :] = map_sums(r.state, r.up[mine, :], states, s * tokens, tokens)
        low_sum.append(
            ChanSum(
                own, r.back_first.at[s], r.back_second.at[s], r.back_mid.at[s],
                r.back_sems.at[s], core_peer, x_peer,
            )
        )
        r.grad_step_low[mine, :] = grad_step_low
        small[tap_row + taps + 1, :] += jnp.sum(grad_step_pre, axis=0)
        small[tap_row + taps + 2, :] += jnp.sum(r.up[mine, :] * act, axis=0)
        r.grad_act[mine, :] = step * second + r.up[mine, :] * r.skip_gain[...]

    def through_conv(s):
        mine = pl.ds(s * tokens, tokens)
        grad_projected = low_sum[s].finish()
        r.grad_proj[:, s * tokens : (s + 1) * tokens] = grad_projected.astype(BF16)
        grad_act = r.grad_act[mine, :] + dot(grad_projected.T.astype(BF16), xw_ref[...])
        conv_pre = r.conv_pre[mine, :]
        grad_conv = (grad_act * silu_slope(conv_pre, jax.nn.sigmoid(conv_pre))).astype(BF16)
        r.rim_own[s] = grad_conv[:HALO]
        rim_copies.append(
            send(r.rim_own.at[s], r.rim.at[s], r.rim_sems.at[2 * s], r.rim_sems.at[2 * s + 1], (left, me_c))
        )
        grad_conv = grad_conv.astype(F32)
        r.grad_conv[s, :tokens, :] = grad_conv
        small[tap_row + taps, :] += jnp.sum(grad_conv, axis=0)
        for k in range(taps):
            shifted = r.inner[s, HALO - taps + 1 + k : HALO - taps + 1 + k + tokens, :]
            small[tap_row + k, :] += jnp.sum(grad_conv * shifted, axis=0)

    def inner_of(s):
        mine = pl.ds(s * tokens, tokens)
        rim_copies[s].wait_recv()
        rim_copies[s].wait_send()
        r.grad_conv[s, tokens:, :] = r.rim[s].astype(F32) * has_right
        grad_inner = sum(
            r.conv_weight[k : k + 1, :] * r.grad_conv[s, taps - 1 - k : taps - 1 - k + tokens, :]
            for k in range(taps)
        )
        grad_inner = (grad_inner * mask_of(s, tokens, 0)).astype(BF16)
        r.grad_inner[mine, :] = grad_inner
        if gathered:
            r.inner_all[me_s, s] = grad_inner
            inner_gathers.append(
                RingGather(
                    partial(block_of, r.inner_all, s), r.inner_sems.at[s], seq_devices, me_s, me_c, s == 0
                )
            )

    def all_advance():
        for item in sums + skip_gathers + inner_gathers:
            item.advance()

    def grid_advance(upto):
        if gathered:
            gather_all.advance()
            gather_all.relay(upto)

    def nothing():
        pass

    scan_back(0, (scatter_out.cross, all_advance, partial(grid_advance, 5), all_advance))
    after_scan(0)
    scan_back(1, (low_sum[0].cross, all_advance, partial(through_conv, 0), all_advance))
    after_scan(1)
    inner_of(0)
    low_sum[1].cross()
    if gathered:
        gather_all.relay(7)
        gather_all.finish()
        lax.fori_loop(1, 3, foreign, 0)
    out_sum = scatter_out.finish()
    for s in range(seqs):
        r.mixed_out[s] = (x_ref[s].astype(F32) + out_sum[s * tokens : (s + 1) * tokens]).astype(BF16)
    through_conv(1)
    for k, lanes in enumerate(lane_chunks(width)):
        small[decay_row:tap_row, lanes] = (rate_sums[0][k] + rate_sums[1][k]) * rate_ref[:, lanes]
    small[proj:decay_row, :] = dot(r.low[...], r.grad_step_low[...])
    small[:proj, :] = dot(r.grad_proj[...], r.act[...].astype(BF16))
    for item in sums:
        item.advance()
    inner_of(1)

    if gathered:
        r.grad_small[...] = small[...].astype(BF16)
        sums.append(SeqSum(r.grad_small, r.land_small, r.out_small, r.small_sems, bits, me_s, me_c))
    else:
        late = r.grad_w_inner
        late[:model, :] = dot(r.normed[...], r.grad_inner[...], ((0,), (0,))).astype(BF16)
        late[model:, :] = small[...].astype(BF16)
        sums.append(SeqSum(late, r.land_w_inner, r.full_w_inner, r.w_inner_sems, bits, me_s, me_c))
    moment = None
    for q in range(4):
        part = dot(r.grad_inner[...], win_ref[0, q * shard : (q + 1) * shard, :], ((1,), (1,)))
        part = part + dot(r.grad_gate[...], win_ref[1, q * shard : (q + 1) * shard, :], ((1,), (1,)))
        values = xo_ref[q, spot, 0].reshape(seqs * tokens, shard).astype(F32)
        term = jnp.sum(part * gain_of(q) * values, axis=1, keepdims=True)
        moment = term if moment is None else moment + term
        r.gn_blocks[q] = part.astype(BF16)
    r.moment[...] = jnp.broadcast_to(moment, (seqs * tokens, LANES)).T[:8]
    scatter_gn = ChanScatter(
        r.gn_blocks, r.gn_first, r.gn_second, r.gn_sems, me_c, core_peer, x_peer,
        (r.moment, r.moment_first, r.moment_mid, r.moment_second),
    )
    if gathered:
        lax.fori_loop(3, 5, foreign, 0)
    scatter_gn.cross()
    all_advance()
    if gathered:
        lax.fori_loop(5, seq_devices, foreign, 0)
        all_advance()
    grad_normed, moment_row = scatter_gn.finish()
    moment = jnp.broadcast_to(moment_row[:1], (LANES, seqs * tokens)).T[:, :1]
    root = r.root[:, :1]
    values = x_ref[...].reshape(seqs * tokens, shard).astype(F32)
    gains = r.norm_gain[...].astype(F32)
    back = root * (grad_normed * gains) - values * (root * root * root) * moment * (1.0 / model)
    for s in range(seqs):
        mine = slice(s * tokens, (s + 1) * tokens)
        cot = og_ref[s].astype(F32) * mask_of(s, tokens, 0)
        r.grad_inputs[s] = (cot + back[mine]).astype(BF16)
    gain_sums_ref = r.gain_sums
    gain_sums_ref[me_s] = jnp.broadcast_to(jnp.sum(grad_normed * values * root, axis=0, keepdims=True), (8, shard))

    def gain_copy(k):
        peer = lax.rem(me_s + k, seq_devices)
        return pltpu.make_async_remote_copy(
            src_ref=gain_sums_ref.at[me_s], dst_ref=gain_sums_ref.at[me_s],
            send_sem=r.gain_sums_send.at[k], recv_sem=r.gain_sums_recv.at[me_s],
            device_id=seq_device(peer), device_id_type=MESH,
        )

    def start_gain(k, _):
        gain_copy(k).start()
        return 0

    lax.fori_loop(1, seq_devices, start_gain, 0)
    if gathered:
        all_advance()
        for gather in skip_gathers:
            gather.finish()
        count = seq_devices * seqs * tokens

        def mix(device, _):
            rows = pl.ds(pl.multiple_of(device * (seqs * tokens), seqs * tokens), seqs * tokens)
            with_skip = r.skip_all[device].reshape(seqs * tokens, width).astype(F32)
            r.gate_act_all[rows, :] = (r.gate_act_all[rows, :].astype(F32) * with_skip).astype(BF16)
            r.gate_slope_all[rows, :] = (r.gate_slope_all[rows, :].astype(F32) * with_skip).astype(BF16)
            return 0

        lax.fori_loop(0, seq_devices, mix, 0)
        results = []

        def deliver(src, dst):
            copy = pltpu.make_async_copy(src, dst, r.result_sems.at[len(results)])
            copy.start()
            results.append(copy)

        staged = r.skip_all.reshape(count, width)
        for q in range(4):
            outs = xo_ref[q, :, 1].reshape(count, shard)
            half, place = (q * shard // width, q * shard % width)
            rows = pl.ds(half * width, width)
            staged[rows, place : place + shard] = dot(r.gate_act_all[...], outs, ((0,), (0,))).astype(BF16)
            if place + shard == width:
                deliver(staged.at[rows], r.out_w_out.at[:, pl.ds(half * width, width)])
            all_advance()
        for q in range(4):
            rows = slice(q * shard, (q + 1) * shard)
            r.gate_act_all[rows, :] = dot(r.normed[:, rows], r.gate_slope_all[...], ((0,), (0,))).astype(BF16)
            all_advance()
        deliver(r.gate_act_all.at[pl.ds(0, model)], r.out_w_in.at[1])
        for gather in inner_gathers:
            gather.finish()
        inner_rows = r.inner_all[...].reshape(count, width)
        for q in range(4):
            rows = slice(model + q * shard, model + (q + 1) * shard)
            cols = slice(q * shard, (q + 1) * shard)
            r.gate_act_all[rows, :] = dot(r.normed[:, cols], inner_rows, ((0,), (0,))).astype(BF16)
            if q % 2 == 1:
                deliver(
                    r.gate_act_all.at[pl.ds(model + (q - 1) * shard, 2 * shard)],
                    r.out_w_in.at[0, pl.ds((q - 1) * shard, 2 * shard)],
                )
            all_advance()
    else:
        for step in range(max(item.total for item in sums)):
            all_advance()

    def take_gain(k, _):
        peer = lax.rem(me_s + k, seq_devices)
        pltpu.make_async_remote_copy(
            src_ref=gain_sums_ref.at[peer], dst_ref=gain_sums_ref.at[peer],
            send_sem=r.gain_sums_send.at[k], recv_sem=r.gain_sums_recv.at[peer],
            device_id=seq_device(peer), device_id_type=MESH,
        ).wait_recv()
        gain_copy(k).wait_send()
        totals_copy(k).wait_send()
        return 0

    lax.fori_loop(1, seq_devices, take_gain, 0)
    r.grad_gain[...] = jnp.sum(gain_sums_ref[...], axis=0)
    for item in sums:
        item.finish()
    if gathered:
        for copy in results:
            copy.wait()
    else:
        r.out_w_in[0] = r.full_w_inner[:model, :]
        r.out_small[...] = r.full_w_inner[model:, :]
    for s in range(seqs):
        wait_carried(ends_refs, s, me_s + 1, seq_devices)
        wait_carried(leaves_refs, s, 0, me_s)


def finish_kernel(
    rows_of, mixed_ref, inputs_ref, w_in_ref, w_out_ref, small_ref, gain_ref,
    mixed_out, grad_inputs, gain_out, w_in_out, conv_w_out, conv_b_out, x_out, dt_w_out, dt_b_out, decay_out,
    skip_out, w_out_out,
):
    mixed_out[...] = mixed_ref[...]
    grad_inputs[...] = inputs_ref[...]
    w_in_out[...] = w_in_ref[...].astype(F32)
    w_out_out[...] = w_out_ref[...].astype(F32)

    @pl.when(pl.program_id(0) == 0)
    def _():
        proj, low_rank, states, taps = rows_of
        small = small_ref[...].astype(F32)
        decay_row = proj + low_rank
        tap_row = decay_row + states
        gain_out[...] = gain_ref[0:1, :]
        x_out[...] = small[:proj]
        dt_w_out[...] = small[proj:decay_row]
        decay_out[...] = small[decay_row:tap_row]
        conv_w_out[...] = small[tap_row : tap_row + taps]
        conv_b_out[...] = small[tap_row + taps : tap_row + taps + 1]
        dt_b_out[...] = small[tap_row + taps + 1 : tap_row + taps + 2]
        skip_out[...] = small[tap_row + taps + 2 : tap_row + taps + 3]


def layer(
    seq_devices,
    inputs, lengths, out_grad, norm_gain, w_in, conv_weight, conv_bias, x_weight, dt_weight,
    dt_bias, log_decay, skip_gain, w_out,
):
    seqs, tokens, shard = inputs.shape
    _, model, width = w_in.shape
    states, low_rank, taps, proj = (log_decay.shape[0], dt_weight.shape[0], conv_weight.shape[0], x_weight.shape[0])
    rows = seqs * tokens
    small_rows = proj + low_rank + states + taps + 3
    grain = 16 * seq_devices
    small_rows = -(-small_rows // grain) * grain
    steps = 4 * (seq_devices.bit_length() - 1)
    gathered = seq_devices <= MOST_GATHERED
    dma = pltpu.SemaphoreType.DMA
    vmem = pltpu.VMEM
    operands = dict(
        inputs=inputs, lengths=lengths, out_grad=out_grad, norm_gain=norm_gain.reshape(1, shard),
        w_in=w_in, conv_weight=conv_weight, conv_bias=conv_bias.reshape(1, width),
        x_weight=x_weight, dt_weight=dt_weight, dt_bias=dt_bias.reshape(1, width),
        log_decay=log_decay, skip_gain=skip_gain.reshape(1, width), w_out=w_out,
    )
    outputs = dict(
        mixed_out=(inputs.shape, BF16), grad_inputs=(inputs.shape, BF16), grad_gain=((8, shard), F32),
        out_w_in=(w_in.shape, BF16), out_w_out=(w_out.shape, BF16), out_small=((small_rows, width), BF16),
    )
    wide = (rows, width)
    scratch = dict(
        xo=vmem((4, seq_devices if gathered else 1, 2) + inputs.shape, BF16),
        halo=vmem((4, seqs + 1, HALO, shard), BF16), known=pltpu.SemaphoreType.REGULAR((8,)),
        x_sems=dma((6,)), og_sems=dma((6,)), halo_sems=dma((8,)),
        rate=vmem((states, width), F32), rate2=vmem((states, width), F32),
        root=vmem((rows, LANES), F32), normed=vmem((seq_devices * rows if gathered else rows, model), BF16),
        inner=vmem((seqs, HALO + tokens, width), F32),
        conv_pre=vmem(wide, F32), act=vmem(wide, F32), gate_pre=vmem(wide, F32),
        grad_mixed=vmem(wide, F32), up=vmem(wide, F32),
        proj_own=vmem((seqs, proj, tokens), F32), proj_first=vmem((seqs, proj, tokens), F32),
        proj_second=vmem((seqs, proj, tokens), F32), proj_mid=vmem((seqs, proj, tokens), F32),
        proj_sems=dma((seqs, 4)),
        back_first=vmem((seqs, proj, tokens), F32), back_second=vmem((seqs, proj, tokens), F32),
        back_mid=vmem((seqs, proj, tokens), F32), back_sems=dma((seqs, 4)),
        low=vmem((low_rank, rows), BF16), step_pre=vmem(wide, F32), step=vmem(wide, F32),
        drive=vmem(wide, F32), b=vmem((rows, states, LANES), F32), c=vmem((rows, states, LANES), F32),
        decay=vmem((rows, states, width), F32),
        totals=vmem((seq_devices, 8, width), F32), totals_send=dma((seq_devices,)),
        totals_recv=dma((seq_devices,)),
        ends=vmem((seqs, seq_devices, states, width), BF16), ends_send=dma((seqs, seq_devices)),
        ends_recv=dma((seqs, seq_devices)),
        leaves=vmem((seqs, seq_devices, states, width), BF16), leaves_send=dma((seqs, seq_devices)),
        leaves_recv=dma((seqs, seq_devices)),
        entering=vmem((seqs, states, width), F32),
        state=vmem((rows, states, width), BF16), adjoint=vmem((tokens, states, width), BF16),
        scanned=vmem((tokens, width), F32), first_sum=vmem((tokens, width), F32),
        second_sum=vmem((tokens, width), F32),
        mixed=vmem(wide, BF16), grad_gate=vmem(wide, BF16), grad_step_low=vmem(wide, BF16),
        grad_act=vmem(wide, F32), grad_proj=vmem((proj, rows), BF16),
        grad_conv=vmem((seqs, tokens + HALO, width), F32), rim_own=vmem((seqs, HALO, width), BF16),
        rim=vmem((seqs, HALO, width), BF16), rim_sems=dma((2 * seqs,)),
        grad_inner=vmem(wide, BF16),
        out_blocks=vmem((4, rows, shard), BF16), out_first=vmem((2, rows, shard), BF16),
        out_second=vmem((rows, shard), BF16), out_sems=dma((6,)),
        gn_blocks=vmem((4, rows, shard), BF16), gn_first=vmem((2, rows, shard), BF16),
        gn_second=vmem((rows, shard), BF16), gn_sems=dma((10,)),
        moment=vmem((8, rows), F32), moment_first=vmem((8, rows), F32),
        moment_mid=vmem((8, rows), F32), moment_second=vmem((8, rows), F32),
        small=vmem((small_rows, width), F32),
        gain_sums=vmem((seq_devices, 8, shard), F32), gain_sums_send=dma((seq_devices,)),
        gain_sums_recv=dma((seq_devices,)),
    )
    if gathered:
        every = (seq_devices * rows, width)
        ring_steps = seq_devices // 2
        scratch.update(
            gate_act_all=vmem(every, BF16), gate_slope_all=vmem(every, BF16),
            skip_all=vmem((seq_devices, seqs, tokens, width), BF16),
            inner_all=vmem((seq_devices, seqs, tokens, width), BF16),
            xo_ring_sems=dma((2, ring_steps, 2)), xo_chan_sems=dma((seq_devices - 1, 6)),
            skip_sems=dma((seqs, 2, ring_steps, 2)), inner_sems=dma((seqs, 2, ring_steps, 2)),
            grad_small=vmem((small_rows, width), BF16), land_small=vmem((small_rows, width), BF16),
            small_sems=dma((steps,)), result_sems=dma((5,)),
        )
    else:
        late = (model + small_rows, width)
        scratch.update(
            cot=vmem((rows, model), BF16),
            grad_w_out=vmem(w_out.shape, BF16), land_w_out=vmem(w_out.shape, BF16), w_out_sems=dma((steps,)),
            grad_w_gate=vmem((model, width), BF16), land_w_gate=vmem((model, width), BF16),
            w_gate_sems=dma((steps,)),
            grad_w_inner=vmem(late, BF16), land_w_inner=vmem(late, BF16), full_w_inner=vmem(late, BF16),
            w_inner_sems=dma((steps,)),
        )
    names = list(operands) + list(outputs) + list(scratch)
    spaces = dict(lengths=pltpu.SMEM)
    mixed_out, grad_inputs, gain, w_in_grad, w_out_grad, small = pl.pallas_call(
        partial(layer_kernel, names, seq_devices),
        out_shape=tuple(jax.ShapeDtypeStruct(*item) for item in outputs.values()),
        in_specs=[pl.BlockSpec(memory_space=spaces.get(name, pltpu.VMEM)) for name in operands],
        out_specs=tuple(
            pl.BlockSpec(memory_space=pl.ANY if gathered and name in ("out_w_in", "out_w_out") else pltpu.VMEM)
            for name in outputs
        ),
        scratch_shapes=list(scratch.values()),
        compiler_params=pltpu.CompilerParams(
            collective_id=0, has_side_effects=True, vmem_limit_bytes=VMEM_LIMIT
        ),
    )(*operands.values())
    parts = 4

    def cut(shape, axis):
        block = tuple(size // parts if k == axis else size for k, size in enumerate(shape))
        return pl.BlockSpec(block, lambda i: tuple(i if k == axis else 0 for k in range(len(shape))))

    def kept(shape):
        return pl.BlockSpec(shape, lambda i: (0,) * len(shape))

    def result(shape, spec, dtype=F32):
        return jax.ShapeDtypeStruct(shape, dtype), spec

    tokens_cut = cut(inputs.shape, 1)
    w_in_cut, w_out_cut = (cut(w_in.shape, 1), cut(w_out.shape, 0))
    wide_row = ((1, width), kept((1, width)))
    results = [
        result(inputs.shape, tokens_cut, BF16), result(inputs.shape, tokens_cut, BF16),
        result((1, shard), kept((1, shard))), result(w_in.shape, w_in_cut),
        result(conv_weight.shape, kept(conv_weight.shape)), result(*wide_row),
        result(x_weight.shape, kept(x_weight.shape)), result(dt_weight.shape, kept(dt_weight.shape)),
        result(*wide_row), result(log_decay.shape, kept(log_decay.shape)), result(*wide_row),
        result(w_out.shape, w_out_cut),
    ]
    out = pl.pallas_call(
        partial(finish_kernel, (proj, low_rank, states, taps)),
        grid=(parts,),
        out_shape=tuple(item[0] for item in results),
        in_specs=[tokens_cut, tokens_cut, w_in_cut, w_out_cut, kept(small.shape), kept(gain.shape)],
        out_specs=tuple(item[1] for item in results),
        compiler_params=pltpu.CompilerParams(vmem_limit_bytes=VMEM_LIMIT),
    )(mixed_out, grad_inputs, w_in_grad, w_out_grad, small, gain)
    flat = (2, 5, 8, 10)
    return tuple(value.reshape(-1) if k in flat else value for k, value in enumerate(out))


def solution(mesh):
    in_specs = (
        P(None, "seq", "chan"), P(), P(None, "seq", "chan"), P("chan"), P(None, None, "chan"),
        P(None, "chan"), P("chan"), P(None, "chan"), P(None, "chan"), P("chan"), P(None, "chan"),
        P("chan"), P("chan", None),
    )
    out_specs = (
        P(None, "seq", "chan"), P(None, "seq", "chan"), P("chan"), P(None, None, "chan"),
        P(None, "chan"), P("chan"), P(None, "chan"), P(None, "chan"), P("chan"), P(None, "chan"),
        P("chan"), P("chan", None),
    )
    body = partial(layer, mesh.shape["seq"])
    return jax.shard_map(body, mesh=mesh, in_specs=in_specs, out_specs=out_specs, check_vma=False)
```

```python
from functools import partial
from types import SimpleNamespace

import jax
import jax.numpy as jnp
from jax import lax
from jax.experimental import pallas as pl
from jax.experimental.pallas import tpu as pltpu
from jax.sharding import PartitionSpec as P

EPSILON = 1e-05
LANES = 128
LOG2E = 1.4426950408889634
VMEM_LIMIT = 60 * 2**20
HALO = 16
MOST_GATHERED = 8
MESH = pl.DeviceIdType.MESH
F32 = jnp.float32
BF16 = jnp.bfloat16


def lane_chunks(width):
    return [slice(k * LANES, (k + 1) * LANES) for k in range(width // LANES)]


def flip(index, bit):
    return index + bit - 2 * bit * lax.rem(lax.div(index, bit), 2)


def dot(a, b, contract=((1,), (0,))):
    return lax.dot_general(a, b, (contract, ((), ())), preferred_element_type=F32)


def silu_slope(values, sigmoid):
    return sigmoid * (1.0 + values * (1.0 - sigmoid))


def softplus(values):
    return jnp.maximum(values, 0.0) + jnp.log1p(jnp.exp(-jnp.abs(values)))


def spread_maps(maps, b_ref, c_ref, first, tokens):
    states = maps.shape[0] // 2

    def block(index, _):
        start = index * 8
        rolled = pltpu.roll(maps, lax.rem(tokens - start, tokens), 1)
        for j in range(8):
            column = jnp.broadcast_to(rolled[:, j : j + 1], (2 * states, LANES))
            b_ref[first + start + j] = column[:states]
            c_ref[first + start + j] = column[states:]
        return 0

    lax.fori_loop(0, tokens // 8, block, 0)


def zero_states(rate_ref):
    states, width = rate_ref.shape
    return tuple(jnp.zeros((states, LANES), F32) for _ in lane_chunks(width))


def local_states(decay_ref, step_ref, drive_ref, b_ref, rate_ref, first, tokens):
    chunks = lane_chunks(rate_ref.shape[1])

    def block(index, held):
        held = list(held)
        rows = pl.ds(pl.multiple_of(first + index * 8, 8), 8)
        steps = [step_ref[rows, lanes] for lanes in chunks]
        drives = [drive_ref[rows, lanes] for lanes in chunks]
        for j in range(8):
            token = first + index * 8 + j
            b = b_ref[token]
            for k, lanes in enumerate(chunks):
                decay = jnp.exp2(steps[k][j : j + 1] * rate_ref[:, lanes])
                decay_ref[token, :, lanes] = decay
                held[k] = decay * held[k] + drives[k][j : j + 1] * b
        return tuple(held)

    return lax.fori_loop(0, tokens // 8, block, zero_states(rate_ref))


def local_adjoints(decay_ref, up_ref, c_ref, rate_ref, first, tokens):
    chunks = lane_chunks(rate_ref.shape[1])

    def block(index, held):
        held = list(held)
        start = first + (tokens // 8 - 1 - index) * 8
        rows = pl.ds(pl.multiple_of(start, 8), 8)
        ups = [up_ref[rows, lanes] for lanes in chunks]
        for j in range(7, -1, -1):
            token = start + j
            c = c_ref[token]
            for k, lanes in enumerate(chunks):
                adjoint = c * ups[k][j : j + 1] + held[k]
                held[k] = decay_ref[token, :, lanes] * adjoint
        return tuple(held)

    return lax.fori_loop(0, tokens // 8, block, zero_states(rate_ref))


def run_states(decay_ref, drive_ref, b_ref, c_ref, enter_ref, state_ref, out_ref, which, first, tokens):
    chunks = lane_chunks(decay_ref.shape[2])

    def block(index, held):
        held = list(held)
        rows = pl.ds(pl.multiple_of(first + index * 8, 8), 8)
        drives = [drive_ref[rows, lanes] for lanes in chunks]
        outs = [[] for _ in chunks]
        for j in range(8):
            token = first + index * 8 + j
            b, c = b_ref[token], c_ref[token]
            for k, lanes in enumerate(chunks):
                held[k] = decay_ref[token, :, lanes] * held[k] + drives[k][j : j + 1] * b
                state_ref[token, :, lanes] = held[k].astype(BF16)
                outs[k].append(jnp.sum(c * held[k], axis=0, keepdims=True))
        for k, lanes in enumerate(chunks):
            out_ref[pl.ds(pl.multiple_of(index * 8, 8), 8), lanes] = jnp.concatenate(outs[k], axis=0)
        return tuple(held)

    lax.fori_loop(0, tokens // 8, block, tuple(enter_ref[which, :, lanes] for lanes in chunks))


def run_adjoints(
    decay_ref, step_ref, up_ref, b_ref, c_ref, rate_ref, enter_ref, state_ref, adjoint_ref,
    first_sum_ref, second_sum_ref, which, first, tokens, span, carried,
):
    chunks = lane_chunks(rate_ref.shape[1])

    def block(index, carried):
        held, total = list(carried[0]), list(carried[1])
        ones = [[None] * 8 for _ in chunks]
        twos = [[None] * 8 for _ in chunks]
        start = first + (tokens // 8 - 1 - index) * 8
        rows = pl.ds(pl.multiple_of(start, 8), 8)
        ups = [up_ref[rows, lanes] for lanes in chunks]
        steps = [step_ref[rows, lanes] for lanes in chunks]
        for j in range(7, -1, -1):
            token = start + j
            b, c = b_ref[token], c_ref[token]
            for k, lanes in enumerate(chunks):
                adjoint = c * ups[k][j : j + 1] + held[k]
                adjoint_ref[token - first, :, lanes] = adjoint.astype(BF16)
                held[k] = decay_ref[token, :, lanes] * adjoint
                if j > 0:
                    before = state_ref[token - 1, :, lanes].astype(F32)
                else:
                    before = state_ref[jnp.maximum(token - 1, first), :, lanes].astype(F32)
                    before = jnp.where(token == first, enter_ref[which, :, lanes], before)
                pulled = held[k] * before
                ones[k][j] = jnp.sum(pulled * rate_ref[:, lanes], axis=0, keepdims=True)
                twos[k][j] = jnp.sum(adjoint * b, axis=0, keepdims=True)
                total[k] = total[k] + pulled * steps[k][j : j + 1]
        own_rows = pl.ds(pl.multiple_of(start - first, 8), 8)
        for k, lanes in enumerate(chunks):
            first_sum_ref[own_rows, lanes] = jnp.concatenate(ones[k], axis=0)
            second_sum_ref[own_rows, lanes] = jnp.concatenate(twos[k], axis=0)
        return tuple(held), tuple(total)

    return lax.fori_loop(span[0], span[1], block, carried)


def map_sums(values_ref, rows, states, first, tokens):
    width = rows.shape[1]
    flat = values_ref[first : first + tokens].reshape(tokens * states, width)
    all_pairs = dot(flat, rows.astype(BF16), ((1,), (1,)))
    row_token = lax.broadcasted_iota(jnp.int32, (tokens * states, tokens), 0) // states
    column_token = lax.broadcasted_iota(jnp.int32, (tokens * states, tokens), 1)
    kept = jnp.where(row_token == column_token, all_pairs, 0.0).astype(BF16)
    state = lax.broadcasted_iota(jnp.int32, (states, tokens * states), 0)
    row_state = lax.broadcasted_iota(jnp.int32, (states, tokens * states), 1) % states
    return dot((state == row_state).astype(BF16), kept)


def send(src, dst, send_sem, recv_sem, device):
    copy = pltpu.make_async_remote_copy(
        src_ref=src, dst_ref=dst, send_sem=send_sem, recv_sem=recv_sem,
        device_id=device, device_id_type=MESH,
    )
    copy.start()
    return copy


class ChanGather:
    def __init__(self, src, place, sems, mine, core_peer, x_peer):
        self.place, self.sems, self.mine, self.core_peer = (place, sems, mine, core_peer)
        self.over_x = send(src, place(mine), sems.at[0], sems.at[1], x_peer)
        self.over_core = send(src, place(mine), sems.at[2], sems.at[3], core_peer)

    def relay(self):
        self.over_x.wait_recv()
        block = self.place(flip(self.mine, 2))
        self.onward = send(block, block, self.sems.at[4], self.sems.at[5], self.core_peer)

    def finish(self):
        self.over_core.wait_recv()
        self.onward.wait_recv()
        for copy in (self.over_x, self.over_core, self.onward):
            copy.wait_send()


def ring_position(index, count):
    return lax.div(index, 2) + lax.rem(index, 2) * (count - 1 - 2 * lax.div(index, 2))


def ring_device(position, count):
    position = lax.rem(position + 2 * count, count)
    back = lax.div(position, count // 2)
    return 2 * position + back * (2 * (count - 1 - position) + 1 - 2 * position)


class RingGather:
    def __init__(self, place, sems, count, mine, chan, more_left):
        self.place, self.sems, self.count, self.chan = (place, sems, count, chan)
        self.position = ring_position(mine, count)
        most = count // 2
        self.steps = (most, count - 1 - most) if more_left else (count - 1 - most, most)
        self.length = most
        self.copies = []
        self.step = 0
        self.launch()

    def source(self, side, step):
        return ring_device(self.position + (step if side else -step), self.count)

    def launch(self):
        for side in range(2):
            if self.step < self.steps[side]:
                block = self.place(self.source(side, self.step))
                towards = ring_device(self.position + (-1 if side else 1), self.count)
                sems = self.sems.at[side, self.step]
                self.copies.append(send(block, block, sems.at[0], sems.at[1], (towards, self.chan)))

    def advance(self):
        if self.step == self.length:
            return []
        arrived = []
        for side in range(2):
            if self.step < self.steps[side]:
                source = self.source(side, self.step + 1)
                block = self.place(source)
                sems = self.sems.at[side, self.step]
                pltpu.make_async_remote_copy(
                    src_ref=block, dst_ref=block, send_sem=sems.at[0], recv_sem=sems.at[1],
                    device_id=(source, self.chan), device_id_type=MESH,
                ).wait_recv()
                arrived.append(source)
        self.step += 1
        self.launch()
        return arrived

    def finish(self):
        while self.step < self.length:
            self.advance()
        for copy in self.copies:
            copy.wait_send()


class GridGather:
    def __init__(self, place, ring_sems, chan_sems, count, me_s, me_c, core_peer, x_peer):
        self.place, self.mine, self.sems = (place, me_c, chan_sems)
        self.peers = (core_peer, x_peer)
        self.ring = RingGather(lambda d: place(me_c, d), ring_sems, count, me_s, me_c, True)
        self.gathers = []
        self.relayed = 0

    def advance(self):
        for source in self.ring.advance():
            self.gathers.append(
                ChanGather(
                    self.place(self.mine, source), partial(self.at, source), self.sems.at[len(self.gathers)],
                    self.mine, *self.peers,
                )
            )

    def at(self, source, chan):
        return self.place(chan, source)

    def relay(self, upto):
        while self.relayed < min(upto, len(self.gathers)):
            self.gathers[self.relayed].relay()
            self.relayed += 1

    def finish(self):
        self.ring.finish()
        for gather in self.gathers:
            gather.finish()


class ChanSum:
    def __init__(self, own, first, second, middle, sems, core_peer, x_peer):
        self.own, self.first, self.second, self.middle = (own, first, second, middle)
        self.sems, self.x_peer = (sems, x_peer)
        self.copies = [send(own, first, sems.at[0], sems.at[1], core_peer)]

    def cross(self):
        self.copies[0].wait_recv()
        self.middle[...] = self.own[...] + self.first[...]
        self.copies.append(send(self.middle, self.second, self.sems.at[2], self.sems.at[3], self.x_peer))

    def finish(self):
        self.copies[1].wait_recv()
        for copy in self.copies:
            copy.wait_send()
        return self.middle[...] + self.second[...]


class ChanScatter:
    def __init__(self, blocks, first, second, sems, mine, core_peer, x_peer, extra=None):
        self.blocks, self.first, self.second, self.sems = (blocks, first, second, sems)
        self.mine, self.x_peer, self.extra = (mine, x_peer, extra)
        other = flip(mine, 1)
        self.copies = [
            send(blocks.at[other], first.at[0], sems.at[0], sems.at[1], core_peer),
            send(blocks.at[flip(other, 2)], first.at[1], sems.at[2], sems.at[3], core_peer),
        ]
        if extra is not None:
            self.copies.append(send(extra[0], extra[1], sems.at[6], sems.at[7], core_peer))

    def cross(self):
        for copy in self.copies:
            copy.wait_recv()
        far = flip(self.mine, 2)
        self.blocks[far] = (self.blocks[far].astype(F32) + self.first[1].astype(F32)).astype(BF16)
        self.last = [send(self.blocks.at[far], self.second, self.sems.at[4], self.sems.at[5], self.x_peer)]
        if self.extra is not None:
            own, near, middle, across = self.extra
            middle[...] = own[...] + near[...]
            self.last.append(send(middle, across, self.sems.at[8], self.sems.at[9], self.x_peer))

    def finish(self):
        for copy in self.last:
            copy.wait_recv()
        for copy in self.copies + self.last:
            copy.wait_send()
        total = self.blocks[self.mine].astype(F32) + self.first[0].astype(F32) + self.second[...].astype(F32)
        if self.extra is None:
            return total
        return total, self.extra[2][...] + self.extra[3][...]


class SeqSum:
    def __init__(self, held, landing, full, sems, bits, mine, chan):
        self.held, self.landing, self.full, self.sems, self.bits = (held, landing, full, sems, bits)
        self.mine, self.chan = (mine, chan)
        self.regions = []
        self.copies = []
        start, size, place = (0, held.shape[0], 0)
        for bit in bits:
            half = size // 2
            mine_bit = lax.rem(lax.div(mine, bit), 2)
            keep = pl.multiple_of(start + mine_bit * half, 16)
            give = pl.multiple_of(start + (1 - mine_bit) * half, 16)
            self.regions.append((keep, give, half, place))
            start, size, place = (keep, half, place + half)
        self.step = 0
        self.total = 2 * len(bits)
        self.launch()

    def launch(self):
        step, count = (self.step, len(self.bits))
        sems = (self.sems.at[2 * step], self.sems.at[2 * step + 1])
        if step < count:
            _, give, half, place = self.regions[step]
            src, dst = (self.held.at[pl.ds(give, half)], self.landing.at[pl.ds(place, half)])
            bit = self.bits[step]
        else:
            keep, _, half, _ = self.regions[self.total - 1 - step]
            src = dst = self.full.at[pl.ds(keep, half)]
            bit = self.bits[self.total - 1 - step]
        self.copies.append(send(src, dst, *sems, (flip(self.mine, bit), self.chan)))

    def advance(self):
        if self.step == self.total:
            return
        self.copies[-1].wait_recv()
        if self.step < len(self.bits):
            keep, _, half, place = self.regions[self.step]
            rows = pl.ds(keep, half)
            got = self.landing[pl.ds(place, half)].astype(F32)
            into = self.held if self.step < len(self.bits) - 1 else self.full
            into[rows] = (self.held[rows].astype(F32) + got).astype(BF16)
        self.step += 1
        if self.step < self.total:
            self.launch()

    def finish(self):
        while self.step < self.total:
            self.advance()
        for copy in self.copies:
            copy.wait_send()


class DirectSum:
    def __init__(self, own, landing, full, sems, count, mine, chan):
        self.own, self.landing, self.full, self.sems = (own, landing, full, sems)
        self.count, self.mine, self.chan = (count, mine, chan)
        self.rows = own.shape[0] // count
        self.each(lambda k, peer: self.apart(peer, self.mine, peer).start())

    def piece(self, ref, device):
        return ref.at[pl.ds(pl.multiple_of(device * self.rows, self.rows), self.rows)]

    def each(self, act):
        def turn(k, _):
            act(k, lax.rem(self.mine + k, self.count))
            return 0

        lax.fori_loop(1, self.count, turn, 0)

    def apart(self, piece, source, peer):
        return pltpu.make_async_remote_copy(
            src_ref=self.piece(self.own, piece), dst_ref=self.landing.at[source],
            send_sem=self.sems.at[0, peer], recv_sem=self.sems.at[1, source],
            device_id=(peer, self.chan), device_id_type=MESH,
        )

    def back(self, source, peer):
        return pltpu.make_async_remote_copy(
            src_ref=self.piece(self.full, source), dst_ref=self.piece(self.full, source),
            send_sem=self.sems.at[2, peer], recv_sem=self.sems.at[3, source],
            device_id=(peer, self.chan), device_id_type=MESH,
        )

    def cross(self):
        self.each(lambda k, peer: self.apart(peer, peer, peer).wait_recv())
        mine = pl.ds(pl.multiple_of(self.mine * self.rows, self.rows), self.rows)

        def add(k, total):
            return total + self.landing[lax.rem(self.mine + k, self.count)].astype(F32)

        total = lax.fori_loop(1, self.count, add, self.own[mine].astype(F32))
        self.full[mine] = total.astype(BF16)
        self.each(lambda k, peer: self.back(self.mine, peer).start())

    def finish(self):
        self.each(lambda k, peer: self.back(peer, peer).wait_recv())
        self.each(lambda k, peer: self.apart(peer, self.mine, peer).wait_send())
        self.each(lambda k, peer: self.back(self.mine, peer).wait_send())


def layer_kernel(names, seq_devices, *refs):
    r = SimpleNamespace(**dict(zip(names, refs)))
    x_ref, og_ref, win_ref, wout_ref = (r.inputs, r.out_grad, r.w_in_here, r.w_out_here)
    xw_ref, dtw_ref = (r.x_weight, r.dt_weight)
    seqs, tokens, shard = x_ref.shape
    model, width = win_ref.shape[1:]
    states = r.log_decay.shape[0]
    low_rank = dtw_ref.shape[0]
    taps = r.conv_weight.shape[0]
    proj = xw_ref.shape[0]
    me_s, me_c = (lax.axis_index("seq"), lax.axis_index("chan"))
    core_peer, x_peer = ((me_s, flip(me_c, 1)), (me_s, flip(me_c, 2)))
    right, left = (lax.rem(me_s + 1, seq_devices), lax.rem(me_s + seq_devices - 1, seq_devices))
    position = ring_position(me_s, seq_devices)
    gathered = seq_devices <= MOST_GATHERED
    spot = me_s if gathered else 0

    loads = []
    for k, (src, dst) in enumerate(((r.w_in, r.w_in_here), (r.w_out, r.w_out_here))):
        loads.append(pltpu.make_async_copy(src, dst, r.load_sems.at[k]))
        loads[k].start()

    barrier = pltpu.get_barrier_semaphore()

    def greet(semaphore, device):
        pl.semaphore_signal(semaphore, inc=1, device_id=device, device_id_type=MESH)

    ring = [(ring_device(position + step, seq_devices), me_c) for step in (1, -1)]
    first_peers = [core_peer, x_peer, (right, me_c), (left, me_c)] + ring
    for device in first_peers:
        greet(barrier, device)
    pl.semaphore_wait(barrier, len(first_peers))

    xo_ref, halo_ref = (r.xo, r.halo)
    gather_x = ChanGather(x_ref, lambda q: xo_ref.at[q, spot, 0], r.x_sems, me_c, core_peer, x_peer)
    halo_copy = send(
        x_ref.at[:, pl.ds(tokens - HALO, HALO), :], halo_ref.at[me_c, pl.ds(0, seqs)],
        r.halo_sems.at[6], r.halo_sems.at[7], (right, me_c),
    )
    for device in ring:
        greet(r.known.at[0], device)
    gather_og = ChanGather(og_ref, lambda q: xo_ref.at[q, spot, 1], r.og_sems, me_c, core_peer, x_peer)
    xo_ref[me_c, spot, 0] = x_ref[...]
    xo_ref[me_c, spot, 1] = og_ref[...]
    halo_ref[me_c, seqs] = jnp.broadcast_to(r.norm_gain[...].astype(F32).reshape(1, shard), (HALO, shard)).astype(BF16)
    if gathered:
        gather_all = GridGather(
            lambda q, d: xo_ref.at[q, d], r.xo_ring_sems, r.xo_chan_sems, seq_devices, me_s, me_c, core_peer, x_peer
        )
    halo_copy.wait_recv()
    gather_halo = ChanGather(
        halo_ref.at[me_c], lambda q: halo_ref.at[q], r.halo_sems, me_c, core_peer, x_peer
    )
    gather_x.relay()
    gather_halo.relay()
    gather_x.finish()
    gather_halo.finish()
    halo_copy.wait_send()
    gather_og.relay()

    reaches = [1]
    while 2 * reaches[-1] < seq_devices // 2:
        reaches.append(2 * reaches[-1])

    def hear(k):
        pl.semaphore_wait(r.known.at[k], 2)
        if k + 1 < len(reaches):
            for step in (reaches[k + 1], -reaches[k + 1]):
                greet(r.known.at[k + 1], (ring_device(position + step, seq_devices), me_c))

    hear(0)

    rate_ref, rate2_ref = (r.rate, r.rate2)
    rate_ref[...] = -jnp.exp(r.log_decay[...])
    rate2_ref[...] = rate_ref[...] * LOG2E

    def mask_of(s, rows, begin):
        positions = me_s * tokens + begin + lax.broadcasted_iota(jnp.int32, (rows, 1), 0)
        return (positions < r.lengths[s]).astype(F32)

    def gain_of(q):
        return halo_ref[q, seqs, 0:1, :].astype(F32)

    def normalize(blocks):
        squares = sum(jnp.sum(b * b, axis=1, keepdims=True) for b in blocks)
        root = lax.rsqrt(squares * (1.0 / model) + EPSILON)
        return root, [(b * root * gain_of(q)).astype(BF16) for q, b in enumerate(blocks)]

    loads[0].wait()

    conv_sum = []
    normed_rows = []
    has_left = (me_s > 0).astype(F32)
    for s in range(seqs):
        mine = pl.ds(s * tokens, tokens)
        root, rows = normalize([xo_ref[q, spot, 0, s].astype(F32) for q in range(4)])
        _, before = normalize([halo_ref[q, s].astype(F32) for q in range(4)])
        r.root[mine, :] = jnp.broadcast_to(root, (tokens, LANES))
        normed, normed_before = (jnp.concatenate(rows, axis=1), jnp.concatenate(before, axis=1))
        normed_rows.append(pl.ds(pl.multiple_of(spot * seqs * tokens + s * tokens, tokens), tokens))
        r.normed[normed_rows[s], :] = normed
        inner = dot(normed, win_ref[0]).astype(BF16).astype(F32) * mask_of(s, tokens, 0)
        inner_before = dot(normed_before, win_ref[0]).astype(BF16).astype(F32)
        inner_before = inner_before * (mask_of(s, HALO, -HALO) * has_left)
        r.inner[s, HALO:, :] = inner
        r.inner[s, :HALO, :] = inner_before
        conv_pre = r.conv_bias[...] + sum(
            r.conv_weight[k : k + 1, :] * r.inner[s, HALO - taps + 1 + k : HALO - taps + 1 + k + tokens, :]
            for k in range(taps)
        )
        r.conv_pre[mine, :] = conv_pre
        act = (conv_pre * jax.nn.sigmoid(conv_pre)).astype(BF16)
        r.act[mine, :] = act.astype(F32)
        r.proj_own[s] = dot(xw_ref[...], act, ((1,), (1,)))
        conv_sum.append(
            ChanSum(
                r.proj_own.at[s], r.proj_first.at[s], r.proj_second.at[s], r.proj_mid.at[s],
                r.proj_sems.at[s], core_peer, x_peer,
            )
        )
    for s in range(seqs):
        conv_sum[s].cross()
    for s in range(seqs):
        mine = pl.ds(s * tokens, tokens)
        r.gate_pre[mine, :] = dot(r.normed[normed_rows[s], :], win_ref[1])
    gather_og.finish()
    loads[1].wait()
    for s in range(seqs):
        mine = pl.ds(s * tokens, tokens)
        cot = jnp.concatenate([xo_ref[q, spot, 1, s] for q in range(4)], axis=1)
        grad_mixed = dot(cot, wout_ref[...], ((1,), (1,))) * mask_of(s, tokens, 0)
        gate = r.gate_pre[mine, :]
        sigmoid = jax.nn.sigmoid(gate)
        r.grad_mixed[mine, :] = grad_mixed
        r.up[mine, :] = grad_mixed * (gate * sigmoid)
        if gathered:
            rows = normed_rows[s]
            r.gate_act_all[rows, :] = (gate * sigmoid * mask_of(s, tokens, 0)).astype(BF16)
            r.gate_slope_all[rows, :] = (grad_mixed * silu_slope(gate, sigmoid)).astype(BF16)
        else:
            r.cot[mine, :] = (cot.astype(F32) * mask_of(s, tokens, 0)).astype(BF16)
    if gathered:
        gather_all.advance()

    totals_ref = r.totals
    step_totals = []
    for s in range(seqs):
        mine = pl.ds(s * tokens, tokens)
        projected = conv_sum[s].finish()
        low = projected[:low_rank].astype(BF16)
        r.low[:, s * tokens : (s + 1) * tokens] = low
        step_pre = dot(projected[:low_rank].T.astype(BF16), dtw_ref[...]) + r.dt_bias[...]
        r.step_pre[mine, :] = step_pre
        step = softplus(step_pre)
        r.step[mine, :] = step
        r.drive[mine, :] = step * r.act[mine, :]
        step_totals.append(jnp.sum(step, axis=0, keepdims=True))
        spread_maps(projected[low_rank:], r.b, r.c, s * tokens, tokens)
    totals_ref[me_s] = jnp.concatenate(step_totals + [jnp.zeros((8 - seqs, width), F32)], axis=0)

    def seq_device(k):
        return (k, me_c)

    def totals_copy(k):
        peer = lax.rem(me_s + k, seq_devices)
        return pltpu.make_async_remote_copy(
            src_ref=totals_ref.at[me_s], dst_ref=totals_ref.at[me_s],
            send_sem=r.totals_send.at[k], recv_sem=r.totals_recv.at[me_s],
            device_id=seq_device(peer), device_id_type=MESH,
        )

    def start_totals(k, _):
        totals_copy(k).start()
        return 0

    for k in range(1, len(reaches)):
        hear(k)
    lax.fori_loop(1, seq_devices, start_totals, 0)

    ends_refs = (r.ends, r.ends_send, r.ends_recv)
    leaves_refs = (r.leaves, r.leaves_send, r.leaves_recv)

    def carried_copy(which, s, peer):
        ref, send_sem, recv_sem = which
        return pltpu.make_async_remote_copy(
            src_ref=ref.at[s, me_s], dst_ref=ref.at[s, me_s],
            send_sem=send_sem.at[s, peer], recv_sem=recv_sem.at[s, me_s],
            device_id=seq_device(peer), device_id_type=MESH,
        )

    def start_carried(which, s, begin, end):
        def start(peer, _):
            carried_copy(which, s, peer).start()
            return 0

        lax.fori_loop(begin, end, start, 0)

    def wait_carried(which, s, begin, end):
        def wait(peer, _):
            carried_copy(which, s, peer).wait_send()
            return 0

        lax.fori_loop(begin, end, wait, 0)

    for s in range(seqs):
        ends = local_states(r.decay, r.step, r.drive, r.b, rate2_ref, s * tokens, tokens)
        for k, lanes in enumerate(lane_chunks(width)):
            r.ends[s, me_s, :, lanes] = ends[k].astype(BF16)
        start_carried(ends_refs, s, me_s + 1, seq_devices)
    if gathered:
        gather_all.advance()
        gather_all.relay(2)
    for s in range(seqs):
        leaves = local_adjoints(r.decay, r.up, r.c, rate_ref, s * tokens, tokens)
        for k, lanes in enumerate(lane_chunks(width)):
            r.leaves[s, me_s, :, lanes] = leaves[k].astype(BF16)
        start_carried(leaves_refs, s, 0, me_s)

    def wait_totals(k, _):
        peer = lax.rem(me_s + k, seq_devices)
        pltpu.make_async_remote_copy(
            src_ref=totals_ref.at[peer], dst_ref=totals_ref.at[peer],
            send_sem=r.totals_send.at[k], recv_sem=r.totals_recv.at[peer],
            device_id=seq_device(peer), device_id_type=MESH,
        ).wait_recv()
        return 0

    lax.fori_loop(1, seq_devices, wait_totals, 0)

    def combine(which, s, count, place):
        ref, send_sem, recv_sem = which

        def turn(k, held):
            peer = place(k)
            pltpu.make_async_remote_copy(
                src_ref=ref.at[s, peer], dst_ref=ref.at[s, peer],
                send_sem=send_sem.at[s, peer], recv_sem=recv_sem.at[s, peer],
                device_id=seq_device(peer), device_id_type=MESH,
            ).wait_recv()
            total = totals_ref[peer][s : s + 1]
            return jnp.exp2(total * rate2_ref[...]) * held + ref[s, peer].astype(F32)

        return lax.fori_loop(0, count, turn, jnp.zeros((states, width), F32))

    skip_gathers, inner_gathers = ([], [])

    def block_of(ref, s, device):
        return ref.at[device, s]

    def foreign(k, _):
        device = lax.rem(me_s + k, seq_devices)
        rows = pl.ds(pl.multiple_of(device * (seqs * tokens), seqs * tokens), seqs * tokens)
        blocks = [xo_ref[q, device, 0].reshape(seqs * tokens, shard).astype(F32) for q in range(4)]
        normed = jnp.concatenate(normalize(blocks)[1], axis=1)
        r.normed[rows, :] = normed
        gate = dot(normed, win_ref[1])
        sigmoid = jax.nn.sigmoid(gate)
        cot = jnp.concatenate([xo_ref[q, device, 1].reshape(seqs * tokens, shard) for q in range(4)], axis=1)
        mask = jnp.concatenate([mask_of(s, tokens, (device - me_s) * tokens) for s in range(seqs)], axis=0)
        grad_mixed = dot(cot, wout_ref[...], ((1,), (1,))) * mask
        r.gate_act_all[rows, :] = (gate * sigmoid * mask).astype(BF16)
        r.gate_slope_all[rows, :] = (grad_mixed * silu_slope(gate, sigmoid)).astype(BF16)
        return 0

    for s in range(seqs):
        mine = pl.ds(s * tokens, tokens)
        r.entering[s] = combine(ends_refs, s, me_s, lambda k: k)
        run_states(
            r.decay, r.drive, r.b, r.c, r.entering, r.state, r.scanned, s, s * tokens, tokens
        )
        gate = r.gate_pre[mine, :]
        sigmoid = jax.nn.sigmoid(gate)
        with_skip = r.scanned[...] + r.skip_gain[...] * r.act[mine, :]
        mixed = (with_skip * (gate * sigmoid)).astype(BF16)
        r.mixed[mine, :] = mixed
        r.grad_gate[mine, :] = (r.grad_mixed[mine, :] * with_skip * silu_slope(gate, sigmoid)).astype(BF16)
        if gathered:
            r.skip_all[me_s, s] = with_skip.astype(BF16)
            skip_gathers.append(
                RingGather(
                    partial(block_of, r.skip_all, s), r.skip_sems.at[s], seq_devices, me_s, me_c, s == 0
                )
            )
            if s == 0:
                gather_all.advance()
                gather_all.relay(2)
    out_part = dot(r.mixed[...], wout_ref[...])
    for q in range(4):
        r.out_blocks[q] = out_part[:, q * shard : (q + 1) * shard].astype(BF16)
    scatter_out = ChanScatter(
        r.out_blocks, r.out_first, r.out_second, r.out_sems, me_c, core_peer, x_peer
    )
    sums = []
    bits = [1 << k for k in range(seq_devices.bit_length() - 1)]
    turned = bits[1:] + bits[:1]
    if gathered:
        skip_gathers[0].advance()
    else:
        r.grad_w_out[...] = dot(r.mixed[...], r.cot[...], ((0,), (0,))).astype(BF16)
        sums.append(SeqSum(r.grad_w_out, r.land_w_out, r.out_w_out, r.w_out_sems, bits, me_s, me_c))
        r.grad_w_gate[...] = dot(r.normed[...], r.grad_gate[...], ((0,), (0,))).astype(BF16)
        sums.append(SeqSum(r.grad_w_gate, r.land_w_gate, r.out_w_in.at[1], r.w_gate_sems, turned, me_s, me_c))

    early, later = (r.early, r.later)
    early[...] = jnp.zeros_like(early)
    later[...] = jnp.zeros_like(later)
    skip_row = low_rank + states + 1
    low_sum, rim_copies, rate_sums = ([], [], [])
    has_right = (me_s < seq_devices - 1).astype(F32)

    def scan_back(s, services):
        leaving = combine(leaves_refs, s, seq_devices - 1 - me_s, lambda k: seq_devices - 1 - k)
        carried = (tuple(leaving[:, lanes] for lanes in lane_chunks(width)), zero_states(rate_ref))
        parts, blocks = (len(services), tokens // 8)
        for part, service in enumerate(services):
            carried = run_adjoints(
                r.decay, r.step, r.up, r.b, r.c, rate_ref, r.entering, r.state,
                r.adjoint, r.first_sum, r.second_sum, s, s * tokens, tokens,
                (part * blocks // parts, (part + 1) * blocks // parts), carried,
            )
            service()
        rate_sums.append(carried[1])

    def after_scan(s):
        mine = pl.ds(s * tokens, tokens)
        act, step, step_pre = (r.act[mine, :], r.step[mine, :], r.step_pre[mine, :])
        second = r.second_sum[...]
        grad_step_pre = (r.first_sum[...] + act * second) * jax.nn.sigmoid(step_pre)
        grad_step_low = grad_step_pre.astype(BF16)
        own = r.proj_own.at[s]
        own[:low_rank, :] = dot(dtw_ref[...], grad_step_low, ((1,), (1,)))
        own[low_rank : low_rank + states, :] = map_sums(r.adjoint, r.drive[mine, :], states, 0, tokens)
        own[low_rank + states :, :] = map_sums(r.state, r.up[mine, :], states, s * tokens, tokens)
        low_sum.append(
            ChanSum(
                own, r.back_first.at[s], r.back_second.at[s], r.back_mid.at[s],
                r.back_sems.at[s], core_peer, x_peer,
            )
        )
        r.grad_step_low[mine, :] = grad_step_low
        early[skip_row - 1, :] += jnp.sum(grad_step_pre, axis=0)
        early[skip_row, :] += jnp.sum(r.up[mine, :] * act, axis=0)
        r.grad_act[mine, :] = step * second + r.up[mine, :] * r.skip_gain[...]

    def through_conv(s):
        mine = pl.ds(s * tokens, tokens)
        grad_projected = low_sum[s].finish()
        r.grad_proj[:, s * tokens : (s + 1) * tokens] = grad_projected.astype(BF16)
        grad_act = r.grad_act[mine, :] + dot(grad_projected.T.astype(BF16), xw_ref[...])
        conv_pre = r.conv_pre[mine, :]
        grad_conv = (grad_act * silu_slope(conv_pre, jax.nn.sigmoid(conv_pre))).astype(BF16)
        r.rim_own[s] = grad_conv[:HALO]
        rim_copies.append(
            send(r.rim_own.at[s], r.rim.at[s], r.rim_sems.at[2 * s], r.rim_sems.at[2 * s + 1], (left, me_c))
        )
        grad_conv = grad_conv.astype(F32)
        r.grad_conv[s, :tokens, :] = grad_conv
        later[proj + taps, :] += jnp.sum(grad_conv, axis=0)
        for k in range(taps):
            shifted = r.inner[s, HALO - taps + 1 + k : HALO - taps + 1 + k + tokens, :]
            later[proj + k, :] += jnp.sum(grad_conv * shifted, axis=0)

    def inner_of(s):
        mine = pl.ds(s * tokens, tokens)
        rim_copies[s].wait_recv()
        rim_copies[s].wait_send()
        r.grad_conv[s, tokens:, :] = r.rim[s].astype(F32) * has_right
        grad_inner = sum(
            r.conv_weight[k : k + 1, :] * r.grad_conv[s, taps - 1 - k : taps - 1 - k + tokens, :]
            for k in range(taps)
        )
        grad_inner = (grad_inner * mask_of(s, tokens, 0)).astype(BF16)
        r.grad_inner[mine, :] = grad_inner
        if gathered:
            r.inner_all[me_s, s] = grad_inner
            inner_gathers.append(
                RingGather(
                    partial(block_of, r.inner_all, s), r.inner_sems.at[s], seq_devices, me_s, me_c, s == 0
                )
            )

    def all_advance():
        for item in sums:
            item.advance()

    def skip_advance(s):
        if gathered:
            skip_gathers[s].advance()
        else:
            all_advance()

    def inner_advance(s):
        if gathered:
            inner_gathers[s].advance()
        else:
            all_advance()

    def nothing():
        pass

    scan_back(0, (nothing, scatter_out.cross, nothing, partial(skip_advance, 1)))
    after_scan(0)
    skip_advance(0)
    if gathered:
        gather_all.advance()
        gather_all.relay(4)
    scan_back(1, (low_sum[0].cross, partial(skip_advance, 1), partial(through_conv, 0), nothing))
    after_scan(1)
    skip_advance(0)
    inner_of(0)
    for k, lanes in enumerate(lane_chunks(width)):
        early[low_rank : low_rank + states, lanes] = (rate_sums[0][k] + rate_sums[1][k]) * rate_ref[:, lanes]
    early[:low_rank, :] = dot(r.low[...], r.grad_step_low[...])
    low_sum[1].cross()
    if gathered:
        r.early_own[...] = early[...].astype(BF16)
        sum_early = DirectSum(
            r.early_own, r.early_land, r.out_early, r.early_sems, seq_devices, me_s, me_c
        )
        gather_all.relay(7)
        gather_all.finish()
        lax.fori_loop(1, 3, foreign, 0)
    skip_advance(1)
    out_sum = scatter_out.finish()
    for s in range(seqs):
        r.mixed_out[s] = (x_ref[s].astype(F32) + out_sum[s * tokens : (s + 1) * tokens]).astype(BF16)
    through_conv(1)
    later[:proj, :] = dot(r.grad_proj[...], r.act[...].astype(BF16))
    if gathered:
        r.later_own[...] = later[...].astype(BF16)
        sum_later = DirectSum(
            r.later_own, r.later_land, r.out_later, r.later_sems, seq_devices, me_s, me_c
        )
    inner_of(1)
    skip_advance(0)
    inner_advance(0)

    if not gathered:
        late = r.grad_w_inner
        late[:model, :] = dot(r.normed[...], r.grad_inner[...], ((0,), (0,))).astype(BF16)
        late[model : model + early.shape[0], :] = early[...].astype(BF16)
        late[model + early.shape[0] :, :] = later[...].astype(BF16)
        sums.append(SeqSum(late, r.land_w_inner, r.full_w_inner, r.w_inner_sems, bits, me_s, me_c))
    moment = None
    for q in range(4):
        part = dot(r.grad_inner[...], win_ref[0, q * shard : (q + 1) * shard, :], ((1,), (1,)))
        part = part + dot(r.grad_gate[...], win_ref[1, q * shard : (q + 1) * shard, :], ((1,), (1,)))
        values = xo_ref[q, spot, 0].reshape(seqs * tokens, shard).astype(F32)
        term = jnp.sum(part * gain_of(q) * values, axis=1, keepdims=True)
        moment = term if moment is None else moment + term
        r.gn_blocks[q] = part.astype(BF16)
    r.moment[...] = jnp.broadcast_to(moment, (seqs * tokens, LANES)).T[:8]
    scatter_gn = ChanScatter(
        r.gn_blocks, r.gn_first, r.gn_second, r.gn_sems, me_c, core_peer, x_peer,
        (r.moment, r.moment_first, r.moment_mid, r.moment_second),
    )
    skip_advance(1)
    if gathered:
        sum_early.cross()
    scatter_gn.cross()
    inner_advance(1)
    if gathered:
        lax.fori_loop(3, 5, foreign, 0)
    inner_advance(0)
    grad_normed, moment_row = scatter_gn.finish()
    moment = jnp.broadcast_to(moment_row[:1], (LANES, seqs * tokens)).T[:, :1]
    root = r.root[:, :1]
    values = x_ref[...].reshape(seqs * tokens, shard).astype(F32)
    gains = gain_of(me_c)
    back = root * (grad_normed * gains) - values * (root * root * root) * moment * (1.0 / model)
    for s in range(seqs):
        mine = slice(s * tokens, (s + 1) * tokens)
        cot = og_ref[s].astype(F32) * mask_of(s, tokens, 0)
        r.grad_inputs[s] = (cot + back[mine]).astype(BF16)
    gain_sums_ref = r.gain_sums
    gain_sums_ref[me_s] = jnp.broadcast_to(jnp.sum(grad_normed * values * root, axis=0, keepdims=True), (8, shard))

    def gain_copy(k):
        peer = lax.rem(me_s + k, seq_devices)
        return pltpu.make_async_remote_copy(
            src_ref=gain_sums_ref.at[me_s], dst_ref=gain_sums_ref.at[me_s],
            send_sem=r.gain_sums_send.at[k], recv_sem=r.gain_sums_recv.at[me_s],
            device_id=seq_device(peer), device_id_type=MESH,
        )

    def start_gain(k, _):
        gain_copy(k).start()
        return 0

    lax.fori_loop(1, seq_devices, start_gain, 0)
    if gathered:
        inner_advance(1)
        sum_later.cross()
        lax.fori_loop(5, seq_devices, foreign, 0)
        for gather in skip_gathers:
            gather.finish()
        inner_advance(0)
        count = seq_devices * seqs * tokens

        def mix(device, _):
            rows = pl.ds(pl.multiple_of(device * (seqs * tokens), seqs * tokens), seqs * tokens)
            with_skip = r.skip_all[device].reshape(seqs * tokens, width).astype(F32)
            r.gate_act_all[rows, :] = (r.gate_act_all[rows, :].astype(F32) * with_skip).astype(BF16)
            r.gate_slope_all[rows, :] = (r.gate_slope_all[rows, :].astype(F32) * with_skip).astype(BF16)
            return 0

        lax.fori_loop(0, seq_devices, mix, 0)
        results = []

        def deliver(src, dst):
            copy = pltpu.make_async_copy(src, dst, r.result_sems.at[len(results)])
            copy.start()
            results.append(copy)

        staged = r.skip_all.reshape(count, width)
        for q in range(4):
            outs = xo_ref[q, :, 1].reshape(count, shard)
            half, place = (q * shard // width, q * shard % width)
            rows = pl.ds(half * width, width)
            staged[rows, place : place + shard] = dot(r.gate_act_all[...], outs, ((0,), (0,))).astype(BF16)
            if place + shard == width:
                deliver(staged.at[rows], r.out_w_out.at[:, pl.ds(half * width, width)])
            if q % 2 == 1:
                inner_advance(1 - q // 2)
        for q in range(4):
            rows = slice(q * shard, (q + 1) * shard)
            r.gate_act_all[rows, :] = dot(r.normed[:, rows], r.gate_slope_all[...], ((0,), (0,))).astype(BF16)
        deliver(r.gate_act_all.at[pl.ds(0, model)], r.out_w_in.at[1])
        for gather in inner_gathers:
            gather.finish()
        inner_rows = r.inner_all[...].reshape(count, width)
        for q in range(4):
            rows = slice(model + q * shard, model + (q + 1) * shard)
            cols = slice(q * shard, (q + 1) * shard)
            r.gate_act_all[rows, :] = dot(r.normed[:, cols], inner_rows, ((0,), (0,))).astype(BF16)
            if q % 2 == 1:
                deliver(
                    r.gate_act_all.at[pl.ds(model + (q - 1) * shard, 2 * shard)],
                    r.out_w_in.at[0, pl.ds((q - 1) * shard, 2 * shard)],
                )
        sum_early.finish()
        sum_later.finish()
    else:
        for step in range(max(item.total for item in sums)):
            all_advance()

    def take_gain(k, _):
        peer = lax.rem(me_s + k, seq_devices)
        pltpu.make_async_remote_copy(
            src_ref=gain_sums_ref.at[peer], dst_ref=gain_sums_ref.at[peer],
            send_sem=r.gain_sums_send.at[k], recv_sem=r.gain_sums_recv.at[peer],
            device_id=seq_device(peer), device_id_type=MESH,
        ).wait_recv()
        gain_copy(k).wait_send()
        totals_copy(k).wait_send()
        return 0

    lax.fori_loop(1, seq_devices, take_gain, 0)
    r.grad_gain[...] = jnp.sum(gain_sums_ref[...], axis=0)
    for item in sums:
        item.finish()
    if gathered:
        for copy in results:
            copy.wait()
    else:
        r.out_w_in[0] = r.full_w_inner[:model, :]
        r.out_early[...] = r.full_w_inner[model : model + early.shape[0], :]
        r.out_later[...] = r.full_w_inner[model + early.shape[0] :, :]
    for s in range(seqs):
        wait_carried(ends_refs, s, me_s + 1, seq_devices)
        wait_carried(leaves_refs, s, 0, me_s)


def finish_kernel(
    rows_of, mixed_ref, inputs_ref, w_in_ref, w_out_ref, early_ref, later_ref, gain_ref,
    mixed_out, grad_inputs, gain_out, w_in_out, conv_w_out, conv_b_out, x_out, dt_w_out, dt_b_out, decay_out,
    skip_out, w_out_out,
):
    mixed_out[...] = mixed_ref[...]
    grad_inputs[...] = inputs_ref[...]
    w_in_out[...] = w_in_ref[...].astype(F32)
    w_out_out[...] = w_out_ref[...].astype(F32)

    @pl.when(pl.program_id(0) == 0)
    def _():
        proj, low_rank, states, taps = rows_of
        early, later = (early_ref[...].astype(F32), later_ref[...].astype(F32))
        skip_row = low_rank + states + 1
        gain_out[...] = gain_ref[0:1, :]
        x_out[...] = later[:proj]
        conv_w_out[...] = later[proj : proj + taps]
        conv_b_out[...] = later[proj + taps : proj + taps + 1]
        dt_w_out[...] = early[:low_rank]
        decay_out[...] = early[low_rank : low_rank + states]
        dt_b_out[...] = early[skip_row - 1 : skip_row]
        skip_out[...] = early[skip_row : skip_row + 1]


def layer(
    seq_devices,
    inputs, lengths, out_grad, norm_gain, w_in, conv_weight, conv_bias, x_weight, dt_weight,
    dt_bias, log_decay, skip_gain, w_out,
):
    seqs, tokens, shard = inputs.shape
    _, model, width = w_in.shape
    states, low_rank, taps, proj = (log_decay.shape[0], dt_weight.shape[0], conv_weight.shape[0], x_weight.shape[0])
    rows = seqs * tokens
    grain = 16 * seq_devices if seq_devices <= MOST_GATHERED else 8 * seq_devices
    early_rows = -(-(low_rank + states + 2) // grain) * grain
    later_rows = -(-(proj + taps + 1) // grain) * grain
    steps = 4 * (seq_devices.bit_length() - 1)
    gathered = seq_devices <= MOST_GATHERED
    dma = pltpu.SemaphoreType.DMA
    vmem = pltpu.VMEM
    operands = dict(
        inputs=inputs, lengths=lengths, out_grad=out_grad, norm_gain=norm_gain,
        w_in=w_in, conv_weight=conv_weight, conv_bias=conv_bias.reshape(1, width),
        x_weight=x_weight, dt_weight=dt_weight, dt_bias=dt_bias.reshape(1, width),
        log_decay=log_decay, skip_gain=skip_gain.reshape(1, width), w_out=w_out,
    )
    outputs = dict(
        mixed_out=(inputs.shape, BF16), grad_inputs=(inputs.shape, BF16), grad_gain=((8, shard), F32),
        out_w_in=(w_in.shape, BF16), out_w_out=(w_out.shape, BF16),
        out_early=((early_rows, width), BF16), out_later=((later_rows, width), BF16),
    )
    wide = (rows, width)
    scratch = dict(
        xo=vmem((4, seq_devices if gathered else 1, 2) + inputs.shape, BF16),
        halo=vmem((4, seqs + 1, HALO, shard), BF16), known=pltpu.SemaphoreType.REGULAR((8,)),
        w_in_here=vmem(w_in.shape, BF16), w_out_here=vmem(w_out.shape, BF16), load_sems=dma((2,)),
        x_sems=dma((6,)), og_sems=dma((6,)), halo_sems=dma((8,)),
        rate=vmem((states, width), F32), rate2=vmem((states, width), F32),
        root=vmem((rows, LANES), F32), normed=vmem((seq_devices * rows if gathered else rows, model), BF16),
        inner=vmem((seqs, HALO + tokens, width), F32),
        conv_pre=vmem(wide, F32), act=vmem(wide, F32), gate_pre=vmem(wide, F32),
        grad_mixed=vmem(wide, F32), up=vmem(wide, F32),
        proj_own=vmem((seqs, proj, tokens), F32), proj_first=vmem((seqs, proj, tokens), F32),
        proj_second=vmem((seqs, proj, tokens), F32), proj_mid=vmem((seqs, proj, tokens), F32),
        proj_sems=dma((seqs, 4)),
        back_first=vmem((seqs, proj, tokens), F32), back_second=vmem((seqs, proj, tokens), F32),
        back_mid=vmem((seqs, proj, tokens), F32), back_sems=dma((seqs, 4)),
        low=vmem((low_rank, rows), BF16), step_pre=vmem(wide, F32), step=vmem(wide, F32),
        drive=vmem(wide, F32), b=vmem((rows, states, LANES), F32), c=vmem((rows, states, LANES), F32),
        decay=vmem((rows, states, width), F32),
        totals=vmem((seq_devices, 8, width), F32), totals_send=dma((seq_devices,)),
        totals_recv=dma((seq_devices,)),
        ends=vmem((seqs, seq_devices, states, width), BF16), ends_send=dma((seqs, seq_devices)),
        ends_recv=dma((seqs, seq_devices)),
        leaves=vmem((seqs, seq_devices, states, width), BF16), leaves_send=dma((seqs, seq_devices)),
        leaves_recv=dma((seqs, seq_devices)),
        entering=vmem((seqs, states, width), F32),
        state=vmem((rows, states, width), BF16), adjoint=vmem((tokens, states, width), BF16),
        scanned=vmem((tokens, width), F32), first_sum=vmem((tokens, width), F32),
        second_sum=vmem((tokens, width), F32),
        mixed=vmem(wide, BF16), grad_gate=vmem(wide, BF16), grad_step_low=vmem(wide, BF16),
        grad_act=vmem(wide, F32), grad_proj=vmem((proj, rows), BF16),
        grad_conv=vmem((seqs, tokens + HALO, width), F32), rim_own=vmem((seqs, HALO, width), BF16),
        rim=vmem((seqs, HALO, width), BF16), rim_sems=dma((2 * seqs,)),
        grad_inner=vmem(wide, BF16),
        out_blocks=vmem((4, rows, shard), BF16), out_first=vmem((2, rows, shard), BF16),
        out_second=vmem((rows, shard), BF16), out_sems=dma((6,)),
        gn_blocks=vmem((4, rows, shard), BF16), gn_first=vmem((2, rows, shard), BF16),
        gn_second=vmem((rows, shard), BF16), gn_sems=dma((10,)),
        moment=vmem((8, rows), F32), moment_first=vmem((8, rows), F32),
        moment_mid=vmem((8, rows), F32), moment_second=vmem((8, rows), F32),
        early=vmem((early_rows, width), F32), later=vmem((later_rows, width), F32),
        gain_sums=vmem((seq_devices, 8, shard), F32), gain_sums_send=dma((seq_devices,)),
        gain_sums_recv=dma((seq_devices,)),
    )
    if gathered:
        every = (seq_devices * rows, width)
        ring_steps = seq_devices // 2
        scratch.update(
            gate_act_all=vmem(every, BF16), gate_slope_all=vmem(every, BF16),
            skip_all=vmem((seq_devices, seqs, tokens, width), BF16),
            inner_all=vmem((seq_devices, seqs, tokens, width), BF16),
            xo_ring_sems=dma((2, ring_steps, 2)), xo_chan_sems=dma((seq_devices - 1, 6)),
            skip_sems=dma((seqs, 2, ring_steps, 2)), inner_sems=dma((seqs, 2, ring_steps, 2)),
            early_own=vmem((early_rows, width), BF16), later_own=vmem((later_rows, width), BF16),
            early_land=vmem((seq_devices, early_rows // seq_devices, width), BF16),
            later_land=vmem((seq_devices, later_rows // seq_devices, width), BF16),
            early_sems=dma((4, seq_devices)), later_sems=dma((4, seq_devices)), result_sems=dma((5,)),
        )
    else:
        late = (model + early_rows + later_rows, width)
        scratch.update(
            cot=vmem((rows, model), BF16),
            grad_w_out=vmem(w_out.shape, BF16), land_w_out=vmem(w_out.shape, BF16), w_out_sems=dma((steps,)),
            grad_w_gate=vmem((model, width), BF16), land_w_gate=vmem((model, width), BF16),
            w_gate_sems=dma((steps,)),
            grad_w_inner=vmem(late, BF16), land_w_inner=vmem(late, BF16), full_w_inner=vmem(late, BF16),
            w_inner_sems=dma((steps,)),
        )
    names = list(operands) + list(outputs) + list(scratch)
    spaces = dict(lengths=pltpu.SMEM, w_in=pl.ANY, w_out=pl.ANY)
    mixed_out, grad_inputs, gain, w_in_grad, w_out_grad, early, later = pl.pallas_call(
        partial(layer_kernel, names, seq_devices),
        out_shape=tuple(jax.ShapeDtypeStruct(*item) for item in outputs.values()),
        in_specs=[pl.BlockSpec(memory_space=spaces.get(name, pltpu.VMEM)) for name in operands],
        out_specs=tuple(
            pl.BlockSpec(memory_space=pl.ANY if gathered and name in ("out_w_in", "out_w_out") else pltpu.VMEM)
            for name in outputs
        ),
        scratch_shapes=list(scratch.values()),
        compiler_params=pltpu.CompilerParams(
            collective_id=0, has_side_effects=True, vmem_limit_bytes=VMEM_LIMIT
        ),
    )(*operands.values())
    parts = 4

    def cut(shape, axis):
        block = tuple(size // parts if k == axis else size for k, size in enumerate(shape))
        return pl.BlockSpec(block, lambda i: tuple(i if k == axis else 0 for k in range(len(shape))))

    def kept(shape):
        return pl.BlockSpec(shape, lambda i: (0,) * len(shape))

    def result(shape, spec, dtype=F32):
        return jax.ShapeDtypeStruct(shape, dtype), spec

    tokens_cut = cut(inputs.shape, 1)
    w_in_cut, w_out_cut = (cut(w_in.shape, 1), cut(w_out.shape, 0))
    wide_row = ((1, width), kept((1, width)))
    results = [
        result(inputs.shape, tokens_cut, BF16), result(inputs.shape, tokens_cut, BF16),
        result((1, shard), kept((1, shard))), result(w_in.shape, w_in_cut),
        result(conv_weight.shape, kept(conv_weight.shape)), result(*wide_row),
        result(x_weight.shape, kept(x_weight.shape)), result(dt_weight.shape, kept(dt_weight.shape)),
        result(*wide_row), result(log_decay.shape, kept(log_decay.shape)), result(*wide_row),
        result(w_out.shape, w_out_cut),
    ]
    out = pl.pallas_call(
        partial(finish_kernel, (proj, low_rank, states, taps)),
        grid=(parts,),
        out_shape=tuple(item[0] for item in results),
        in_specs=[tokens_cut, tokens_cut, w_in_cut, w_out_cut, kept(early.shape), kept(later.shape), kept(gain.shape)],
        out_specs=tuple(item[1] for item in results),
        compiler_params=pltpu.CompilerParams(vmem_limit_bytes=VMEM_LIMIT),
    )(mixed_out, grad_inputs, w_in_grad, w_out_grad, early, later, gain)
    flat = (2, 5, 8, 10)
    return tuple(value.reshape(-1) if k in flat else value for k, value in enumerate(out))


def solution(mesh):
    in_specs = (
        P(None, "seq", "chan"), P(), P(None, "seq", "chan"), P("chan"), P(None, None, "chan"),
        P(None, "chan"), P("chan"), P(None, "chan"), P(None, "chan"), P("chan"), P(None, "chan"),
        P("chan"), P("chan", None),
    )
    out_specs = (
        P(None, "seq", "chan"), P(None, "seq", "chan"), P("chan"), P(None, None, "chan"),
        P(None, "chan"), P("chan"), P(None, "chan"), P(None, "chan"), P("chan"), P(None, "chan"),
        P("chan"), P("chan", None),
    )
    body = partial(layer, mesh.shape["seq"])
    return jax.shard_map(body, mesh=mesh, in_specs=in_specs, out_specs=out_specs, check_vma=False)
```

```python
from functools import partial
from types import SimpleNamespace

import jax
import jax.numpy as jnp
from jax import lax
from jax.experimental import pallas as pl
from jax.experimental.pallas import tpu as pltpu
from jax.sharding import PartitionSpec as P

EPSILON = 1e-05
LANES = 128
LOG2E = 1.4426950408889634
ROWS, RELAY, SKIP, INNER, SMALL, OTHERS = range(6)
SCHEDULE = {
    1: ((ROWS, 0),),
    3: ((ROWS, 0), (RELAY, 2),),
    5: ((ROWS, 0),),
    6: ((SKIP, 0),),
    8: ((SKIP, 1),),
    9: ((SKIP, 0),),
    10: ((SKIP, 1),),
    12: ((SKIP, 0), (ROWS, 0), (RELAY, 4),),
    13: ((OTHERS, 1),),
    14: ((SKIP, 1),),
    16: ((INNER, 0),),
    17: ((SKIP, 0), (INNER, 1),),
    18: ((SKIP, 1), (RELAY, 6), (OTHERS, 2), (INNER, 0),),
    19: ((INNER, 1), (RELAY, 7), (OTHERS, 3), (INNER, 0), (SMALL, 0), (OTHERS, 4), (INNER, 1),),
    24: ((INNER, 0),),
}
VMEM_LIMIT = 60 * 2**20
HALO = 16
MOST_GATHERED = 8
MESH = pl.DeviceIdType.MESH
F32 = jnp.float32
BF16 = jnp.bfloat16


def lane_chunks(width):
    return [slice(k * LANES, (k + 1) * LANES) for k in range(width // LANES)]


def flip(index, bit):
    return index + bit - 2 * bit * lax.rem(lax.div(index, bit), 2)


def dot(a, b, contract=((1,), (0,))):
    return lax.dot_general(a, b, (contract, ((), ())), preferred_element_type=F32)


def silu_slope(values, sigmoid):
    return sigmoid * (1.0 + values * (1.0 - sigmoid))


def softplus(values):
    return jnp.maximum(values, 0.0) + jnp.log1p(jnp.exp(-jnp.abs(values)))


def spread_maps(maps, b_ref, c_ref, first, tokens):
    states = maps.shape[0] // 2

    def block(index, _):
        start = index * 8
        rolled = pltpu.roll(maps, lax.rem(tokens - start, tokens), 1)
        for j in range(8):
            column = jnp.broadcast_to(rolled[:, j : j + 1], (2 * states, LANES))
            b_ref[first + start + j] = column[:states]
            c_ref[first + start + j] = column[states:]
        return 0

    lax.fori_loop(0, tokens // 8, block, 0)


def zero_states(rate_ref):
    states, width = rate_ref.shape
    return tuple(jnp.zeros((states, LANES), F32) for _ in lane_chunks(width))


def local_states(decay_ref, step_ref, drive_ref, b_ref, rate_ref, first, tokens):
    chunks = lane_chunks(rate_ref.shape[1])

    def block(index, held):
        held = list(held)
        rows = pl.ds(pl.multiple_of(first + index * 8, 8), 8)
        steps = [step_ref[rows, lanes] for lanes in chunks]
        drives = [drive_ref[rows, lanes] for lanes in chunks]
        for j in range(8):
            token = first + index * 8 + j
            b = b_ref[token]
            for k, lanes in enumerate(chunks):
                decay = jnp.exp2(steps[k][j : j + 1] * rate_ref[:, lanes])
                decay_ref[token, :, lanes] = decay
                held[k] = decay * held[k] + drives[k][j : j + 1] * b
        return tuple(held)

    return lax.fori_loop(0, tokens // 8, block, zero_states(rate_ref))


def local_adjoints(decay_ref, up_ref, c_ref, rate_ref, first, tokens):
    chunks = lane_chunks(rate_ref.shape[1])

    def block(index, held):
        held = list(held)
        start = first + (tokens // 8 - 1 - index) * 8
        rows = pl.ds(pl.multiple_of(start, 8), 8)
        ups = [up_ref[rows, lanes] for lanes in chunks]
        for j in range(7, -1, -1):
            token = start + j
            c = c_ref[token]
            for k, lanes in enumerate(chunks):
                adjoint = c * ups[k][j : j + 1] + held[k]
                held[k] = decay_ref[token, :, lanes] * adjoint
        return tuple(held)

    return lax.fori_loop(0, tokens // 8, block, zero_states(rate_ref))


def run_states(decay_ref, drive_ref, b_ref, c_ref, enter_ref, state_ref, out_ref, which, first, tokens):
    chunks = lane_chunks(decay_ref.shape[2])

    def block(index, held):
        held = list(held)
        rows = pl.ds(pl.multiple_of(first + index * 8, 8), 8)
        drives = [drive_ref[rows, lanes] for lanes in chunks]
        outs = [[] for _ in chunks]
        for j in range(8):
            token = first + index * 8 + j
            b, c = b_ref[token], c_ref[token]
            for k, lanes in enumerate(chunks):
                held[k] = decay_ref[token, :, lanes] * held[k] + drives[k][j : j + 1] * b
                state_ref[token, :, lanes] = held[k].astype(BF16)
                outs[k].append(jnp.sum(c * held[k], axis=0, keepdims=True))
        for k, lanes in enumerate(chunks):
            out_ref[pl.ds(pl.multiple_of(index * 8, 8), 8), lanes] = jnp.concatenate(outs[k], axis=0)
        return tuple(held)

    lax.fori_loop(0, tokens // 8, block, tuple(enter_ref[which, :, lanes] for lanes in chunks))


def run_adjoints(
    decay_ref, step_ref, up_ref, b_ref, c_ref, rate_ref, enter_ref, state_ref, adjoint_ref,
    first_sum_ref, second_sum_ref, which, first, tokens, span, carried,
):
    chunks = lane_chunks(rate_ref.shape[1])

    def block(index, carried):
        held, total = list(carried[0]), list(carried[1])
        ones = [[None] * 8 for _ in chunks]
        twos = [[None] * 8 for _ in chunks]
        start = first + (tokens // 8 - 1 - index) * 8
        rows = pl.ds(pl.multiple_of(start, 8), 8)
        ups = [up_ref[rows, lanes] for lanes in chunks]
        steps = [step_ref[rows, lanes] for lanes in chunks]
        for j in range(7, -1, -1):
            token = start + j
            b, c = b_ref[token], c_ref[token]
            for k, lanes in enumerate(chunks):
                adjoint = c * ups[k][j : j + 1] + held[k]
                adjoint_ref[token - first, :, lanes] = adjoint.astype(BF16)
                held[k] = decay_ref[token, :, lanes] * adjoint
                if j > 0:
                    before = state_ref[token - 1, :, lanes].astype(F32)
                else:
                    before = state_ref[jnp.maximum(token - 1, first), :, lanes].astype(F32)
                    before = jnp.where(token == first, enter_ref[which, :, lanes], before)
                pulled = held[k] * before
                ones[k][j] = jnp.sum(pulled * rate_ref[:, lanes], axis=0, keepdims=True)
                twos[k][j] = jnp.sum(adjoint * b, axis=0, keepdims=True)
                total[k] = total[k] + pulled * steps[k][j : j + 1]
        own_rows = pl.ds(pl.multiple_of(start - first, 8), 8)
        for k, lanes in enumerate(chunks):
            first_sum_ref[own_rows, lanes] = jnp.concatenate(ones[k], axis=0)
            second_sum_ref[own_rows, lanes] = jnp.concatenate(twos[k], axis=0)
        return tuple(held), tuple(total)

    return lax.fori_loop(span[0], span[1], block, carried)


def map_sums(values_ref, rows, states, first, tokens):
    width = rows.shape[1]
    flat = values_ref[first : first + tokens].reshape(tokens * states, width)
    all_pairs = dot(flat, rows.astype(BF16), ((1,), (1,)))
    row_token = lax.broadcasted_iota(jnp.int32, (tokens * states, tokens), 0) // states
    column_token = lax.broadcasted_iota(jnp.int32, (tokens * states, tokens), 1)
    kept = jnp.where(row_token == column_token, all_pairs, 0.0).astype(BF16)
    state = lax.broadcasted_iota(jnp.int32, (states, tokens * states), 0)
    row_state = lax.broadcasted_iota(jnp.int32, (states, tokens * states), 1) % states
    return dot((state == row_state).astype(BF16), kept)


def send(src, dst, send_sem, recv_sem, device):
    copy = pltpu.make_async_remote_copy(
        src_ref=src, dst_ref=dst, send_sem=send_sem, recv_sem=recv_sem,
        device_id=device, device_id_type=MESH,
    )
    copy.start()
    return copy


class ChanGather:
    def __init__(self, src, place, sems, mine, core_peer, x_peer):
        self.place, self.sems, self.mine, self.core_peer = (place, sems, mine, core_peer)
        self.over_x = send(src, place(mine), sems.at[0], sems.at[1], x_peer)
        self.over_core = send(src, place(mine), sems.at[2], sems.at[3], core_peer)

    def relay(self):
        self.over_x.wait_recv()
        block = self.place(flip(self.mine, 2))
        self.onward = send(block, block, self.sems.at[4], self.sems.at[5], self.core_peer)

    def finish(self):
        self.over_core.wait_recv()
        self.onward.wait_recv()
        for copy in (self.over_x, self.over_core, self.onward):
            copy.wait_send()


def ring_position(index, count):
    return lax.div(index, 2) + lax.rem(index, 2) * (count - 1 - 2 * lax.div(index, 2))


def ring_device(position, count):
    position = lax.rem(position + 2 * count, count)
    back = lax.div(position, count // 2)
    return 2 * position + back * (2 * (count - 1 - position) + 1 - 2 * position)


class RingGather:
    def __init__(self, place, sems, count, mine, chan, more_left):
        self.place, self.sems, self.count, self.chan = (place, sems, count, chan)
        self.position = ring_position(mine, count)
        most = count // 2
        self.steps = (most, count - 1 - most) if more_left else (count - 1 - most, most)
        self.length = most
        self.copies = []
        self.step = 0
        self.launch()

    def source(self, side, step):
        return ring_device(self.position + (step if side else -step), self.count)

    def launch(self):
        for side in range(2):
            if self.step < self.steps[side]:
                block = self.place(self.source(side, self.step))
                towards = ring_device(self.position + (-1 if side else 1), self.count)
                sems = self.sems.at[side, self.step]
                self.copies.append(send(block, block, sems.at[0], sems.at[1], (towards, self.chan)))

    def advance(self):
        if self.step == self.length:
            return []
        arrived = []
        for side in range(2):
            if self.step < self.steps[side]:
                source = self.source(side, self.step + 1)
                block = self.place(source)
                sems = self.sems.at[side, self.step]
                pltpu.make_async_remote_copy(
                    src_ref=block, dst_ref=block, send_sem=sems.at[0], recv_sem=sems.at[1],
                    device_id=(source, self.chan), device_id_type=MESH,
                ).wait_recv()
                arrived.append(source)
        self.step += 1
        self.launch()
        return arrived

    def finish(self):
        while self.step < self.length:
            self.advance()
        for copy in self.copies:
            copy.wait_send()


class GridGather:
    def __init__(self, place, ring_sems, chan_sems, count, me_s, me_c, core_peer, x_peer):
        self.place, self.mine, self.sems = (place, me_c, chan_sems)
        self.peers = (core_peer, x_peer)
        self.ring = RingGather(lambda d: place(me_c, d), ring_sems, count, me_s, me_c, True)
        self.gathers = []
        self.relayed = 0

    def advance(self):
        for source in self.ring.advance():
            self.gathers.append(
                ChanGather(
                    self.place(self.mine, source), partial(self.at, source), self.sems.at[len(self.gathers)],
                    self.mine, *self.peers,
                )
            )

    def at(self, source, chan):
        return self.place(chan, source)

    def relay(self, upto):
        while self.relayed < min(upto, len(self.gathers)):
            self.gathers[self.relayed].relay()
            self.relayed += 1

    def finish(self, step):
        for gather in self.gathers[2 * step - 2 : 2 * step]:
            gather.finish()


class ChanSum:
    def __init__(self, own, first, second, middle, sems, core_peer, x_peer):
        self.own, self.first, self.second, self.middle = (own, first, second, middle)
        self.sems, self.x_peer = (sems, x_peer)
        self.copies = [send(own, first, sems.at[0], sems.at[1], core_peer)]

    def cross(self):
        self.copies[0].wait_recv()
        self.middle[...] = self.own[...] + self.first[...]
        self.copies.append(send(self.middle, self.second, self.sems.at[2], self.sems.at[3], self.x_peer))

    def finish(self):
        self.copies[1].wait_recv()
        for copy in self.copies:
            copy.wait_send()
        return self.middle[...] + self.second[...]


class ChanScatter:
    def __init__(self, blocks, first, second, sems, mine, core_peer, x_peer, extra=None):
        self.blocks, self.first, self.second, self.sems = (blocks, first, second, sems)
        self.mine, self.x_peer, self.extra = (mine, x_peer, extra)
        other = flip(mine, 1)
        self.copies = [
            send(blocks.at[other], first.at[0], sems.at[0], sems.at[1], core_peer),
            send(blocks.at[flip(other, 2)], first.at[1], sems.at[2], sems.at[3], core_peer),
        ]
        if extra is not None:
            self.copies.append(send(extra[0], extra[1], sems.at[6], sems.at[7], core_peer))

    def cross(self):
        for copy in self.copies:
            copy.wait_recv()
        far = flip(self.mine, 2)
        self.blocks[far] = (self.blocks[far].astype(F32) + self.first[1].astype(F32)).astype(BF16)
        self.last = [send(self.blocks.at[far], self.second, self.sems.at[4], self.sems.at[5], self.x_peer)]
        if self.extra is not None:
            own, near, middle, across = self.extra
            middle[...] = own[...] + near[...]
            self.last.append(send(middle, across, self.sems.at[8], self.sems.at[9], self.x_peer))

    def finish(self):
        for copy in self.last:
            copy.wait_recv()
        for copy in self.copies + self.last:
            copy.wait_send()
        total = self.blocks[self.mine].astype(F32) + self.first[0].astype(F32) + self.second[...].astype(F32)
        if self.extra is None:
            return total
        return total, self.extra[2][...] + self.extra[3][...]


class SeqSum:
    def __init__(self, held, landing, full, sems, bits, mine, chan):
        self.held, self.landing, self.full, self.sems, self.bits = (held, landing, full, sems, bits)
        self.mine, self.chan = (mine, chan)
        self.regions = []
        self.copies = []
        start, size, place = (0, held.shape[0], 0)
        for bit in bits:
            half = size // 2
            mine_bit = lax.rem(lax.div(mine, bit), 2)
            keep = pl.multiple_of(start + mine_bit * half, 16)
            give = pl.multiple_of(start + (1 - mine_bit) * half, 16)
            self.regions.append((keep, give, half, place))
            start, size, place = (keep, half, place + half)
        self.step = 0
        self.total = 2 * len(bits)
        self.launch()

    def launch(self):
        step, count = (self.step, len(self.bits))
        sems = (self.sems.at[2 * step], self.sems.at[2 * step + 1])
        if step < count:
            _, give, half, place = self.regions[step]
            src, dst = (self.held.at[pl.ds(give, half)], self.landing.at[pl.ds(place, half)])
            bit = self.bits[step]
        else:
            keep, _, half, _ = self.regions[self.total - 1 - step]
            src = dst = self.full.at[pl.ds(keep, half)]
            bit = self.bits[self.total - 1 - step]
        self.copies.append(send(src, dst, *sems, (flip(self.mine, bit), self.chan)))

    def advance(self):
        if self.step == self.total:
            return
        self.copies[-1].wait_recv()
        if self.step < len(self.bits):
            keep, _, half, place = self.regions[self.step]
            rows = pl.ds(keep, half)
            got = self.landing[pl.ds(place, half)].astype(F32)
            into = self.held if self.step < len(self.bits) - 1 else self.full
            into[rows] = (self.held[rows].astype(F32) + got).astype(BF16)
        self.step += 1
        if self.step < self.total:
            self.launch()

    def finish(self):
        while self.step < self.total:
            self.advance()
        for copy in self.copies:
            copy.wait_send()


class DirectSum:
    def __init__(self, own, landing, full, sems, count, mine, chan):
        self.own, self.landing, self.full, self.sems = (own, landing, full, sems)
        self.count, self.mine, self.chan = (count, mine, chan)
        self.rows = own.shape[0] // count
        self.each(lambda k, peer: self.apart(peer, self.mine, peer).start())

    def piece(self, ref, device):
        return ref.at[pl.ds(pl.multiple_of(device * self.rows, self.rows), self.rows)]

    def each(self, act):
        def turn(k, _):
            act(k, lax.rem(self.mine + k, self.count))
            return 0

        lax.fori_loop(1, self.count, turn, 0)

    def apart(self, piece, source, peer):
        return pltpu.make_async_remote_copy(
            src_ref=self.piece(self.own, piece), dst_ref=self.landing.at[source],
            send_sem=self.sems.at[0, peer], recv_sem=self.sems.at[1, source],
            device_id=(peer, self.chan), device_id_type=MESH,
        )

    def back(self, source, peer):
        return pltpu.make_async_remote_copy(
            src_ref=self.piece(self.full, source), dst_ref=self.piece(self.full, source),
            send_sem=self.sems.at[2, peer], recv_sem=self.sems.at[3, source],
            device_id=(peer, self.chan), device_id_type=MESH,
        )

    def cross(self):
        self.each(lambda k, peer: self.apart(peer, peer, peer).wait_recv())
        mine = pl.ds(pl.multiple_of(self.mine * self.rows, self.rows), self.rows)

        def add(k, total):
            return total + self.landing[lax.rem(self.mine + k, self.count)].astype(F32)

        total = lax.fori_loop(1, self.count, add, self.own[mine].astype(F32))
        self.full[mine] = total.astype(BF16)
        self.each(lambda k, peer: self.back(self.mine, peer).start())

    def finish(self):
        self.each(lambda k, peer: self.back(peer, peer).wait_recv())
        self.each(lambda k, peer: self.apart(peer, self.mine, peer).wait_send())
        self.each(lambda k, peer: self.back(self.mine, peer).wait_send())


def pack_small(early, later, low_rank, proj):
    half = early.shape[1] // 2
    rest = [early[low_rank:], later[proj:]]
    spare = 2 * low_rank - proj - sum(part.shape[0] for part in rest)
    rest.append(jnp.zeros((spare, early.shape[1]), early.dtype))
    left = jnp.concatenate([later[:proj]] + rest, axis=0)
    right = jnp.concatenate([early[:low_rank, :half], early[:low_rank, half:]], axis=0)
    return jnp.concatenate([left, right], axis=1)


def layer_kernel(names, seq_devices, *refs):
    r = SimpleNamespace(**dict(zip(names, refs)))
    x_ref, og_ref, win_ref, wout_ref = (r.inputs, r.out_grad, r.w_in_here, r.w_out_here)
    xw_ref, dtw_ref = (r.x_weight, r.dt_weight)
    seqs, tokens, shard = x_ref.shape
    model, width = win_ref.shape[1:]
    states = r.log_decay.shape[0]
    low_rank = dtw_ref.shape[0]
    taps = r.conv_weight.shape[0]
    proj = xw_ref.shape[0]
    me_s, me_c = (lax.axis_index("seq"), lax.axis_index("chan"))
    core_peer, x_peer = ((me_s, flip(me_c, 1)), (me_s, flip(me_c, 2)))
    right, left = (lax.rem(me_s + 1, seq_devices), lax.rem(me_s + seq_devices - 1, seq_devices))
    position = ring_position(me_s, seq_devices)
    gathered = seq_devices <= MOST_GATHERED
    spot = me_s if gathered else 0

    loads = []
    for k, (src, dst) in enumerate(((r.w_in, r.w_in_here), (r.w_out, r.w_out_here))):
        loads.append(pltpu.make_async_copy(src, dst, r.load_sems.at[k]))
        loads[k].start()

    barrier = pltpu.get_barrier_semaphore()

    def greet(semaphore, device):
        pl.semaphore_signal(semaphore, inc=1, device_id=device, device_id_type=MESH)

    ring = [(ring_device(position + step, seq_devices), me_c) for step in (1, -1)]
    first_peers = [core_peer, x_peer, (right, me_c), (left, me_c)] + ring
    for device in first_peers:
        greet(barrier, device)
    pl.semaphore_wait(barrier, len(first_peers))

    xo_ref, halo_ref = (r.xo, r.halo)
    gather_x = [
        ChanGather(
            x_ref.at[s], partial(lambda s, q: xo_ref.at[q, spot, 0, s], s), r.x_sems.at[s], me_c, core_peer, x_peer
        )
        for s in range(seqs)
    ]
    halo_copy = send(
        x_ref.at[:, pl.ds(tokens - HALO, HALO), :], halo_ref.at[me_c, pl.ds(0, seqs)],
        r.halo_sems.at[6], r.halo_sems.at[7], (right, me_c),
    )
    for device in ring:
        greet(r.known.at[0], device)
    gather_og = ChanGather(og_ref, lambda q: xo_ref.at[q, spot, 1], r.og_sems, me_c, core_peer, x_peer)
    xo_ref[me_c, spot, 0] = x_ref[...]
    xo_ref[me_c, spot, 1] = og_ref[...]
    halo_ref[me_c, seqs] = jnp.broadcast_to(r.norm_gain[...].astype(F32).reshape(1, shard), (HALO, shard)).astype(BF16)
    if gathered:
        gather_all = GridGather(
            lambda q, d: xo_ref.at[q, d], r.xo_ring_sems, r.xo_chan_sems, seq_devices, me_s, me_c, core_peer, x_peer
        )
    skip_gathers, inner_gathers, small_sums, sums = ([], [], [], [])

    def hook(place):
        if not gathered:
            if place > 6:
                for item in sums:
                    item.advance()
            return
        for kind, which in SCHEDULE.get(place, ()):
            if kind == ROWS:
                gather_all.advance()
            elif kind == RELAY:
                gather_all.relay(which)
            elif kind == SKIP:
                skip_gathers[which].advance()
            elif kind == INNER:
                inner_gathers[which].advance()
            elif kind == SMALL:
                small_sums[0].cross()
            else:
                foreign_pair(which)

    halo_copy.wait_recv()
    gather_halo = ChanGather(
        halo_ref.at[me_c], lambda q: halo_ref.at[q], r.halo_sems, me_c, core_peer, x_peer
    )
    for s in range(seqs):
        gather_x[s].relay()
    gather_halo.relay()
    gather_x[0].finish()
    gather_halo.finish()
    halo_copy.wait_send()

    reaches = [1]
    while 2 * reaches[-1] < seq_devices // 2:
        reaches.append(2 * reaches[-1])

    def hear(k):
        pl.semaphore_wait(r.known.at[k], 2)
        if k + 1 < len(reaches):
            for step in (reaches[k + 1], -reaches[k + 1]):
                greet(r.known.at[k + 1], (ring_device(position + step, seq_devices), me_c))

    rate_ref, rate2_ref = (r.rate, r.rate2)
    rate_ref[...] = -jnp.exp(r.log_decay[...])
    rate2_ref[...] = rate_ref[...] * LOG2E

    def mask_of(s, rows, begin):
        positions = me_s * tokens + begin + lax.broadcasted_iota(jnp.int32, (rows, 1), 0)
        return (positions < r.lengths[s]).astype(F32)

    def gain_of(q):
        return halo_ref[q, seqs, 0:1, :].astype(F32)

    def normalize(blocks):
        squares = sum(jnp.sum(b * b, axis=1, keepdims=True) for b in blocks)
        root = lax.rsqrt(squares * (1.0 / model) + EPSILON)
        return root, [(b * root * gain_of(q)).astype(BF16) for q, b in enumerate(blocks)]

    hear(0)
    loads[0].wait()

    conv_sum = []
    normed_rows = []
    has_left = (me_s > 0).astype(F32)
    for s in range(seqs):
        mine = pl.ds(s * tokens, tokens)
        if s > 0:
            gather_x[s].finish()
        root, rows = normalize([xo_ref[q, spot, 0, s].astype(F32) for q in range(4)])
        _, before = normalize([halo_ref[q, s].astype(F32) for q in range(4)])
        r.root[mine, :] = jnp.broadcast_to(root, (tokens, LANES))
        normed, normed_before = (jnp.concatenate(rows, axis=1), jnp.concatenate(before, axis=1))
        normed_rows.append(pl.ds(pl.multiple_of(spot * seqs * tokens + s * tokens, tokens), tokens))
        r.normed[normed_rows[s], :] = normed
        inner = dot(normed, win_ref[0]).astype(BF16).astype(F32) * mask_of(s, tokens, 0)
        inner_before = dot(normed_before, win_ref[0]).astype(BF16).astype(F32)
        inner_before = inner_before * (mask_of(s, HALO, -HALO) * has_left)
        r.inner[s, HALO:, :] = inner
        r.inner[s, :HALO, :] = inner_before
        conv_pre = r.conv_bias[...] + sum(
            r.conv_weight[k : k + 1, :] * r.inner[s, HALO - taps + 1 + k : HALO - taps + 1 + k + tokens, :]
            for k in range(taps)
        )
        r.conv_pre[mine, :] = conv_pre
        act = (conv_pre * jax.nn.sigmoid(conv_pre)).astype(BF16)
        r.act[mine, :] = act.astype(F32)
        r.proj_own[s] = dot(xw_ref[...], act, ((1,), (1,)))
        conv_sum.append(
            ChanSum(
                r.proj_own.at[s], r.proj_first.at[s], r.proj_second.at[s], r.proj_mid.at[s],
                r.proj_sems.at[s], core_peer, x_peer,
            )
        )
    gather_og.relay()
    for s in range(seqs):
        conv_sum[s].cross()
    hook(0)
    for s in range(seqs):
        mine = pl.ds(s * tokens, tokens)
        r.gate_pre[mine, :] = dot(r.normed[normed_rows[s], :], win_ref[1])
    gather_og.finish()
    loads[1].wait()
    for s in range(seqs):
        mine = pl.ds(s * tokens, tokens)
        cot = jnp.concatenate([xo_ref[q, spot, 1, s] for q in range(4)], axis=1)
        grad_mixed = dot(cot, wout_ref[...], ((1,), (1,))) * mask_of(s, tokens, 0)
        gate = r.gate_pre[mine, :]
        sigmoid = jax.nn.sigmoid(gate)
        r.grad_mixed[mine, :] = grad_mixed
        r.up[mine, :] = grad_mixed * (gate * sigmoid)
        if gathered:
            rows = normed_rows[s]
            r.gate_act_all[rows, :] = (gate * sigmoid * mask_of(s, tokens, 0)).astype(BF16)
            r.gate_slope_all[rows, :] = (grad_mixed * silu_slope(gate, sigmoid)).astype(BF16)
        else:
            r.cot[mine, :] = (cot.astype(F32) * mask_of(s, tokens, 0)).astype(BF16)
    hook(1)

    totals_ref = r.totals
    step_totals = []
    for s in range(seqs):
        mine = pl.ds(s * tokens, tokens)
        projected = conv_sum[s].finish()
        low = projected[:low_rank].astype(BF16)
        r.low[:, s * tokens : (s + 1) * tokens] = low
        step_pre = dot(projected[:low_rank].T.astype(BF16), dtw_ref[...]) + r.dt_bias[...]
        r.step_pre[mine, :] = step_pre
        step = softplus(step_pre)
        r.step[mine, :] = step
        r.drive[mine, :] = step * r.act[mine, :]
        step_totals.append(jnp.sum(step, axis=0, keepdims=True))
        spread_maps(projected[low_rank:], r.b, r.c, s * tokens, tokens)
    hook(2)
    totals_ref[me_s] = jnp.concatenate(step_totals + [jnp.zeros((8 - seqs, width), F32)], axis=0)

    def seq_device(k):
        return (k, me_c)

    def totals_copy(k):
        peer = lax.rem(me_s + k, seq_devices)
        return pltpu.make_async_remote_copy(
            src_ref=totals_ref.at[me_s], dst_ref=totals_ref.at[me_s],
            send_sem=r.totals_send.at[k], recv_sem=r.totals_recv.at[me_s],
            device_id=seq_device(peer), device_id_type=MESH,
        )

    def start_totals(k, _):
        totals_copy(k).start()
        return 0

    for k in range(1, len(reaches)):
        hear(k)
    lax.fori_loop(1, seq_devices, start_totals, 0)

    ends_refs = (r.ends, r.ends_send, r.ends_recv)
    leaves_refs = (r.leaves, r.leaves_send, r.leaves_recv)

    def carried_copy(which, s, peer):
        ref, send_sem, recv_sem = which
        return pltpu.make_async_remote_copy(
            src_ref=ref.at[s, me_s], dst_ref=ref.at[s, me_s],
            send_sem=send_sem.at[s, peer], recv_sem=recv_sem.at[s, me_s],
            device_id=seq_device(peer), device_id_type=MESH,
        )

    def start_carried(which, s, begin, end):
        def start(peer, _):
            carried_copy(which, s, peer).start()
            return 0

        lax.fori_loop(begin, end, start, 0)

    def wait_carried(which, s, begin, end):
        def wait(peer, _):
            carried_copy(which, s, peer).wait_send()
            return 0

        lax.fori_loop(begin, end, wait, 0)

    for s in range(seqs):
        ends = local_states(r.decay, r.step, r.drive, r.b, rate2_ref, s * tokens, tokens)
        for k, lanes in enumerate(lane_chunks(width)):
            r.ends[s, me_s, :, lanes] = ends[k].astype(BF16)
        start_carried(ends_refs, s, me_s + 1, seq_devices)
    hook(3)
    for s in range(seqs):
        leaves = local_adjoints(r.decay, r.up, r.c, rate_ref, s * tokens, tokens)
        for k, lanes in enumerate(lane_chunks(width)):
            r.leaves[s, me_s, :, lanes] = leaves[k].astype(BF16)
        start_carried(leaves_refs, s, 0, me_s)

    hook(4)

    def wait_totals(k, _):
        peer = lax.rem(me_s + k, seq_devices)
        pltpu.make_async_remote_copy(
            src_ref=totals_ref.at[peer], dst_ref=totals_ref.at[peer],
            send_sem=r.totals_send.at[k], recv_sem=r.totals_recv.at[peer],
            device_id=seq_device(peer), device_id_type=MESH,
        ).wait_recv()
        return 0

    lax.fori_loop(1, seq_devices, wait_totals, 0)

    def combine(which, s, count, place):
        ref, send_sem, recv_sem = which

        def turn(k, held):
            peer = place(k)
            pltpu.make_async_remote_copy(
                src_ref=ref.at[s, peer], dst_ref=ref.at[s, peer],
                send_sem=send_sem.at[s, peer], recv_sem=recv_sem.at[s, peer],
                device_id=seq_device(peer), device_id_type=MESH,
            ).wait_recv()
            total = totals_ref[peer][s : s + 1]
            return jnp.exp2(total * rate2_ref[...]) * held + ref[s, peer].astype(F32)

        return lax.fori_loop(0, count, turn, jnp.zeros((states, width), F32))

    def block_of(ref, s, device):
        return ref.at[device, s]

    def foreign_pair(step):
        gather_all.finish(step)
        last = 2 * step == seq_devices
        lax.fori_loop(0, 1 if last else 2, partial(foreign, step), 0)

    def foreign(step, side, _):
        device = ring_device(position + step - 2 * step * side, seq_devices)
        rows = pl.ds(pl.multiple_of(device * (seqs * tokens), seqs * tokens), seqs * tokens)
        blocks = [xo_ref[q, device, 0].reshape(seqs * tokens, shard).astype(F32) for q in range(4)]
        normed = jnp.concatenate(normalize(blocks)[1], axis=1)
        r.normed[rows, :] = normed
        gate = dot(normed, win_ref[1])
        sigmoid = jax.nn.sigmoid(gate)
        cot = jnp.concatenate([xo_ref[q, device, 1].reshape(seqs * tokens, shard) for q in range(4)], axis=1)
        mask = jnp.concatenate([mask_of(s, tokens, (device - me_s) * tokens) for s in range(seqs)], axis=0)
        grad_mixed = dot(cot, wout_ref[...], ((1,), (1,))) * mask
        r.gate_act_all[rows, :] = (gate * sigmoid * mask).astype(BF16)
        r.gate_slope_all[rows, :] = (grad_mixed * silu_slope(gate, sigmoid)).astype(BF16)
        return 0

    for s in range(seqs):
        mine = pl.ds(s * tokens, tokens)
        r.entering[s] = combine(ends_refs, s, me_s, lambda k: k)
        run_states(
            r.decay, r.drive, r.b, r.c, r.entering, r.state, r.scanned, s, s * tokens, tokens
        )
        gate = r.gate_pre[mine, :]
        sigmoid = jax.nn.sigmoid(gate)
        with_skip = r.scanned[...] + r.skip_gain[...] * r.act[mine, :]
        mixed = (with_skip * (gate * sigmoid)).astype(BF16)
        r.mixed[mine, :] = mixed
        r.grad_gate[mine, :] = (r.grad_mixed[mine, :] * with_skip * silu_slope(gate, sigmoid)).astype(BF16)
        if gathered:
            r.skip_all[me_s, s] = with_skip.astype(BF16)
            skip_gathers.append(
                RingGather(
                    partial(block_of, r.skip_all, s), r.skip_sems.at[s], seq_devices, me_s, me_c, s == 0
                )
            )
        if s == 0:
            hook(5)
    out_part = dot(r.mixed[...], wout_ref[...])
    for q in range(4):
        r.out_blocks[q] = out_part[:, q * shard : (q + 1) * shard].astype(BF16)
    scatter_out = ChanScatter(
        r.out_blocks, r.out_first, r.out_second, r.out_sems, me_c, core_peer, x_peer
    )
    bits = [1 << k for k in range(seq_devices.bit_length() - 1)]
    turned = bits[1:] + bits[:1]
    hook(6)
    if not gathered:
        r.grad_w_out[...] = dot(r.mixed[...], r.cot[...], ((0,), (0,))).astype(BF16)
        sums.append(SeqSum(r.grad_w_out, r.land_w_out, r.out_w_out, r.w_out_sems, bits, me_s, me_c))
        r.grad_w_gate[...] = dot(r.normed[...], r.grad_gate[...], ((0,), (0,))).astype(BF16)
        sums.append(SeqSum(r.grad_w_gate, r.land_w_gate, r.out_w_in.at[1], r.w_gate_sems, turned, me_s, me_c))

    early, later = (r.early, r.later)
    early[...] = jnp.zeros_like(early)
    later[...] = jnp.zeros_like(later)
    skip_row = low_rank + states + 1
    low_sum, rim_copies, rate_sums = ([], [], [])
    has_right = (me_s < seq_devices - 1).astype(F32)

    def scan_back(s, services):
        leaving = combine(leaves_refs, s, seq_devices - 1 - me_s, lambda k: seq_devices - 1 - k)
        carried = (tuple(leaving[:, lanes] for lanes in lane_chunks(width)), zero_states(rate_ref))
        parts, blocks = (len(services), tokens // 8)
        for part, service in enumerate(services):
            carried = run_adjoints(
                r.decay, r.step, r.up, r.b, r.c, rate_ref, r.entering, r.state,
                r.adjoint, r.first_sum, r.second_sum, s, s * tokens, tokens,
                (part * blocks // parts, (part + 1) * blocks // parts), carried,
            )
            service()
        rate_sums.append(carried[1])

    def after_scan(s):
        mine = pl.ds(s * tokens, tokens)
        act, step, step_pre = (r.act[mine, :], r.step[mine, :], r.step_pre[mine, :])
        second = r.second_sum[...]
        grad_step_pre = (r.first_sum[...] + act * second) * jax.nn.sigmoid(step_pre)
        grad_step_low = grad_step_pre.astype(BF16)
        own = r.proj_own.at[s]
        own[:low_rank, :] = dot(dtw_ref[...], grad_step_low, ((1,), (1,)))
        own[low_rank : low_rank + states, :] = map_sums(r.adjoint, r.drive[mine, :], states, 0, tokens)
        own[low_rank + states :, :] = map_sums(r.state, r.up[mine, :], states, s * tokens, tokens)
        low_sum.append(
            ChanSum(
                own, r.back_first.at[s], r.back_second.at[s], r.back_mid.at[s],
                r.back_sems.at[s], core_peer, x_peer,
            )
        )
        r.grad_step_low[mine, :] = grad_step_low
        early[skip_row - 1, :] += jnp.sum(grad_step_pre, axis=0)
        early[skip_row, :] += jnp.sum(r.up[mine, :] * act, axis=0)
        r.grad_act[mine, :] = step * second + r.up[mine, :] * r.skip_gain[...]

    def through_conv(s):
        mine = pl.ds(s * tokens, tokens)
        grad_projected = low_sum[s].finish()
        r.grad_proj[:, s * tokens : (s + 1) * tokens] = grad_projected.astype(BF16)
        grad_act = r.grad_act[mine, :] + dot(grad_projected.T.astype(BF16), xw_ref[...])
        conv_pre = r.conv_pre[mine, :]
        grad_conv = (grad_act * silu_slope(conv_pre, jax.nn.sigmoid(conv_pre))).astype(BF16)
        r.rim_own[s] = grad_conv[:HALO]
        rim_copies.append(
            send(r.rim_own.at[s], r.rim.at[s], r.rim_sems.at[2 * s], r.rim_sems.at[2 * s + 1], (left, me_c))
        )
        grad_conv = grad_conv.astype(F32)
        r.grad_conv[s, :tokens, :] = grad_conv
        later[proj + taps, :] += jnp.sum(grad_conv, axis=0)
        for k in range(taps):
            shifted = r.inner[s, HALO - taps + 1 + k : HALO - taps + 1 + k + tokens, :]
            later[proj + k, :] += jnp.sum(grad_conv * shifted, axis=0)

    def inner_of(s):
        mine = pl.ds(s * tokens, tokens)
        rim_copies[s].wait_recv()
        rim_copies[s].wait_send()
        r.grad_conv[s, tokens:, :] = r.rim[s].astype(F32) * has_right
        grad_inner = sum(
            r.conv_weight[k : k + 1, :] * r.grad_conv[s, taps - 1 - k : taps - 1 - k + tokens, :]
            for k in range(taps)
        )
        grad_inner = (grad_inner * mask_of(s, tokens, 0)).astype(BF16)
        r.grad_inner[mine, :] = grad_inner
        if gathered:
            r.inner_all[me_s, s] = grad_inner
            inner_gathers.append(
                RingGather(
                    partial(block_of, r.inner_all, s), r.inner_sems.at[s], seq_devices, me_s, me_c, s == 0
                )
            )

    def nothing():
        pass

    def scatter_and_hook():
        scatter_out.cross()
        hook(7)

    scan_back(0, (nothing, scatter_and_hook, nothing, partial(hook, 8)))
    after_scan(0)
    hook(9)
    scan_back(1, (low_sum[0].cross, partial(hook, 10), partial(through_conv, 0), partial(hook, 11)))
    after_scan(1)
    hook(12)
    inner_of(0)
    for k, lanes in enumerate(lane_chunks(width)):
        early[low_rank : low_rank + states, lanes] = (rate_sums[0][k] + rate_sums[1][k]) * rate_ref[:, lanes]
    early[:low_rank, :] = dot(r.low[...], r.grad_step_low[...])
    low_sum[1].cross()
    hook(13)
    out_sum = scatter_out.finish()
    for s in range(seqs):
        r.mixed_out[s] = (x_ref[s].astype(F32) + out_sum[s * tokens : (s + 1) * tokens]).astype(BF16)
    hook(14)
    through_conv(1)
    later[:proj, :] = dot(r.grad_proj[...], r.act[...].astype(BF16))
    if gathered:
        r.small_own[...] = pack_small(
            early[: skip_row + 1, :], later[: proj + taps + 1, :], low_rank, proj
        ).astype(BF16)
        small_sums.append(
            DirectSum(r.small_own, r.small_land, r.out_small, r.small_sems, seq_devices, me_s, me_c)
        )
    hook(15)
    inner_of(1)
    hook(16)

    if not gathered:
        late = r.grad_w_inner
        late[:model, :] = dot(r.normed[...], r.grad_inner[...], ((0,), (0,))).astype(BF16)
        late[model : model + early.shape[0], :] = early[...].astype(BF16)
        late[model + early.shape[0] :, :] = later[...].astype(BF16)
        sums.append(SeqSum(late, r.land_w_inner, r.full_w_inner, r.w_inner_sems, bits, me_s, me_c))
    moment = None
    for q in range(4):
        part = dot(r.grad_inner[...], win_ref[0, q * shard : (q + 1) * shard, :], ((1,), (1,)))
        part = part + dot(r.grad_gate[...], win_ref[1, q * shard : (q + 1) * shard, :], ((1,), (1,)))
        values = xo_ref[q, spot, 0].reshape(seqs * tokens, shard).astype(F32)
        term = jnp.sum(part * gain_of(q) * values, axis=1, keepdims=True)
        moment = term if moment is None else moment + term
        r.gn_blocks[q] = part.astype(BF16)
    r.moment[...] = jnp.broadcast_to(moment, (seqs * tokens, LANES)).T[:8]
    scatter_gn = ChanScatter(
        r.gn_blocks, r.gn_first, r.gn_second, r.gn_sems, me_c, core_peer, x_peer,
        (r.moment, r.moment_first, r.moment_mid, r.moment_second),
    )
    hook(17)
    scatter_gn.cross()
    hook(18)
    grad_normed, moment_row = scatter_gn.finish()
    moment = jnp.broadcast_to(moment_row[:1], (LANES, seqs * tokens)).T[:, :1]
    root = r.root[:, :1]
    values = x_ref[...].reshape(seqs * tokens, shard).astype(F32)
    gains = gain_of(me_c)
    back = root * (grad_normed * gains) - values * (root * root * root) * moment * (1.0 / model)
    for s in range(seqs):
        mine = slice(s * tokens, (s + 1) * tokens)
        cot = og_ref[s].astype(F32) * mask_of(s, tokens, 0)
        r.grad_inputs[s] = (cot + back[mine]).astype(BF16)
    gain_sums_ref = r.gain_sums
    gain_sums_ref[me_s] = jnp.broadcast_to(jnp.sum(grad_normed * values * root, axis=0, keepdims=True), (8, shard))

    def gain_copy(k):
        peer = lax.rem(me_s + k, seq_devices)
        return pltpu.make_async_remote_copy(
            src_ref=gain_sums_ref.at[me_s], dst_ref=gain_sums_ref.at[me_s],
            send_sem=r.gain_sums_send.at[k], recv_sem=r.gain_sums_recv.at[me_s],
            device_id=seq_device(peer), device_id_type=MESH,
        )

    def start_gain(k, _):
        gain_copy(k).start()
        return 0

    lax.fori_loop(1, seq_devices, start_gain, 0)
    hook(19)
    if gathered:
        gather_all.ring.finish()
        for gather in skip_gathers:
            gather.finish()
        count = seq_devices * seqs * tokens

        def mix(device, _):
            rows = pl.ds(pl.multiple_of(device * (seqs * tokens), seqs * tokens), seqs * tokens)
            with_skip = r.skip_all[device].reshape(seqs * tokens, width).astype(F32)
            r.gate_act_all[rows, :] = (r.gate_act_all[rows, :].astype(F32) * with_skip).astype(BF16)
            r.gate_slope_all[rows, :] = (r.gate_slope_all[rows, :].astype(F32) * with_skip).astype(BF16)
            return 0

        lax.fori_loop(0, seq_devices, mix, 0)
        hook(20)
        results = []

        def deliver(src, dst):
            copy = pltpu.make_async_copy(src, dst, r.result_sems.at[len(results)])
            copy.start()
            results.append(copy)

        staged = r.skip_all.reshape(count, width)
        for q in range(4):
            outs = xo_ref[q, :, 1].reshape(count, shard)
            half, place = (q * shard // width, q * shard % width)
            rows = pl.ds(half * width, width)
            staged[rows, place : place + shard] = dot(r.gate_act_all[...], outs, ((0,), (0,))).astype(BF16)
            if place + shard == width:
                deliver(staged.at[rows], r.out_w_out.at[:, pl.ds(half * width, width)])
            hook(21 + q)
        for q in range(4):
            rows = slice(q * shard, (q + 1) * shard)
            r.gate_act_all[rows, :] = dot(r.normed[:, rows], r.gate_slope_all[...], ((0,), (0,))).astype(BF16)
            hook(25 + q)
        deliver(r.gate_act_all.at[pl.ds(0, model)], r.out_w_in.at[1])
        for gather in inner_gathers:
            gather.finish()
        inner_rows = r.inner_all[...].reshape(count, width)
        for q in range(4):
            rows = slice(model + q * shard, model + (q + 1) * shard)
            cols = slice(q * shard, (q + 1) * shard)
            r.gate_act_all[rows, :] = dot(r.normed[:, cols], inner_rows, ((0,), (0,))).astype(BF16)
            if q % 2 == 1:
                deliver(
                    r.gate_act_all.at[pl.ds(model + (q - 1) * shard, 2 * shard)],
                    r.out_w_in.at[0, pl.ds((q - 1) * shard, 2 * shard)],
                )
        small_sums[0].finish()
    else:
        for step in range(max(item.total for item in sums)):
            for item in sums:
                item.advance()

    def take_gain(k, _):
        peer = lax.rem(me_s + k, seq_devices)
        pltpu.make_async_remote_copy(
            src_ref=gain_sums_ref.at[peer], dst_ref=gain_sums_ref.at[peer],
            send_sem=r.gain_sums_send.at[k], recv_sem=r.gain_sums_recv.at[peer],
            device_id=seq_device(peer), device_id_type=MESH,
        ).wait_recv()
        gain_copy(k).wait_send()
        totals_copy(k).wait_send()
        return 0

    lax.fori_loop(1, seq_devices, take_gain, 0)
    r.grad_gain[...] = jnp.sum(gain_sums_ref[...], axis=0)
    for item in sums:
        item.finish()
    if gathered:
        for copy in results:
            copy.wait()
    else:
        r.out_w_in[0] = r.full_w_inner[:model, :]
        full, rest = (r.full_w_inner, model + early.shape[0])
        r.out_small[...] = pack_small(
            full[model : model + skip_row + 1, :].astype(F32), full[rest : rest + proj + taps + 1, :].astype(F32),
            low_rank, proj,
        ).astype(BF16)
    for s in range(seqs):
        wait_carried(ends_refs, s, me_s + 1, seq_devices)
        wait_carried(leaves_refs, s, 0, me_s)


def finish_kernel(
    rows_of, mixed_ref, inputs_ref, w_in_ref, w_out_ref, small_ref, gain_ref,
    mixed_out, grad_inputs, gain_out, w_in_out, conv_w_out, conv_b_out, x_out, dt_w_out, dt_b_out, decay_out,
    skip_out, w_out_out,
):
    mixed_out[...] = mixed_ref[...]
    grad_inputs[...] = inputs_ref[...]
    w_in_out[...] = w_in_ref[...].astype(F32)
    w_out_out[...] = w_out_ref[...].astype(F32)

    @pl.when(pl.program_id(0) == 0)
    def _():
        proj, low_rank, states, taps = rows_of
        small, width = (small_ref[...].astype(F32), x_out.shape[1])
        left, right = (small[:, :width], small[:, width:])
        tap_row = proj + states + 2
        gain_out[...] = gain_ref[0:1, :]
        x_out[...] = left[:proj]
        dt_w_out[:, : width // 2] = right[:low_rank]
        dt_w_out[:, width // 2 :] = right[low_rank:]
        decay_out[...] = left[proj : proj + states]
        dt_b_out[...] = left[tap_row - 2 : tap_row - 1]
        skip_out[...] = left[tap_row - 1 : tap_row]
        conv_w_out[...] = left[tap_row : tap_row + taps]
        conv_b_out[...] = left[tap_row + taps : tap_row + taps + 1]


def layer(
    seq_devices,
    inputs, lengths, out_grad, norm_gain, w_in, conv_weight, conv_bias, x_weight, dt_weight,
    dt_bias, log_decay, skip_gain, w_out,
):
    seqs, tokens, shard = inputs.shape
    _, model, width = w_in.shape
    states, low_rank, taps, proj = (log_decay.shape[0], dt_weight.shape[0], conv_weight.shape[0], x_weight.shape[0])
    rows = seqs * tokens
    grain = 16 * seq_devices if seq_devices <= MOST_GATHERED else 8 * seq_devices
    early_rows = -(-(low_rank + states + 2) // grain) * grain
    later_rows = -(-(proj + taps + 1) // grain) * grain
    steps = 4 * (seq_devices.bit_length() - 1)
    gathered = seq_devices <= MOST_GATHERED
    dma = pltpu.SemaphoreType.DMA
    vmem = pltpu.VMEM
    operands = dict(
        inputs=inputs, lengths=lengths, out_grad=out_grad, norm_gain=norm_gain,
        w_in=w_in, conv_weight=conv_weight, conv_bias=conv_bias.reshape(1, width),
        x_weight=x_weight, dt_weight=dt_weight, dt_bias=dt_bias.reshape(1, width),
        log_decay=log_decay, skip_gain=skip_gain.reshape(1, width), w_out=w_out,
    )
    outputs = dict(
        mixed_out=(inputs.shape, BF16), grad_inputs=(inputs.shape, BF16), grad_gain=((8, shard), F32),
        out_w_in=(w_in.shape, BF16), out_w_out=(w_out.shape, BF16),
        out_small=((2 * low_rank, width + width // 2), BF16),
    )
    wide = (rows, width)
    scratch = dict(
        xo=vmem((4, seq_devices if gathered else 1, 2) + inputs.shape, BF16),
        halo=vmem((4, seqs + 1, HALO, shard), BF16), known=pltpu.SemaphoreType.REGULAR((8,)),
        w_in_here=vmem(w_in.shape, BF16), w_out_here=vmem(w_out.shape, BF16), load_sems=dma((2,)),
        x_sems=dma((seqs, 6)), og_sems=dma((6,)), halo_sems=dma((8,)),
        rate=vmem((states, width), F32), rate2=vmem((states, width), F32),
        root=vmem((rows, LANES), F32), normed=vmem((seq_devices * rows if gathered else rows, model), BF16),
        inner=vmem((seqs, HALO + tokens, width), F32),
        conv_pre=vmem(wide, F32), act=vmem(wide, F32), gate_pre=vmem(wide, F32),
        grad_mixed=vmem(wide, F32), up=vmem(wide, F32),
        proj_own=vmem((seqs, proj, tokens), F32), proj_first=vmem((seqs, proj, tokens), F32),
        proj_second=vmem((seqs, proj, tokens), F32), proj_mid=vmem((seqs, proj, tokens), F32),
        proj_sems=dma((seqs, 4)),
        back_first=vmem((seqs, proj, tokens), F32), back_second=vmem((seqs, proj, tokens), F32),
        back_mid=vmem((seqs, proj, tokens), F32), back_sems=dma((seqs, 4)),
        low=vmem((low_rank, rows), BF16), step_pre=vmem(wide, F32), step=vmem(wide, F32),
        drive=vmem(wide, F32), b=vmem((rows, states, LANES), F32), c=vmem((rows, states, LANES), F32),
        decay=vmem((rows, states, width), F32),
        totals=vmem((seq_devices, 8, width), F32), totals_send=dma((seq_devices,)),
        totals_recv=dma((seq_devices,)),
        ends=vmem((seqs, seq_devices, states, width), BF16), ends_send=dma((seqs, seq_devices)),
        ends_recv=dma((seqs, seq_devices)),
        leaves=vmem((seqs, seq_devices, states, width), BF16), leaves_send=dma((seqs, seq_devices)),
        leaves_recv=dma((seqs, seq_devices)),
        entering=vmem((seqs, states, width), F32),
        state=vmem((rows, states, width), BF16), adjoint=vmem((tokens, states, width), BF16),
        scanned=vmem((tokens, width), F32), first_sum=vmem((tokens, width), F32),
        second_sum=vmem((tokens, width), F32),
        mixed=vmem(wide, BF16), grad_gate=vmem(wide, BF16), grad_step_low=vmem(wide, BF16),
        grad_act=vmem(wide, F32), grad_proj=vmem((proj, rows), BF16),
        grad_conv=vmem((seqs, tokens + HALO, width), F32), rim_own=vmem((seqs, HALO, width), BF16),
        rim=vmem((seqs, HALO, width), BF16), rim_sems=dma((2 * seqs,)),
        grad_inner=vmem(wide, BF16),
        out_blocks=vmem((4, rows, shard), BF16), out_first=vmem((2, rows, shard), BF16),
        out_second=vmem((rows, shard), BF16), out_sems=dma((6,)),
        gn_blocks=vmem((4, rows, shard), BF16), gn_first=vmem((2, rows, shard), BF16),
        gn_second=vmem((rows, shard), BF16), gn_sems=dma((10,)),
        moment=vmem((8, rows), F32), moment_first=vmem((8, rows), F32),
        moment_mid=vmem((8, rows), F32), moment_second=vmem((8, rows), F32),
        early=vmem((early_rows, width), F32), later=vmem((later_rows, width), F32),
        gain_sums=vmem((seq_devices, 8, shard), F32), gain_sums_send=dma((seq_devices,)),
        gain_sums_recv=dma((seq_devices,)),
    )
    if gathered:
        every = (seq_devices * rows, width)
        ring_steps = seq_devices // 2
        scratch.update(
            gate_act_all=vmem(every, BF16), gate_slope_all=vmem(every, BF16),
            skip_all=vmem((seq_devices, seqs, tokens, width), BF16),
            inner_all=vmem((seq_devices, seqs, tokens, width), BF16),
            xo_ring_sems=dma((2, ring_steps, 2)), xo_chan_sems=dma((seq_devices - 1, 6)),
            skip_sems=dma((seqs, 2, ring_steps, 2)), inner_sems=dma((seqs, 2, ring_steps, 2)),
            small_own=vmem((2 * low_rank, width + width // 2), BF16),
            small_land=vmem((seq_devices, 2 * low_rank // seq_devices, width + width // 2), BF16),
            small_sems=dma((4, seq_devices)), result_sems=dma((5,)),
        )
    else:
        late = (model + early_rows + later_rows, width)
        scratch.update(
            cot=vmem((rows, model), BF16),
            grad_w_out=vmem(w_out.shape, BF16), land_w_out=vmem(w_out.shape, BF16), w_out_sems=dma((steps,)),
            grad_w_gate=vmem((model, width), BF16), land_w_gate=vmem((model, width), BF16),
            w_gate_sems=dma((steps,)),
            grad_w_inner=vmem(late, BF16), land_w_inner=vmem(late, BF16), full_w_inner=vmem(late, BF16),
            w_inner_sems=dma((steps,)),
        )
    names = list(operands) + list(outputs) + list(scratch)
    spaces = dict(lengths=pltpu.SMEM, w_in=pl.ANY, w_out=pl.ANY)
    mixed_out, grad_inputs, gain, w_in_grad, w_out_grad, small = pl.pallas_call(
        partial(layer_kernel, names, seq_devices),
        out_shape=tuple(jax.ShapeDtypeStruct(*item) for item in outputs.values()),
        in_specs=[pl.BlockSpec(memory_space=spaces.get(name, pltpu.VMEM)) for name in operands],
        out_specs=tuple(
            pl.BlockSpec(memory_space=pl.ANY if gathered and name in ("out_w_in", "out_w_out") else pltpu.VMEM)
            for name in outputs
        ),
        scratch_shapes=list(scratch.values()),
        compiler_params=pltpu.CompilerParams(
            collective_id=0, has_side_effects=True, vmem_limit_bytes=VMEM_LIMIT
        ),
    )(*operands.values())
    parts = 4

    def cut(shape, axis):
        block = tuple(size // parts if k == axis else size for k, size in enumerate(shape))
        return pl.BlockSpec(block, lambda i: tuple(i if k == axis else 0 for k in range(len(shape))))

    def kept(shape):
        return pl.BlockSpec(shape, lambda i: (0,) * len(shape))

    def result(shape, spec, dtype=F32):
        return jax.ShapeDtypeStruct(shape, dtype), spec

    tokens_cut = cut(inputs.shape, 1)
    w_in_cut, w_out_cut = (cut(w_in.shape, 1), cut(w_out.shape, 0))
    wide_row = ((1, width), kept((1, width)))
    results = [
        result(inputs.shape, tokens_cut, BF16), result(inputs.shape, tokens_cut, BF16),
        result((1, shard), kept((1, shard))), result(w_in.shape, w_in_cut),
        result(conv_weight.shape, kept(conv_weight.shape)), result(*wide_row),
        result(x_weight.shape, kept(x_weight.shape)), result(dt_weight.shape, kept(dt_weight.shape)),
        result(*wide_row), result(log_decay.shape, kept(log_decay.shape)), result(*wide_row),
        result(w_out.shape, w_out_cut),
    ]
    out = pl.pallas_call(
        partial(finish_kernel, (proj, low_rank, states, taps)),
        grid=(parts,),
        out_shape=tuple(item[0] for item in results),
        in_specs=[tokens_cut, tokens_cut, w_in_cut, w_out_cut, kept(small.shape), kept(gain.shape)],
        out_specs=tuple(item[1] for item in results),
        compiler_params=pltpu.CompilerParams(vmem_limit_bytes=VMEM_LIMIT),
    )(mixed_out, grad_inputs, w_in_grad, w_out_grad, small, gain)
    flat = (2, 5, 8, 10)
    return tuple(value.reshape(-1) if k in flat else value for k, value in enumerate(out))


def solution(mesh):
    in_specs = (
        P(None, "seq", "chan"), P(), P(None, "seq", "chan"), P("chan"), P(None, None, "chan"),
        P(None, "chan"), P("chan"), P(None, "chan"), P(None, "chan"), P("chan"), P(None, "chan"),
        P("chan"), P("chan", None),
    )
    out_specs = (
        P(None, "seq", "chan"), P(None, "seq", "chan"), P("chan"), P(None, None, "chan"),
        P(None, "chan"), P("chan"), P(None, "chan"), P(None, "chan"), P("chan"), P(None, "chan"),
        P("chan"), P("chan", None),
    )
    body = partial(layer, mesh.shape["seq"])
    return jax.shard_map(body, mesh=mesh, in_specs=in_specs, out_specs=out_specs, check_vma=False)
```

```python
from functools import partial
from types import SimpleNamespace

import jax
import jax.numpy as jnp
from jax import lax
from jax.experimental import pallas as pl
from jax.experimental.pallas import tpu as pltpu
from jax.sharding import PartitionSpec as P

EPSILON = 1e-05
LANES = 128
LOG2E = 1.4426950408889634
ROWS, RELAY, SKIP, INNER, SMALL, OTHERS = range(6)
SCHEDULE = {
    1: ((ROWS, 0),),
    3: ((ROWS, 0), (RELAY, 2),),
    5: ((ROWS, 0),),
    6: ((SKIP, 0),),
    8: ((SKIP, 1),),
    9: ((SKIP, 0),),
    10: ((SKIP, 1),),
    12: ((SKIP, 0), (ROWS, 0), (RELAY, 4),),
    13: ((OTHERS, 1),),
    14: ((SKIP, 1),),
    16: ((INNER, 0),),
    17: ((SKIP, 0), (INNER, 1),),
    18: ((SKIP, 1), (RELAY, 6), (OTHERS, 2), (INNER, 0),),
    19: ((INNER, 1), (RELAY, 7), (OTHERS, 3), (INNER, 0), (SMALL, 0), (OTHERS, 4), (INNER, 1),),
    24: ((INNER, 0),),
}
VMEM_LIMIT = 60 * 2**20
HALO = 16
MOST_GATHERED = 8
MESH = pl.DeviceIdType.MESH
F32 = jnp.float32
BF16 = jnp.bfloat16


def lane_chunks(width):
    return [slice(k * LANES, (k + 1) * LANES) for k in range(width // LANES)]


def flip(index, bit):
    return index + bit - 2 * bit * lax.rem(lax.div(index, bit), 2)


def dot(a, b, contract=((1,), (0,))):
    return lax.dot_general(a, b, (contract, ((), ())), preferred_element_type=F32)


def silu_slope(values, sigmoid):
    return sigmoid * (1.0 + values * (1.0 - sigmoid))


def softplus(values):
    return jnp.maximum(values, 0.0) + jnp.log1p(jnp.exp(-jnp.abs(values)))


def spread_maps(maps, b_ref, c_ref, first, tokens):
    states = maps.shape[0] // 2

    def block(index, _):
        start = index * 8
        rolled = pltpu.roll(maps, lax.rem(tokens - start, tokens), 1)
        for j in range(8):
            column = jnp.broadcast_to(rolled[:, j : j + 1], (2 * states, LANES))
            b_ref[first + start + j] = column[:states]
            c_ref[first + start + j] = column[states:]
        return 0

    lax.fori_loop(0, tokens // 8, block, 0)


def zero_states(rate_ref):
    states, width = rate_ref.shape
    return tuple(jnp.zeros((states, LANES), F32) for _ in lane_chunks(width))


def local_states(decay_ref, step_ref, drive_ref, b_ref, rate_ref, first, tokens):
    chunks = lane_chunks(rate_ref.shape[1])

    def block(index, held):
        held = list(held)
        rows = pl.ds(pl.multiple_of(first + index * 8, 8), 8)
        steps = [step_ref[rows, lanes] for lanes in chunks]
        drives = [drive_ref[rows, lanes] for lanes in chunks]
        for j in range(8):
            token = first + index * 8 + j
            b = b_ref[token]
            for k, lanes in enumerate(chunks):
                decay = jnp.exp2(steps[k][j : j + 1] * rate_ref[:, lanes])
                decay_ref[token, :, lanes] = decay
                held[k] = decay * held[k] + drives[k][j : j + 1] * b
        return tuple(held)

    return lax.fori_loop(0, tokens // 8, block, zero_states(rate_ref))


def local_adjoints(decay_ref, up_ref, c_ref, rate_ref, first, tokens):
    chunks = lane_chunks(rate_ref.shape[1])

    def block(index, held):
        held = list(held)
        start = first + (tokens // 8 - 1 - index) * 8
        rows = pl.ds(pl.multiple_of(start, 8), 8)
        ups = [up_ref[rows, lanes] for lanes in chunks]
        for j in range(7, -1, -1):
            token = start + j
            c = c_ref[token]
            for k, lanes in enumerate(chunks):
                adjoint = c * ups[k][j : j + 1] + held[k]
                held[k] = decay_ref[token, :, lanes] * adjoint
        return tuple(held)

    return lax.fori_loop(0, tokens // 8, block, zero_states(rate_ref))


def run_states(decay_ref, drive_ref, b_ref, c_ref, enter_ref, state_ref, out_ref, which, first, tokens):
    chunks = lane_chunks(decay_ref.shape[2])

    def block(index, held):
        held = list(held)
        rows = pl.ds(pl.multiple_of(first + index * 8, 8), 8)
        drives = [drive_ref[rows, lanes] for lanes in chunks]
        outs = [[] for _ in chunks]
        for j in range(8):
            token = first + index * 8 + j
            b, c = b_ref[token], c_ref[token]
            for k, lanes in enumerate(chunks):
                held[k] = decay_ref[token, :, lanes] * held[k] + drives[k][j : j + 1] * b
                state_ref[token, :, lanes] = held[k].astype(BF16)
                outs[k].append(jnp.sum(c * held[k], axis=0, keepdims=True))
        for k, lanes in enumerate(chunks):
            out_ref[pl.ds(pl.multiple_of(index * 8, 8), 8), lanes] = jnp.concatenate(outs[k], axis=0)
        return tuple(held)

    lax.fori_loop(0, tokens // 8, block, tuple(enter_ref[which, :, lanes] for lanes in chunks))


def run_adjoints(
    decay_ref, step_ref, up_ref, b_ref, c_ref, rate_ref, enter_ref, state_ref, adjoint_ref,
    first_sum_ref, second_sum_ref, which, first, tokens, span, carried,
):
    chunks = lane_chunks(rate_ref.shape[1])

    def block(index, carried):
        held, total = list(carried[0]), list(carried[1])
        ones = [[None] * 8 for _ in chunks]
        twos = [[None] * 8 for _ in chunks]
        start = first + (tokens // 8 - 1 - index) * 8
        rows = pl.ds(pl.multiple_of(start, 8), 8)
        ups = [up_ref[rows, lanes] for lanes in chunks]
        steps = [step_ref[rows, lanes] for lanes in chunks]
        for j in range(7, -1, -1):
            token = start + j
            b, c = b_ref[token], c_ref[token]
            for k, lanes in enumerate(chunks):
                adjoint = c * ups[k][j : j + 1] + held[k]
                adjoint_ref[token - first, :, lanes] = adjoint.astype(BF16)
                held[k] = decay_ref[token, :, lanes] * adjoint
                if j > 0:
                    before = state_ref[token - 1, :, lanes].astype(F32)
                else:
                    before = state_ref[jnp.maximum(token - 1, first), :, lanes].astype(F32)
                    before = jnp.where(token == first, enter_ref[which, :, lanes], before)
                pulled = held[k] * before
                ones[k][j] = jnp.sum(pulled * rate_ref[:, lanes], axis=0, keepdims=True)
                twos[k][j] = jnp.sum(adjoint * b, axis=0, keepdims=True)
                total[k] = total[k] + pulled * steps[k][j : j + 1]
        own_rows = pl.ds(pl.multiple_of(start - first, 8), 8)
        for k, lanes in enumerate(chunks):
            first_sum_ref[own_rows, lanes] = jnp.concatenate(ones[k], axis=0)
            second_sum_ref[own_rows, lanes] = jnp.concatenate(twos[k], axis=0)
        return tuple(held), tuple(total)

    return lax.fori_loop(span[0], span[1], block, carried)


def map_sums(values_ref, rows, states, first, tokens):
    width = rows.shape[1]
    flat = values_ref[first : first + tokens].reshape(tokens * states, width)
    all_pairs = dot(flat, rows.astype(BF16), ((1,), (1,)))
    row_token = lax.broadcasted_iota(jnp.int32, (tokens * states, tokens), 0) // states
    column_token = lax.broadcasted_iota(jnp.int32, (tokens * states, tokens), 1)
    kept = jnp.where(row_token == column_token, all_pairs, 0.0).astype(BF16)
    state = lax.broadcasted_iota(jnp.int32, (states, tokens * states), 0)
    row_state = lax.broadcasted_iota(jnp.int32, (states, tokens * states), 1) % states
    return dot((state == row_state).astype(BF16), kept)


def send(src, dst, send_sem, recv_sem, device):
    copy = pltpu.make_async_remote_copy(
        src_ref=src, dst_ref=dst, send_sem=send_sem, recv_sem=recv_sem,
        device_id=device, device_id_type=MESH,
    )
    copy.start()
    return copy


class ChanGather:
    def __init__(self, src, place, sems, mine, core_peer, x_peer):
        self.place, self.sems, self.mine, self.core_peer = (place, sems, mine, core_peer)
        self.over_x = send(src, place(mine), sems.at[0], sems.at[1], x_peer)
        self.over_core = send(src, place(mine), sems.at[2], sems.at[3], core_peer)

    def relay(self):
        self.over_x.wait_recv()
        block = self.place(flip(self.mine, 2))
        self.onward = send(block, block, self.sems.at[4], self.sems.at[5], self.core_peer)

    def finish(self):
        self.over_core.wait_recv()
        self.onward.wait_recv()
        for copy in (self.over_x, self.over_core, self.onward):
            copy.wait_send()


def ring_position(index, count):
    return lax.div(index, 2) + lax.rem(index, 2) * (count - 1 - 2 * lax.div(index, 2))


def ring_device(position, count):
    position = lax.rem(position + 2 * count, count)
    back = lax.div(position, count // 2)
    return 2 * position + back * (2 * (count - 1 - position) + 1 - 2 * position)


class RingGather:
    def __init__(self, place, sems, count, mine, chan, more_left):
        self.place, self.sems, self.count, self.chan = (place, sems, count, chan)
        self.position = ring_position(mine, count)
        most = count // 2
        self.steps = (most, count - 1 - most) if more_left else (count - 1 - most, most)
        self.length = most
        self.copies = []
        self.step = 0
        self.launch()

    def source(self, side, step):
        return ring_device(self.position + (step if side else -step), self.count)

    def launch(self):
        for side in range(2):
            if self.step < self.steps[side]:
                block = self.place(self.source(side, self.step))
                towards = ring_device(self.position + (-1 if side else 1), self.count)
                sems = self.sems.at[side, self.step]
                self.copies.append(send(block, block, sems.at[0], sems.at[1], (towards, self.chan)))

    def advance(self):
        if self.step == self.length:
            return []
        arrived = []
        for side in range(2):
            if self.step < self.steps[side]:
                source = self.source(side, self.step + 1)
                block = self.place(source)
                sems = self.sems.at[side, self.step]
                pltpu.make_async_remote_copy(
                    src_ref=block, dst_ref=block, send_sem=sems.at[0], recv_sem=sems.at[1],
                    device_id=(source, self.chan), device_id_type=MESH,
                ).wait_recv()
                arrived.append(source)
        self.step += 1
        self.launch()
        return arrived

    def finish(self):
        while self.step < self.length:
            self.advance()
        for copy in self.copies:
            copy.wait_send()


class GridGather:
    def __init__(self, place, ring_sems, chan_sems, count, me_s, me_c, core_peer, x_peer):
        self.place, self.mine, self.sems = (place, me_c, chan_sems)
        self.peers = (core_peer, x_peer)
        self.ring = RingGather(lambda d: place(me_c, d), ring_sems, count, me_s, me_c, True)
        self.gathers = []
        self.relayed = 0

    def advance(self):
        for source in self.ring.advance():
            self.gathers.append(
                ChanGather(
                    self.place(self.mine, source), partial(self.at, source), self.sems.at[len(self.gathers)],
                    self.mine, *self.peers,
                )
            )

    def at(self, source, chan):
        return self.place(chan, source)

    def relay(self, upto):
        while self.relayed < min(upto, len(self.gathers)):
            self.gathers[self.relayed].relay()
            self.relayed += 1

    def finish(self, step):
        for gather in self.gathers[2 * step - 2 : 2 * step]:
            gather.finish()


class ChanSum:
    def __init__(self, own, first, second, middle, sems, core_peer, x_peer):
        self.own, self.first, self.second, self.middle = (own, first, second, middle)
        self.sems, self.x_peer = (sems, x_peer)
        self.copies = [send(own, first, sems.at[0], sems.at[1], core_peer)]

    def cross(self):
        self.copies[0].wait_recv()
        self.middle[...] = (self.own[...].astype(F32) + self.first[...].astype(F32)).astype(BF16)
        self.copies.append(send(self.middle, self.second, self.sems.at[2], self.sems.at[3], self.x_peer))

    def finish(self):
        self.copies[1].wait_recv()
        for copy in self.copies:
            copy.wait_send()
        return self.middle[...].astype(F32) + self.second[...].astype(F32)


class ChanScatter:
    def __init__(self, blocks, first, second, sems, mine, core_peer, x_peer, extra=None):
        self.blocks, self.first, self.second, self.sems = (blocks, first, second, sems)
        self.mine, self.x_peer, self.extra = (mine, x_peer, extra)
        other = flip(mine, 1)
        self.copies = [
            send(blocks.at[other], first.at[0], sems.at[0], sems.at[1], core_peer),
            send(blocks.at[flip(other, 2)], first.at[1], sems.at[2], sems.at[3], core_peer),
        ]
        if extra is not None:
            self.copies.append(send(extra[0], extra[1], sems.at[6], sems.at[7], core_peer))

    def cross(self):
        for copy in self.copies:
            copy.wait_recv()
        far = flip(self.mine, 2)
        self.blocks[far] = (self.blocks[far].astype(F32) + self.first[1].astype(F32)).astype(BF16)
        self.last = [send(self.blocks.at[far], self.second, self.sems.at[4], self.sems.at[5], self.x_peer)]
        if self.extra is not None:
            own, near, middle, across = self.extra
            middle[...] = own[...] + near[...]
            self.last.append(send(middle, across, self.sems.at[8], self.sems.at[9], self.x_peer))

    def finish(self):
        for copy in self.last:
            copy.wait_recv()
        for copy in self.copies + self.last:
            copy.wait_send()
        total = self.blocks[self.mine].astype(F32) + self.first[0].astype(F32) + self.second[...].astype(F32)
        if self.extra is None:
            return total
        return total, self.extra[2][...] + self.extra[3][...]


class SeqSum:
    def __init__(self, held, landing, full, sems, bits, mine, chan):
        self.held, self.landing, self.full, self.sems, self.bits = (held, landing, full, sems, bits)
        self.mine, self.chan = (mine, chan)
        self.regions = []
        self.copies = []
        start, size, place = (0, held.shape[0], 0)
        for bit in bits:
            half = size // 2
            mine_bit = lax.rem(lax.div(mine, bit), 2)
            keep = pl.multiple_of(start + mine_bit * half, 16)
            give = pl.multiple_of(start + (1 - mine_bit) * half, 16)
            self.regions.append((keep, give, half, place))
            start, size, place = (keep, half, place + half)
        self.step = 0
        self.total = 2 * len(bits)
        self.launch()

    def launch(self):
        step, count = (self.step, len(self.bits))
        sems = (self.sems.at[2 * step], self.sems.at[2 * step + 1])
        if step < count:
            _, give, half, place = self.regions[step]
            src, dst = (self.held.at[pl.ds(give, half)], self.landing.at[pl.ds(place, half)])
            bit = self.bits[step]
        else:
            keep, _, half, _ = self.regions[self.total - 1 - step]
            src = dst = self.full.at[pl.ds(keep, half)]
            bit = self.bits[self.total - 1 - step]
        self.copies.append(send(src, dst, *sems, (flip(self.mine, bit), self.chan)))

    def advance(self):
        if self.step == self.total:
            return
        self.copies[-1].wait_recv()
        if self.step < len(self.bits):
            keep, _, half, place = self.regions[self.step]
            rows = pl.ds(keep, half)
            got = self.landing[pl.ds(place, half)].astype(F32)
            into = self.held if self.step < len(self.bits) - 1 else self.full
            into[rows] = (self.held[rows].astype(F32) + got).astype(BF16)
        self.step += 1
        if self.step < self.total:
            self.launch()

    def finish(self):
        while self.step < self.total:
            self.advance()
        for copy in self.copies:
            copy.wait_send()


class DirectSum:
    def __init__(self, own, landing, full, sems, count, mine, chan):
        self.own, self.landing, self.full, self.sems = (own, landing, full, sems)
        self.count, self.mine, self.chan = (count, mine, chan)
        self.rows = own.shape[0] // count
        self.each(lambda k, peer: self.apart(peer, self.mine, peer).start())

    def piece(self, ref, device):
        return ref.at[pl.ds(pl.multiple_of(device * self.rows, self.rows), self.rows)]

    def each(self, act):
        def turn(k, _):
            act(k, lax.rem(self.mine + k, self.count))
            return 0

        lax.fori_loop(1, self.count, turn, 0)

    def apart(self, piece, source, peer):
        return pltpu.make_async_remote_copy(
            src_ref=self.piece(self.own, piece), dst_ref=self.landing.at[source],
            send_sem=self.sems.at[0, peer], recv_sem=self.sems.at[1, source],
            device_id=(peer, self.chan), device_id_type=MESH,
        )

    def back(self, source, peer):
        return pltpu.make_async_remote_copy(
            src_ref=self.piece(self.full, source), dst_ref=self.piece(self.full, source),
            send_sem=self.sems.at[2, peer], recv_sem=self.sems.at[3, source],
            device_id=(peer, self.chan), device_id_type=MESH,
        )

    def cross(self):
        self.each(lambda k, peer: self.apart(peer, peer, peer).wait_recv())
        mine = pl.ds(pl.multiple_of(self.mine * self.rows, self.rows), self.rows)

        def add(k, total):
            return total + self.landing[lax.rem(self.mine + k, self.count)].astype(F32)

        total = lax.fori_loop(1, self.count, add, self.own[mine].astype(F32))
        self.full[mine] = total.astype(BF16)
        self.each(lambda k, peer: self.back(self.mine, peer).start())

    def finish(self):
        self.each(lambda k, peer: self.back(peer, peer).wait_recv())
        self.each(lambda k, peer: self.apart(peer, self.mine, peer).wait_send())
        self.each(lambda k, peer: self.back(self.mine, peer).wait_send())


def pack_small(early, later, low_rank, proj):
    half = early.shape[1] // 2
    rest = [early[low_rank:], later[proj:]]
    spare = 2 * low_rank - proj - sum(part.shape[0] for part in rest)
    rest.append(jnp.zeros((spare, early.shape[1]), early.dtype))
    left = jnp.concatenate([later[:proj]] + rest, axis=0)
    right = jnp.concatenate([early[:low_rank, :half], early[:low_rank, half:]], axis=0)
    return jnp.concatenate([left, right], axis=1)


def layer_kernel(names, seq_devices, *refs):
    r = SimpleNamespace(**dict(zip(names, refs)))
    x_ref, og_ref, win_ref, wout_ref = (r.inputs, r.out_grad, r.w_in_here, r.w_out_here)
    xw_ref, dtw_ref = (r.x_weight, r.dt_weight)
    seqs, tokens, shard = x_ref.shape
    model, width = win_ref.shape[1:]
    states = r.log_decay.shape[0]
    low_rank = dtw_ref.shape[0]
    taps = r.conv_weight.shape[0]
    proj = xw_ref.shape[0]
    me_s, me_c = (lax.axis_index("seq"), lax.axis_index("chan"))
    core_peer, x_peer = ((me_s, flip(me_c, 1)), (me_s, flip(me_c, 2)))
    right, left = (lax.rem(me_s + 1, seq_devices), lax.rem(me_s + seq_devices - 1, seq_devices))
    position = ring_position(me_s, seq_devices)
    gathered = seq_devices <= MOST_GATHERED
    spot = me_s if gathered else 0

    loads = []
    for k, (src, dst) in enumerate(((r.w_in, r.w_in_here), (r.w_out, r.w_out_here))):
        loads.append(pltpu.make_async_copy(src, dst, r.load_sems.at[k]))
        loads[k].start()

    barrier = pltpu.get_barrier_semaphore()

    def greet(semaphore, device):
        pl.semaphore_signal(semaphore, inc=1, device_id=device, device_id_type=MESH)

    ring = [(ring_device(position + step, seq_devices), me_c) for step in (1, -1)]
    first_peers = [core_peer, x_peer, (right, me_c), (left, me_c)] + ring
    for device in first_peers:
        greet(barrier, device)
    pl.semaphore_wait(barrier, len(first_peers))

    xo_ref, halo_ref = (r.xo, r.halo)
    gather_x = [
        ChanGather(
            x_ref.at[s], partial(lambda s, q: xo_ref.at[q, spot, 0, s], s), r.x_sems.at[s], me_c, core_peer, x_peer
        )
        for s in range(seqs)
    ]
    halo_copy = send(
        x_ref.at[:, pl.ds(tokens - HALO, HALO), :], halo_ref.at[me_c, pl.ds(0, seqs)],
        r.halo_sems.at[6], r.halo_sems.at[7], (right, me_c),
    )
    for device in ring:
        greet(r.known.at[0], device)
    gather_og = ChanGather(og_ref, lambda q: xo_ref.at[q, spot, 1], r.og_sems, me_c, core_peer, x_peer)
    xo_ref[me_c, spot, 0] = x_ref[...]
    xo_ref[me_c, spot, 1] = og_ref[...]
    halo_ref[me_c, seqs] = jnp.broadcast_to(r.norm_gain[...].astype(F32).reshape(1, shard), (HALO, shard)).astype(BF16)
    if gathered:
        gather_all = GridGather(
            lambda q, d: xo_ref.at[q, d], r.xo_ring_sems, r.xo_chan_sems, seq_devices, me_s, me_c, core_peer, x_peer
        )
    skip_gathers, inner_gathers, small_sums, sums = ([], [], [], [])

    def hook(place):
        if not gathered:
            if place > 6:
                for item in sums:
                    item.advance()
            return
        for kind, which in SCHEDULE.get(place, ()):
            if kind == ROWS:
                gather_all.advance()
            elif kind == RELAY:
                gather_all.relay(which)
            elif kind == SKIP:
                skip_gathers[which].advance()
            elif kind == INNER:
                inner_gathers[which].advance()
            elif kind == SMALL:
                small_sums[0].cross()
            else:
                foreign_pair(which)

    halo_copy.wait_recv()
    gather_halo = ChanGather(
        halo_ref.at[me_c], lambda q: halo_ref.at[q], r.halo_sems, me_c, core_peer, x_peer
    )
    for s in range(seqs):
        gather_x[s].relay()
    gather_halo.relay()
    gather_x[0].finish()
    gather_halo.finish()
    halo_copy.wait_send()

    reaches = [1]
    while 2 * reaches[-1] < seq_devices // 2:
        reaches.append(2 * reaches[-1])

    def hear(k):
        pl.semaphore_wait(r.known.at[k], 2)
        if k + 1 < len(reaches):
            for step in (reaches[k + 1], -reaches[k + 1]):
                greet(r.known.at[k + 1], (ring_device(position + step, seq_devices), me_c))

    rate_ref, rate2_ref = (r.rate, r.rate2)
    rate_ref[...] = -jnp.exp(r.log_decay[...])
    rate2_ref[...] = rate_ref[...] * LOG2E

    def mask_of(s, rows, begin):
        positions = me_s * tokens + begin + lax.broadcasted_iota(jnp.int32, (rows, 1), 0)
        return (positions < r.lengths[s]).astype(F32)

    def gain_of(q):
        return halo_ref[q, seqs, 0:1, :].astype(F32)

    def normalize(blocks):
        squares = sum(jnp.sum(b * b, axis=1, keepdims=True) for b in blocks)
        root = lax.rsqrt(squares * (1.0 / model) + EPSILON)
        return root, [(b * root * gain_of(q)).astype(BF16) for q, b in enumerate(blocks)]

    hear(0)
    loads[0].wait()

    conv_sum = []
    normed_rows = []
    has_left = (me_s > 0).astype(F32)
    for s in range(seqs):
        mine = pl.ds(s * tokens, tokens)
        if s > 0:
            gather_x[s].finish()
        root, rows = normalize([xo_ref[q, spot, 0, s].astype(F32) for q in range(4)])
        _, before = normalize([halo_ref[q, s].astype(F32) for q in range(4)])
        r.root[mine, :] = jnp.broadcast_to(root, (tokens, LANES))
        normed, normed_before = (jnp.concatenate(rows, axis=1), jnp.concatenate(before, axis=1))
        normed_rows.append(pl.ds(pl.multiple_of(spot * seqs * tokens + s * tokens, tokens), tokens))
        r.normed[normed_rows[s], :] = normed
        inner = dot(normed, win_ref[0]).astype(BF16).astype(F32) * mask_of(s, tokens, 0)
        inner_before = dot(normed_before, win_ref[0]).astype(BF16).astype(F32)
        inner_before = inner_before * (mask_of(s, HALO, -HALO) * has_left)
        r.inner[s, HALO:, :] = inner
        r.inner[s, :HALO, :] = inner_before
        conv_pre = r.conv_bias[...] + sum(
            r.conv_weight[k : k + 1, :] * r.inner[s, HALO - taps + 1 + k : HALO - taps + 1 + k + tokens, :]
            for k in range(taps)
        )
        r.conv_pre[mine, :] = conv_pre
        act = (conv_pre * jax.nn.sigmoid(conv_pre)).astype(BF16)
        r.act[mine, :] = act.astype(F32)
        r.proj_own[s] = dot(xw_ref[...], act, ((1,), (1,))).astype(BF16)
        conv_sum.append(
            ChanSum(
                r.proj_own.at[s], r.proj_first.at[s], r.proj_second.at[s], r.proj_mid.at[s],
                r.proj_sems.at[s], core_peer, x_peer,
            )
        )
    gather_og.relay()
    for s in range(seqs):
        conv_sum[s].cross()
    hook(0)
    for s in range(seqs):
        mine = pl.ds(s * tokens, tokens)
        r.gate_pre[mine, :] = dot(r.normed[normed_rows[s], :], win_ref[1])
    gather_og.finish()
    loads[1].wait()
    for s in range(seqs):
        mine = pl.ds(s * tokens, tokens)
        cot = jnp.concatenate([xo_ref[q, spot, 1, s] for q in range(4)], axis=1)
        grad_mixed = dot(cot, wout_ref[...], ((1,), (1,))) * mask_of(s, tokens, 0)
        gate = r.gate_pre[mine, :]
        sigmoid = jax.nn.sigmoid(gate)
        r.grad_mixed[mine, :] = grad_mixed
        r.up[mine, :] = grad_mixed * (gate * sigmoid)
        if gathered:
            rows = normed_rows[s]
            r.gate_act_all[rows, :] = (gate * sigmoid * mask_of(s, tokens, 0)).astype(BF16)
            r.gate_slope_all[rows, :] = (grad_mixed * silu_slope(gate, sigmoid)).astype(BF16)
        else:
            r.cot[mine, :] = (cot.astype(F32) * mask_of(s, tokens, 0)).astype(BF16)
    hook(1)

    totals_ref = r.totals
    step_totals = []
    for s in range(seqs):
        mine = pl.ds(s * tokens, tokens)
        projected = conv_sum[s].finish()
        low = projected[:low_rank].astype(BF16)
        r.low[:, s * tokens : (s + 1) * tokens] = low
        step_pre = dot(projected[:low_rank].T.astype(BF16), dtw_ref[...]) + r.dt_bias[...]
        r.step_pre[mine, :] = step_pre
        step = softplus(step_pre)
        r.step[mine, :] = step
        r.drive[mine, :] = step * r.act[mine, :]
        step_totals.append(jnp.sum(step, axis=0, keepdims=True))
        spread_maps(projected[low_rank:], r.b, r.c, s * tokens, tokens)
    hook(2)
    totals_ref[me_s] = jnp.concatenate(step_totals + [jnp.zeros((8 - seqs, width), F32)], axis=0)

    def seq_device(k):
        return (k, me_c)

    def totals_copy(k):
        peer = lax.rem(me_s + k, seq_devices)
        return pltpu.make_async_remote_copy(
            src_ref=totals_ref.at[me_s], dst_ref=totals_ref.at[me_s],
            send_sem=r.totals_send.at[k], recv_sem=r.totals_recv.at[me_s],
            device_id=seq_device(peer), device_id_type=MESH,
        )

    def start_totals(k, _):
        totals_copy(k).start()
        return 0

    for k in range(1, len(reaches)):
        hear(k)
    lax.fori_loop(1, seq_devices, start_totals, 0)

    ends_refs = (r.ends, r.ends_send, r.ends_recv)
    leaves_refs = (r.leaves, r.leaves_send, r.leaves_recv)

    def carried_copy(which, s, peer):
        ref, send_sem, recv_sem = which
        return pltpu.make_async_remote_copy(
            src_ref=ref.at[s, me_s], dst_ref=ref.at[s, me_s],
            send_sem=send_sem.at[s, peer], recv_sem=recv_sem.at[s, me_s],
            device_id=seq_device(peer), device_id_type=MESH,
        )

    def start_carried(which, s, begin, end):
        def start(peer, _):
            carried_copy(which, s, peer).start()
            return 0

        lax.fori_loop(begin, end, start, 0)

    def wait_carried(which, s, begin, end):
        def wait(peer, _):
            carried_copy(which, s, peer).wait_send()
            return 0

        lax.fori_loop(begin, end, wait, 0)

    for s in range(seqs):
        ends = local_states(r.decay, r.step, r.drive, r.b, rate2_ref, s * tokens, tokens)
        for k, lanes in enumerate(lane_chunks(width)):
            r.ends[s, me_s, :, lanes] = ends[k].astype(BF16)
        start_carried(ends_refs, s, me_s + 1, seq_devices)
    hook(3)
    for s in range(seqs):
        leaves = local_adjoints(r.decay, r.up, r.c, rate_ref, s * tokens, tokens)
        for k, lanes in enumerate(lane_chunks(width)):
            r.leaves[s, me_s, :, lanes] = leaves[k].astype(BF16)
        start_carried(leaves_refs, s, 0, me_s)

    hook(4)

    def wait_totals(k, _):
        peer = lax.rem(me_s + k, seq_devices)
        pltpu.make_async_remote_copy(
            src_ref=totals_ref.at[peer], dst_ref=totals_ref.at[peer],
            send_sem=r.totals_send.at[k], recv_sem=r.totals_recv.at[peer],
            device_id=seq_device(peer), device_id_type=MESH,
        ).wait_recv()
        return 0

    lax.fori_loop(1, seq_devices, wait_totals, 0)

    def combine(which, s, count, place):
        ref, send_sem, recv_sem = which

        def turn(k, held):
            peer = place(k)
            pltpu.make_async_remote_copy(
                src_ref=ref.at[s, peer], dst_ref=ref.at[s, peer],
                send_sem=send_sem.at[s, peer], recv_sem=recv_sem.at[s, peer],
                device_id=seq_device(peer), device_id_type=MESH,
            ).wait_recv()
            total = totals_ref[peer][s : s + 1]
            return jnp.exp2(total * rate2_ref[...]) * held + ref[s, peer].astype(F32)

        return lax.fori_loop(0, count, turn, jnp.zeros((states, width), F32))

    def block_of(ref, s, device):
        return ref.at[device, s]

    def foreign_pair(step):
        gather_all.finish(step)
        last = 2 * step == seq_devices
        lax.fori_loop(0, 1 if last else 2, partial(foreign, step), 0)

    def foreign(step, side, _):
        device = ring_device(position + step - 2 * step * side, seq_devices)
        rows = pl.ds(pl.multiple_of(device * (seqs * tokens), seqs * tokens), seqs * tokens)
        blocks = [xo_ref[q, device, 0].reshape(seqs * tokens, shard).astype(F32) for q in range(4)]
        normed = jnp.concatenate(normalize(blocks)[1], axis=1)
        r.normed[rows, :] = normed
        gate = dot(normed, win_ref[1])
        sigmoid = jax.nn.sigmoid(gate)
        cot = jnp.concatenate([xo_ref[q, device, 1].reshape(seqs * tokens, shard) for q in range(4)], axis=1)
        mask = jnp.concatenate([mask_of(s, tokens, (device - me_s) * tokens) for s in range(seqs)], axis=0)
        grad_mixed = dot(cot, wout_ref[...], ((1,), (1,))) * mask
        r.gate_act_all[rows, :] = (gate * sigmoid * mask).astype(BF16)
        r.gate_slope_all[rows, :] = (grad_mixed * silu_slope(gate, sigmoid)).astype(BF16)
        return 0

    for s in range(seqs):
        mine = pl.ds(s * tokens, tokens)
        r.entering[s] = combine(ends_refs, s, me_s, lambda k: k)
        run_states(
            r.decay, r.drive, r.b, r.c, r.entering, r.state, r.scanned, s, s * tokens, tokens
        )
        gate = r.gate_pre[mine, :]
        sigmoid = jax.nn.sigmoid(gate)
        with_skip = r.scanned[...] + r.skip_gain[...] * r.act[mine, :]
        mixed = (with_skip * (gate * sigmoid)).astype(BF16)
        r.mixed[mine, :] = mixed
        r.grad_gate[mine, :] = (r.grad_mixed[mine, :] * with_skip * silu_slope(gate, sigmoid)).astype(BF16)
        if gathered:
            r.skip_all[me_s, s] = with_skip.astype(BF16)
            skip_gathers.append(
                RingGather(
                    partial(block_of, r.skip_all, s), r.skip_sems.at[s], seq_devices, me_s, me_c, s == 0
                )
            )
        if s == 0:
            hook(5)
    out_part = dot(r.mixed[...], wout_ref[...])
    for q in range(4):
        r.out_blocks[q] = out_part[:, q * shard : (q + 1) * shard].astype(BF16)
    scatter_out = ChanScatter(
        r.out_blocks, r.out_first, r.out_second, r.out_sems, me_c, core_peer, x_peer
    )
    bits = [1 << k for k in range(seq_devices.bit_length() - 1)]
    turned = bits[1:] + bits[:1]
    hook(6)
    if not gathered:
        r.grad_w_out[...] = dot(r.mixed[...], r.cot[...], ((0,), (0,))).astype(BF16)
        sums.append(SeqSum(r.grad_w_out, r.land_w_out, r.out_w_out, r.w_out_sems, bits, me_s, me_c))
        r.grad_w_gate[...] = dot(r.normed[...], r.grad_gate[...], ((0,), (0,))).astype(BF16)
        sums.append(SeqSum(r.grad_w_gate, r.land_w_gate, r.out_w_in.at[1], r.w_gate_sems, turned, me_s, me_c))

    early, later = (r.early, r.later)
    early[...] = jnp.zeros_like(early)
    later[...] = jnp.zeros_like(later)
    skip_row = low_rank + states + 1
    low_sum, rim_copies, rate_sums = ([], [], [])
    has_right = (me_s < seq_devices - 1).astype(F32)

    def scan_back(s, services):
        leaving = combine(leaves_refs, s, seq_devices - 1 - me_s, lambda k: seq_devices - 1 - k)
        carried = (tuple(leaving[:, lanes] for lanes in lane_chunks(width)), zero_states(rate_ref))
        parts, blocks = (len(services), tokens // 8)
        for part, service in enumerate(services):
            carried = run_adjoints(
                r.decay, r.step, r.up, r.b, r.c, rate_ref, r.entering, r.state,
                r.adjoint, r.first_sum, r.second_sum, s, s * tokens, tokens,
                (part * blocks // parts, (part + 1) * blocks // parts), carried,
            )
            service()
        rate_sums.append(carried[1])

    def after_scan(s):
        mine = pl.ds(s * tokens, tokens)
        act, step, step_pre = (r.act[mine, :], r.step[mine, :], r.step_pre[mine, :])
        second = r.second_sum[...]
        grad_step_pre = (r.first_sum[...] + act * second) * jax.nn.sigmoid(step_pre)
        grad_step_low = grad_step_pre.astype(BF16)
        own = r.proj_own.at[s]
        own[:low_rank, :] = dot(dtw_ref[...], grad_step_low, ((1,), (1,))).astype(BF16)
        own[low_rank : low_rank + states, :] = map_sums(r.adjoint, r.drive[mine, :], states, 0, tokens).astype(BF16)
        own[low_rank + states :, :] = map_sums(r.state, r.up[mine, :], states, s * tokens, tokens).astype(BF16)
        low_sum.append(
            ChanSum(
                own, r.back_first.at[s], r.back_second.at[s], r.back_mid.at[s],
                r.back_sems.at[s], core_peer, x_peer,
            )
        )
        r.grad_step_low[mine, :] = grad_step_low
        early[skip_row - 1, :] += jnp.sum(grad_step_pre, axis=0)
        early[skip_row, :] += jnp.sum(r.up[mine, :] * act, axis=0)
        r.grad_act[mine, :] = step * second + r.up[mine, :] * r.skip_gain[...]

    def through_conv(s):
        mine = pl.ds(s * tokens, tokens)
        grad_projected = low_sum[s].finish()
        r.grad_proj[:, s * tokens : (s + 1) * tokens] = grad_projected.astype(BF16)
        grad_act = r.grad_act[mine, :] + dot(grad_projected.T.astype(BF16), xw_ref[...])
        conv_pre = r.conv_pre[mine, :]
        grad_conv = (grad_act * silu_slope(conv_pre, jax.nn.sigmoid(conv_pre))).astype(BF16)
        r.rim_own[s] = grad_conv[:HALO]
        rim_copies.append(
            send(r.rim_own.at[s], r.rim.at[s], r.rim_sems.at[2 * s], r.rim_sems.at[2 * s + 1], (left, me_c))
        )
        grad_conv = grad_conv.astype(F32)
        r.grad_conv[s, :tokens, :] = grad_conv
        later[proj + taps, :] += jnp.sum(grad_conv, axis=0)
        for k in range(taps):
            shifted = r.inner[s, HALO - taps + 1 + k : HALO - taps + 1 + k + tokens, :]
            later[proj + k, :] += jnp.sum(grad_conv * shifted, axis=0)

    def inner_of(s):
        mine = pl.ds(s * tokens, tokens)
        rim_copies[s].wait_recv()
        rim_copies[s].wait_send()
        r.grad_conv[s, tokens:, :] = r.rim[s].astype(F32) * has_right
        grad_inner = sum(
            r.conv_weight[k : k + 1, :] * r.grad_conv[s, taps - 1 - k : taps - 1 - k + tokens, :]
            for k in range(taps)
        )
        grad_inner = (grad_inner * mask_of(s, tokens, 0)).astype(BF16)
        r.grad_inner[mine, :] = grad_inner
        if gathered:
            r.inner_all[me_s, s] = grad_inner
            inner_gathers.append(
                RingGather(
                    partial(block_of, r.inner_all, s), r.inner_sems.at[s], seq_devices, me_s, me_c, s == 0
                )
            )

    def nothing():
        pass

    def scatter_and_hook():
        scatter_out.cross()
        hook(7)

    scan_back(0, (nothing, scatter_and_hook, nothing, partial(hook, 8)))
    after_scan(0)
    hook(9)
    scan_back(1, (low_sum[0].cross, partial(hook, 10), partial(through_conv, 0), partial(hook, 11)))
    after_scan(1)
    hook(12)
    inner_of(0)
    for k, lanes in enumerate(lane_chunks(width)):
        early[low_rank : low_rank + states, lanes] = (rate_sums[0][k] + rate_sums[1][k]) * rate_ref[:, lanes]
    early[:low_rank, :] = dot(r.low[...], r.grad_step_low[...])
    low_sum[1].cross()
    hook(13)
    out_sum = scatter_out.finish()
    for s in range(seqs):
        r.mixed_out[s] = (x_ref[s].astype(F32) + out_sum[s * tokens : (s + 1) * tokens]).astype(BF16)
    hook(14)
    through_conv(1)
    later[:proj, :] = dot(r.grad_proj[...], r.act[...].astype(BF16))
    if gathered:
        r.small_own[...] = pack_small(
            early[: skip_row + 1, :], later[: proj + taps + 1, :], low_rank, proj
        ).astype(BF16)
        small_sums.append(
            DirectSum(r.small_own, r.small_land, r.out_small, r.small_sems, seq_devices, me_s, me_c)
        )
    hook(15)
    inner_of(1)
    hook(16)

    if not gathered:
        late = r.grad_w_inner
        late[:model, :] = dot(r.normed[...], r.grad_inner[...], ((0,), (0,))).astype(BF16)
        late[model : model + early.shape[0], :] = early[...].astype(BF16)
        late[model + early.shape[0] :, :] = later[...].astype(BF16)
        sums.append(SeqSum(late, r.land_w_inner, r.full_w_inner, r.w_inner_sems, bits, me_s, me_c))
    moment = None
    for q in range(4):
        part = dot(r.grad_inner[...], win_ref[0, q * shard : (q + 1) * shard, :], ((1,), (1,)))
        part = part + dot(r.grad_gate[...], win_ref[1, q * shard : (q + 1) * shard, :], ((1,), (1,)))
        values = xo_ref[q, spot, 0].reshape(seqs * tokens, shard).astype(F32)
        term = jnp.sum(part * gain_of(q) * values, axis=1, keepdims=True)
        moment = term if moment is None else moment + term
        r.gn_blocks[q] = part.astype(BF16)
    r.moment[...] = jnp.broadcast_to(moment, (seqs * tokens, LANES)).T[:8]
    scatter_gn = ChanScatter(
        r.gn_blocks, r.gn_first, r.gn_second, r.gn_sems, me_c, core_peer, x_peer,
        (r.moment, r.moment_first, r.moment_mid, r.moment_second),
    )
    hook(17)
    scatter_gn.cross()
    hook(18)
    grad_normed, moment_row = scatter_gn.finish()
    moment = jnp.broadcast_to(moment_row[:1], (LANES, seqs * tokens)).T[:, :1]
    root = r.root[:, :1]
    values = x_ref[...].reshape(seqs * tokens, shard).astype(F32)
    gains = gain_of(me_c)
    back = root * (grad_normed * gains) - values * (root * root * root) * moment * (1.0 / model)
    for s in range(seqs):
        mine = slice(s * tokens, (s + 1) * tokens)
        cot = og_ref[s].astype(F32) * mask_of(s, tokens, 0)
        r.grad_inputs[s] = (cot + back[mine]).astype(BF16)
    gain_sums_ref = r.gain_sums
    gain_sums_ref[me_s] = jnp.broadcast_to(jnp.sum(grad_normed * values * root, axis=0, keepdims=True), (8, shard))

    def gain_copy(k):
        peer = lax.rem(me_s + k, seq_devices)
        return pltpu.make_async_remote_copy(
            src_ref=gain_sums_ref.at[me_s], dst_ref=gain_sums_ref.at[me_s],
            send_sem=r.gain_sums_send.at[k], recv_sem=r.gain_sums_recv.at[me_s],
            device_id=seq_device(peer), device_id_type=MESH,
        )

    def start_gain(k, _):
        gain_copy(k).start()
        return 0

    lax.fori_loop(1, seq_devices, start_gain, 0)
    hook(19)
    if gathered:
        gather_all.ring.finish()
        for gather in skip_gathers:
            gather.finish()
        count = seq_devices * seqs * tokens

        def mix(device, _):
            rows = pl.ds(pl.multiple_of(device * (seqs * tokens), seqs * tokens), seqs * tokens)
            with_skip = r.skip_all[device].reshape(seqs * tokens, width).astype(F32)
            r.gate_act_all[rows, :] = (r.gate_act_all[rows, :].astype(F32) * with_skip).astype(BF16)
            r.gate_slope_all[rows, :] = (r.gate_slope_all[rows, :].astype(F32) * with_skip).astype(BF16)
            return 0

        lax.fori_loop(0, seq_devices, mix, 0)
        hook(20)
        results = []

        def deliver(src, dst):
            copy = pltpu.make_async_copy(src, dst, r.result_sems.at[len(results)])
            copy.start()
            results.append(copy)

        staged = r.skip_all.reshape(count, width)
        for q in range(4):
            outs = xo_ref[q, :, 1].reshape(count, shard)
            half, place = (q * shard // width, q * shard % width)
            rows = pl.ds(half * width, width)
            staged[rows, place : place + shard] = dot(r.gate_act_all[...], outs, ((0,), (0,))).astype(BF16)
            if place + shard == width:
                deliver(staged.at[rows], r.out_w_out.at[:, pl.ds(half * width, width)])
            hook(21 + q)
        for q in range(4):
            rows = slice(q * shard, (q + 1) * shard)
            r.gate_act_all[rows, :] = dot(r.normed[:, rows], r.gate_slope_all[...], ((0,), (0,))).astype(BF16)
            hook(25 + q)
        deliver(r.gate_act_all.at[pl.ds(0, model)], r.out_w_in.at[1])
        for gather in inner_gathers:
            gather.finish()
        inner_rows = r.inner_all[...].reshape(count, width)
        for q in range(4):
            rows = slice(model + q * shard, model + (q + 1) * shard)
            cols = slice(q * shard, (q + 1) * shard)
            r.gate_act_all[rows, :] = dot(r.normed[:, cols], inner_rows, ((0,), (0,))).astype(BF16)
            if q % 2 == 1:
                deliver(
                    r.gate_act_all.at[pl.ds(model + (q - 1) * shard, 2 * shard)],
                    r.out_w_in.at[0, pl.ds((q - 1) * shard, 2 * shard)],
                )
        small_sums[0].finish()
    else:
        for step in range(max(item.total for item in sums)):
            for item in sums:
                item.advance()

    def take_gain(k, _):
        peer = lax.rem(me_s + k, seq_devices)
        pltpu.make_async_remote_copy(
            src_ref=gain_sums_ref.at[peer], dst_ref=gain_sums_ref.at[peer],
            send_sem=r.gain_sums_send.at[k], recv_sem=r.gain_sums_recv.at[peer],
            device_id=seq_device(peer), device_id_type=MESH,
        ).wait_recv()
        gain_copy(k).wait_send()
        totals_copy(k).wait_send()
        return 0

    lax.fori_loop(1, seq_devices, take_gain, 0)
    r.grad_gain[...] = jnp.sum(gain_sums_ref[...], axis=0)
    for item in sums:
        item.finish()
    if gathered:
        for copy in results:
            copy.wait()
    else:
        r.out_w_in[0] = r.full_w_inner[:model, :]
        full, rest = (r.full_w_inner, model + early.shape[0])
        r.out_small[...] = pack_small(
            full[model : model + skip_row + 1, :].astype(F32), full[rest : rest + proj + taps + 1, :].astype(F32),
            low_rank, proj,
        ).astype(BF16)
    for s in range(seqs):
        wait_carried(ends_refs, s, me_s + 1, seq_devices)
        wait_carried(leaves_refs, s, 0, me_s)


def finish_kernel(
    rows_of, mixed_ref, inputs_ref, w_in_ref, w_out_ref, small_ref, gain_ref,
    mixed_out, grad_inputs, gain_out, w_in_out, conv_w_out, conv_b_out, x_out, dt_w_out, dt_b_out, decay_out,
    skip_out, w_out_out,
):
    mixed_out[...] = mixed_ref[...]
    grad_inputs[...] = inputs_ref[...]
    w_in_out[...] = w_in_ref[...].astype(F32)
    w_out_out[...] = w_out_ref[...].astype(F32)

    @pl.when(pl.program_id(0) == 0)
    def _():
        proj, low_rank, states, taps = rows_of
        small, width = (small_ref[...].astype(F32), x_out.shape[1])
        left, right = (small[:, :width], small[:, width:])
        tap_row = proj + states + 2
        gain_out[...] = gain_ref[0:1, :]
        x_out[...] = left[:proj]
        dt_w_out[:, : width // 2] = right[:low_rank]
        dt_w_out[:, width // 2 :] = right[low_rank:]
        decay_out[...] = left[proj : proj + states]
        dt_b_out[...] = left[tap_row - 2 : tap_row - 1]
        skip_out[...] = left[tap_row - 1 : tap_row]
        conv_w_out[...] = left[tap_row : tap_row + taps]
        conv_b_out[...] = left[tap_row + taps : tap_row + taps + 1]


def layer(
    seq_devices,
    inputs, lengths, out_grad, norm_gain, w_in, conv_weight, conv_bias, x_weight, dt_weight,
    dt_bias, log_decay, skip_gain, w_out,
):
    seqs, tokens, shard = inputs.shape
    _, model, width = w_in.shape
    states, low_rank, taps, proj = (log_decay.shape[0], dt_weight.shape[0], conv_weight.shape[0], x_weight.shape[0])
    rows = seqs * tokens
    grain = 16 * seq_devices if seq_devices <= MOST_GATHERED else 8 * seq_devices
    early_rows = -(-(low_rank + states + 2) // grain) * grain
    later_rows = -(-(proj + taps + 1) // grain) * grain
    steps = 4 * (seq_devices.bit_length() - 1)
    gathered = seq_devices <= MOST_GATHERED
    dma = pltpu.SemaphoreType.DMA
    vmem = pltpu.VMEM
    operands = dict(
        inputs=inputs, lengths=lengths, out_grad=out_grad, norm_gain=norm_gain,
        w_in=w_in, conv_weight=conv_weight, conv_bias=conv_bias.reshape(1, width),
        x_weight=x_weight, dt_weight=dt_weight, dt_bias=dt_bias.reshape(1, width),
        log_decay=log_decay, skip_gain=skip_gain.reshape(1, width), w_out=w_out,
    )
    outputs = dict(
        mixed_out=(inputs.shape, BF16), grad_inputs=(inputs.shape, BF16), grad_gain=((8, shard), F32),
        out_w_in=(w_in.shape, BF16), out_w_out=(w_out.shape, BF16),
        out_small=((2 * low_rank, width + width // 2), BF16),
    )
    wide = (rows, width)
    scratch = dict(
        xo=vmem((4, seq_devices if gathered else 1, 2) + inputs.shape, BF16),
        halo=vmem((4, seqs + 1, HALO, shard), BF16), known=pltpu.SemaphoreType.REGULAR((8,)),
        w_in_here=vmem(w_in.shape, BF16), w_out_here=vmem(w_out.shape, BF16), load_sems=dma((2,)),
        x_sems=dma((seqs, 6)), og_sems=dma((6,)), halo_sems=dma((8,)),
        rate=vmem((states, width), F32), rate2=vmem((states, width), F32),
        root=vmem((rows, LANES), F32), normed=vmem((seq_devices * rows if gathered else rows, model), BF16),
        inner=vmem((seqs, HALO + tokens, width), F32),
        conv_pre=vmem(wide, F32), act=vmem(wide, F32), gate_pre=vmem(wide, F32),
        grad_mixed=vmem(wide, F32), up=vmem(wide, F32),
        proj_own=vmem((seqs, proj, tokens), BF16), proj_first=vmem((seqs, proj, tokens), BF16),
        proj_second=vmem((seqs, proj, tokens), BF16), proj_mid=vmem((seqs, proj, tokens), BF16),
        proj_sems=dma((seqs, 4)),
        back_first=vmem((seqs, proj, tokens), BF16), back_second=vmem((seqs, proj, tokens), BF16),
        back_mid=vmem((seqs, proj, tokens), BF16), back_sems=dma((seqs, 4)),
        low=vmem((low_rank, rows), BF16), step_pre=vmem(wide, F32), step=vmem(wide, F32),
        drive=vmem(wide, F32), b=vmem((rows, states, LANES), F32), c=vmem((rows, states, LANES), F32),
        decay=vmem((rows, states, width), F32),
        totals=vmem((seq_devices, 8, width), F32), totals_send=dma((seq_devices,)),
        totals_recv=dma((seq_devices,)),
        ends=vmem((seqs, seq_devices, states, width), BF16), ends_send=dma((seqs, seq_devices)),
        ends_recv=dma((seqs, seq_devices)),
        leaves=vmem((seqs, seq_devices, states, width), BF16), leaves_send=dma((seqs, seq_devices)),
        leaves_recv=dma((seqs, seq_devices)),
        entering=vmem((seqs, states, width), F32),
        state=vmem((rows, states, width), BF16), adjoint=vmem((tokens, states, width), BF16),
        scanned=vmem((tokens, width), F32), first_sum=vmem((tokens, width), F32),
        second_sum=vmem((tokens, width), F32),
        mixed=vmem(wide, BF16), grad_gate=vmem(wide, BF16), grad_step_low=vmem(wide, BF16),
        grad_act=vmem(wide, F32), grad_proj=vmem((proj, rows), BF16),
        grad_conv=vmem((seqs, tokens + HALO, width), F32), rim_own=vmem((seqs, HALO, width), BF16),
        rim=vmem((seqs, HALO, width), BF16), rim_sems=dma((2 * seqs,)),
        grad_inner=vmem(wide, BF16),
        out_blocks=vmem((4, rows, shard), BF16), out_first=vmem((2, rows, shard), BF16),
        out_second=vmem((rows, shard), BF16), out_sems=dma((6,)),
        gn_blocks=vmem((4, rows, shard), BF16), gn_first=vmem((2, rows, shard), BF16),
        gn_second=vmem((rows, shard), BF16), gn_sems=dma((10,)),
        moment=vmem((8, rows), F32), moment_first=vmem((8, rows), F32),
        moment_mid=vmem((8, rows), F32), moment_second=vmem((8, rows), F32),
        early=vmem((early_rows, width), F32), later=vmem((later_rows, width), F32),
        gain_sums=vmem((seq_devices, 8, shard), F32), gain_sums_send=dma((seq_devices,)),
        gain_sums_recv=dma((seq_devices,)),
    )
    if gathered:
        every = (seq_devices * rows, width)
        ring_steps = seq_devices // 2
        scratch.update(
            gate_act_all=vmem(every, BF16), gate_slope_all=vmem(every, BF16),
            skip_all=vmem((seq_devices, seqs, tokens, width), BF16),
            inner_all=vmem((seq_devices, seqs, tokens, width), BF16),
            xo_ring_sems=dma((2, ring_steps, 2)), xo_chan_sems=dma((seq_devices - 1, 6)),
            skip_sems=dma((seqs, 2, ring_steps, 2)), inner_sems=dma((seqs, 2, ring_steps, 2)),
            small_own=vmem((2 * low_rank, width + width // 2), BF16),
            small_land=vmem((seq_devices, 2 * low_rank // seq_devices, width + width // 2), BF16),
            small_sems=dma((4, seq_devices)), result_sems=dma((5,)),
        )
    else:
        late = (model + early_rows + later_rows, width)
        scratch.update(
            cot=vmem((rows, model), BF16),
            grad_w_out=vmem(w_out.shape, BF16), land_w_out=vmem(w_out.shape, BF16), w_out_sems=dma((steps,)),
            grad_w_gate=vmem((model, width), BF16), land_w_gate=vmem((model, width), BF16),
            w_gate_sems=dma((steps,)),
            grad_w_inner=vmem(late, BF16), land_w_inner=vmem(late, BF16), full_w_inner=vmem(late, BF16),
            w_inner_sems=dma((steps,)),
        )
    names = list(operands) + list(outputs) + list(scratch)
    spaces = dict(lengths=pltpu.SMEM, w_in=pl.ANY, w_out=pl.ANY)
    mixed_out, grad_inputs, gain, w_in_grad, w_out_grad, small = pl.pallas_call(
        partial(layer_kernel, names, seq_devices),
        out_shape=tuple(jax.ShapeDtypeStruct(*item) for item in outputs.values()),
        in_specs=[pl.BlockSpec(memory_space=spaces.get(name, pltpu.VMEM)) for name in operands],
        out_specs=tuple(
            pl.BlockSpec(memory_space=pl.ANY if gathered and name in ("out_w_in", "out_w_out") else pltpu.VMEM)
            for name in outputs
        ),
        scratch_shapes=list(scratch.values()),
        compiler_params=pltpu.CompilerParams(
            collective_id=0, has_side_effects=True, vmem_limit_bytes=VMEM_LIMIT
        ),
    )(*operands.values())
    parts = 2

    def cut(shape, axis):
        block = tuple(size // parts if k == axis else size for k, size in enumerate(shape))
        return pl.BlockSpec(block, lambda i: tuple(i if k == axis else 0 for k in range(len(shape))))

    def kept(shape):
        return pl.BlockSpec(shape, lambda i: (0,) * len(shape))

    def result(shape, spec, dtype=F32):
        return jax.ShapeDtypeStruct(shape, dtype), spec

    tokens_cut = cut(inputs.shape, 1)
    w_in_cut, w_out_cut = (cut(w_in.shape, 1), cut(w_out.shape, 0))
    wide_row = ((1, width), kept((1, width)))
    results = [
        result(inputs.shape, tokens_cut, BF16), result(inputs.shape, tokens_cut, BF16),
        result((1, shard), kept((1, shard))), result(w_in.shape, w_in_cut),
        result(conv_weight.shape, kept(conv_weight.shape)), result(*wide_row),
        result(x_weight.shape, kept(x_weight.shape)), result(dt_weight.shape, kept(dt_weight.shape)),
        result(*wide_row), result(log_decay.shape, kept(log_decay.shape)), result(*wide_row),
        result(w_out.shape, w_out_cut),
    ]
    out = pl.pallas_call(
        partial(finish_kernel, (proj, low_rank, states, taps)),
        grid=(parts,),
        out_shape=tuple(item[0] for item in results),
        in_specs=[tokens_cut, tokens_cut, w_in_cut, w_out_cut, kept(small.shape), kept(gain.shape)],
        out_specs=tuple(item[1] for item in results),
        compiler_params=pltpu.CompilerParams(vmem_limit_bytes=VMEM_LIMIT),
    )(mixed_out, grad_inputs, w_in_grad, w_out_grad, small, gain)
    flat = (2, 5, 8, 10)
    return tuple(value.reshape(-1) if k in flat else value for k, value in enumerate(out))


def solution(mesh):
    in_specs = (
        P(None, "seq", "chan"), P(), P(None, "seq", "chan"), P("chan"), P(None, None, "chan"),
        P(None, "chan"), P("chan"), P(None, "chan"), P(None, "chan"), P("chan"), P(None, "chan"),
        P("chan"), P("chan", None),
    )
    out_specs = (
        P(None, "seq", "chan"), P(None, "seq", "chan"), P("chan"), P(None, None, "chan"),
        P(None, "chan"), P("chan"), P(None, "chan"), P(None, "chan"), P("chan"), P(None, "chan"),
        P("chan"), P("chan", None),
    )
    body = partial(layer, mesh.shape["seq"])
    return jax.shard_map(body, mesh=mesh, in_specs=in_specs, out_specs=out_specs, check_vma=False)
```
